32 devices in a mesh: wide: 8 (over z, core), narrow: 4 (over y, x).
Axes of the slice: x: 2, y: 2, z: 4, core: 2. Of those that a mesh axis runs over, the one named last changes fastest.
Arguments:
- inputs: bfloat16 [1, 4096, 4096], P(None, 'narrow', 'wide'), may hold values from -6 to 6
- out_cotangent: bfloat16 [1, 1, 4096, 14336], P(None, None, ('wide', 'narrow')), may hold values from -0.0014648438 to 0.0014648438
- sign_bits: int32 [1, 4096, 16384], P(None, 'wide', 'narrow'), may hold values 0 or 1
- row_pick: int32 [1, 8192], replicated, may hold values from 0 to 4095
- col_pick: int32 [1, 8192], replicated, may hold values from 0 to 16383
Outputs:
- sketch: float32 [1, 1, 8192], P(None, None, ('wide', 'narrow'))
The draws below stay inside these ranges and needn't reach their ends.
All inputs are finite; a program needn't handle non-finite values. No bound on the sum of `sign_bits` on one device may be relied on, other than what follows from the above.
Results may differ from the reference program's by a relative error of at most 0.0003.
Values may be sent and summed in bfloat16 or wider, within the bound.
No kernel may reach another device: no remote copies, remote signals or barrier semaphores. Data moves between devices by JAX's collectives and lax.ppermute only.
A program may use at most 128 MiB of HBM per device.

```python
import jax
import jax.numpy as jnp
from jax import lax

D = 4096
FF = 14336
FFP = 16384
MATS = 1
EXAMPLES = 1
TOK = 4096
SKETCH = 8192


def place_ends(array, stream_key, smallest, high):
    dims = array.shape
    spot = [jax.random.randint(jax.random.fold_in(stream_key, axis), (), 0, dims[axis]) for axis in range(len(dims))]
    array = array.at[tuple(spot)].set(smallest)
    longest = dims.index(max(dims))
    spot[longest] = (spot[longest] + 1) % dims[longest]
    return array.at[tuple(spot)].set(high)


def levels(stream_key, extent, pieces, smallest, largest):
    def one(position, parts):
        heights = jax.random.uniform(jax.random.fold_in(jax.random.fold_in(stream_key, 6), position), (parts,), jnp.float32, smallest / len(pieces), largest / len(pieces))
        return jnp.repeat(jnp.exp(heights), extent[position] // parts).reshape((-1,) + (1,) * (len(extent) - position - 1))

    gain = one(*pieces[0])
    for cut in pieces[1:]:
        gain = gain * one(*cut)
    return gain


def bell_draw(own_key, dims, deviation, limit, shards=(), held_as=jnp.bfloat16):
    result = deviation * jax.random.normal(own_key, dims, jnp.float32)
    if shards:
        result = result * levels(own_key, dims, shards, -0.22, 0.18)
    return jnp.clip(result, -limit, limit).astype(held_as)


def setup_inputs(seed: int = 0) -> dict:
    streams_of = jax.random.split(jax.random.key(seed), 6)
    return {
        "inputs": bell_draw(streams_of[0], (EXAMPLES, TOK, D), 1.0, 6.0, ((1, 4), (2, 8))),
        "out_cotangent": bell_draw(streams_of[1], (MATS, EXAMPLES, TOK, FF), (1.0 / TOK), 0.0014648438, ((2, 32),)),
        "sign_bits": place_ends((jax.random.randint(streams_of[2], (MATS, D, FFP), 0, 2) < 1).astype(jnp.int32), jax.random.fold_in(streams_of[2], 1), 0, 1),
        "row_pick": place_ends(jax.random.randint(streams_of[3], (MATS, SKETCH), 0, D), jax.random.fold_in(streams_of[3], 1), 0, D - 1).astype(jnp.int32),
        "col_pick": place_ends(jax.random.randint(streams_of[4], (MATS, SKETCH), 0, FFP), jax.random.fold_in(streams_of[4], 1), 0, FFP - 1).astype(jnp.int32),
    }


def hadamard(length):
    index = jnp.arange(length, dtype=jnp.int32)
    parity = jnp.zeros((length, length), jnp.int32)
    for bit_number in range(length.bit_length() - 1):
        parity = parity ^ index[:, None] >> bit_number & 1 & (index[None, :] >> bit_number & 1)
    return (1 - 2 * parity).astype(jnp.float32)

def transform_last(block):
    width_all = block.shape[-1]
    leading = block.ndim - 1
    factors = []
    remain = width_all
    while remain > 1:
        factor = min(128, remain)
        factors.append(factor)
        remain = remain // factor
    shaped = block.reshape(block.shape[:-1] + tuple(factors))
    for placed, factor in enumerate(factors):
        mixed = jnp.tensordot(shaped, hadamard(factor), axes=([leading + placed], [0]), precision=lax.Precision.HIGHEST)
        shaped = jnp.moveaxis(mixed, -1, leading + placed)
    return shaped.reshape(block.shape)

def reference(inputs, out_cotangent, sign_bits, row_pick, col_pick):
    row_index = jnp.arange(D, dtype=jnp.int32)
    results = []
    for example in range(EXAMPLES):
        per_matrix = []
        for matrix in range(MATS):
            grad = jnp.dot(inputs[example].T, out_cotangent[matrix, example], preferred_element_type=jnp.float32)
            padded = jnp.pad(grad, ((0, 0), (0, FFP - FF)))
            padded = padded * (2 * sign_bits[matrix] - 1).astype(jnp.float32)
            columns_done = transform_last(padded)
            chosen = columns_done[:, col_pick[matrix]]
            parity = jnp.zeros((SKETCH, D), jnp.int32)
            for bit_number in range(D.bit_length() - 1):
                parity = parity ^ row_pick[matrix][:, None] >> bit_number & 1 & (row_index[None, :] >> bit_number & 1)
            row_signs = (1 - 2 * parity).astype(jnp.float32)
            values = lax.optimization_barrier(jnp.sum(row_signs * chosen.T, axis=1))
            per_matrix.append(values / jnp.sqrt(jnp.float32(SKETCH)))
        results.append(jnp.stack(per_matrix))
    return jnp.stack(results)
```

```python
import functools

import jax
import jax.numpy as jnp
import numpy as np
from jax import lax
from jax.experimental import pallas as pl
from jax.experimental.pallas import tpu as pltpu
from jax.sharding import Mesh, PartitionSpec as P

LANES = 128
CHUNKS = 4
MIB = 1024 * 1024
ALL_AXES = ("hi", "zl", "core", "narrow")


def hadamard(length):
    h = np.ones((1, 1), np.float32)
    while h.shape[0] < length:
        h = np.block([[h, h], [h, -h]])
    return h


def butterfly(parts):
    step = 1
    while step < len(parts):
        parts = [
            parts[i] + parts[i ^ step] if not i & step else parts[i ^ step] - parts[i]
            for i in range(len(parts))
        ]
        step *= 2
    return parts


def prep_kernel(real_blocks, zl_count, chunk, in_ref, *out_refs):
    block = pl.program_id(1) * zl_count + pl.program_id(0)
    keep = block < real_blocks
    for c, out_ref in enumerate(out_refs):
        value = in_ref[:, c * chunk : (c + 1) * chunk]
        out_ref[0] = jnp.where(keep, value, jnp.zeros_like(value))


def prepare(cot, zl_count, narrow_count, col_dev, chunks):
    tokens, hidden = cot.shape
    real_blocks = hidden // col_dev
    chunk = col_dev // chunks
    return pl.pallas_call(
        functools.partial(prep_kernel, real_blocks, zl_count, chunk),
        grid=(zl_count, narrow_count),
        in_specs=[
            pl.BlockSpec(
                (tokens, col_dev),
                lambda z, n: (0, jnp.minimum(n * zl_count + z, real_blocks - 1)),
            )
        ],
        out_specs=[
            pl.BlockSpec((1, tokens, chunk), lambda z, n: (z * narrow_count + n, 0, 0))
            for _ in range(chunks)
        ],
        out_shape=[
            jax.ShapeDtypeStruct((zl_count * narrow_count, tokens, chunk), cot.dtype)
            for _ in range(chunks)
        ],
        compiler_params=pltpu.CompilerParams(vmem_limit_bytes=24 * MIB),
        cost_estimate=pl.CostEstimate(
            flops=0, bytes_accessed=4 * cot.size, transcendentals=0
        ),
        name="cut_columns",
    )(cot)


def chunk_kernel(hi_count, zl_count, place_ref, *refs):
    xt = refs[:zl_count]
    cots = refs[zl_count : zl_count + 2 * hi_count]
    signs = refs[zl_count + 2 * hi_count : 2 * zl_count + 2 * hi_count]
    row_mix = refs[-2]
    out_ref = refs[-1]
    hi, core = place_ref[0], place_ref[2]
    mixed = []
    for d in range(zl_count):
        total = None
        for h in range(hi_count):
            for c in range(2):
                for z in range(zl_count):
                    source = ((hi ^ h) * zl_count + z) * 2 + (core ^ c)
                    term = jnp.dot(
                        xt[d][source],
                        cots[h * 2 + c][z],
                        preferred_element_type=jnp.float32,
                    )
                    total = term if total is None else total + term
        value = total * signs[d][...].astype(jnp.float32)
        high = value.astype(jnp.bfloat16)
        low = (value - high.astype(jnp.float32)).astype(jnp.bfloat16)
        mixed.append(
            jnp.dot(row_mix[...], high, preferred_element_type=jnp.float32)
            + jnp.dot(row_mix[...], low, preferred_element_type=jnp.float32)
        )
    mixed = butterfly(mixed)
    for b in range(out_ref.shape[0]):
        for d in range(zl_count):
            out_ref[b, d] = mixed[d][:, b * LANES : (b + 1) * LANES]


def chunk_call(place, xt, cots, signs, row_mix, index, chunk, hi_count):
    zl_count = len(xt)
    sources, rows, tokens = xt[0].shape
    tile = min(256, chunk)
    steps = chunk // tile
    resident = pl.Buffered(1)
    return pl.pallas_call(
        functools.partial(chunk_kernel, hi_count, zl_count),
        grid_spec=pltpu.PrefetchScalarGridSpec(
            num_scalar_prefetch=1,
            grid=(steps,),
            in_specs=[
                pl.BlockSpec(
                    (sources, rows, tokens), lambda i, p: (0, 0, 0), pipeline_mode=resident
                )
                for _ in xt
            ]
            + [
                pl.BlockSpec((zl_count, tokens, tile), lambda i, p: (0, 0, i))
                for _ in cots
            ]
            + [
                pl.BlockSpec((rows, tile), lambda i, p: (0, index * steps + i))
                for _ in signs
            ]
            + [
                pl.BlockSpec((rows, rows), lambda i, p: (0, 0), pipeline_mode=resident)
            ],
            out_specs=pl.BlockSpec(
                (tile // LANES, zl_count, rows, LANES), lambda i, p: (i, 0, 0, 0)
            ),
        ),
        out_shape=jax.ShapeDtypeStruct(
            (chunk // LANES, zl_count, rows, LANES), jnp.float32
        ),
        compiler_params=pltpu.CompilerParams(vmem_limit_bytes=40 * MIB),
        cost_estimate=pl.CostEstimate(
            flops=2 * zl_count * rows * chunk * (sources * tokens + 2 * rows),
            bytes_accessed=2 * zl_count * rows * (sources * tokens + 3 * chunk)
            + 2 * sources * tokens * chunk,
            transcendentals=0,
        ),
        name="gradient_rows",
    )(place, *xt, *cots, *signs, row_mix)


def pick_kernel(parts, index_ref, *refs):
    blocks = refs[:parts]
    lane_signs, out_ref, mixed_ref, rows_ref = refs[parts:]
    per_part = blocks[0].shape[0]
    rows = blocks[0].shape[1]
    count = parts * per_part

    def mix(i, carry):
        spot = pl.ds(pl.multiple_of(i * 8, 8), 8)
        values = [blocks[b // per_part][b % per_part, spot, :] for b in range(count)]
        for b, value in enumerate(butterfly(values)):
            mixed_ref[pl.ds(pl.multiple_of(b * rows + i * 8, 8), 8), :] = value
        return carry

    lax.fori_loop(0, rows // 8, mix, 0)

    def group(g, carry):
        for j in range(LANES):
            row = index_ref[g * LANES + j]
            rows_ref[pl.ds(j, 1), :] = mixed_ref[pl.ds(row, 1), :]
        spot = pl.ds(pl.multiple_of(g * LANES, LANES), LANES)
        product = rows_ref[...] * lane_signs[spot, :].astype(jnp.float32)
        out_ref[pl.ds(g, 1), :] = jnp.sum(product.T, axis=0, keepdims=True)
        return carry

    lax.fori_loop(0, out_ref.shape[0], group, 0)


def pick_call(index, blocks, lane_signs):
    picks = index.shape[0]
    per_part, rows, _ = blocks[0].shape
    total = per_part * rows * len(blocks)
    return pl.pallas_call(
        functools.partial(pick_kernel, len(blocks)),
        grid_spec=pltpu.PrefetchScalarGridSpec(
            num_scalar_prefetch=1,
            grid=(1,),
            in_specs=[
                pl.BlockSpec(
                    (per_part, rows, LANES),
                    lambda i, p: (0, 0, 0),
                    pipeline_mode=pl.Buffered(1),
                )
                for _ in blocks
            ]
            + [
                pl.BlockSpec(
                    (picks, LANES), lambda i, p: (0, 0), pipeline_mode=pl.Buffered(1)
                )
            ],
            out_specs=pl.BlockSpec((picks // LANES, LANES), lambda i, p: (0, 0)),
            scratch_shapes=[
                pltpu.VMEM((total, LANES), jnp.float32),
                pltpu.VMEM((LANES, LANES), jnp.float32),
            ],
        ),
        out_shape=jax.ShapeDtypeStruct((picks // LANES, LANES), jnp.float32),
        compiler_params=pltpu.CompilerParams(vmem_limit_bytes=40 * MIB),
        cost_estimate=pl.CostEstimate(
            flops=8 * total * LANES, bytes_accessed=4 * total * LANES, transcendentals=0
        ),
        name="pick_samples",
    )(index, *blocks, lane_signs)


def parity_sign(bits):
    for shift in (16, 8, 4, 2, 1):
        bits = bits ^ (bits >> shift)
    return 1 - 2 * (bits & 1)


def swap(value, axis, offset):
    count = lax.axis_size(axis)
    return lax.ppermute(value, axis, [(i, i ^ offset) for i in range(count)])


def body(inputs, out_cotangent, sign_bits, row_pick, col_pick):
    hi_count = lax.axis_size("hi")
    zl_count = lax.axis_size("zl")
    narrow_count = lax.axis_size("narrow")
    hi, zl, core, narrow = [lax.axis_index(a) for a in ALL_AXES]
    wide_count = hi_count * zl_count * 2
    token_shard, rows = inputs.shape[1:]
    col_shard = sign_bits.shape[2]
    col_dev = col_shard // zl_count
    chunk = col_dev // CHUNKS
    tokens = token_shard * narrow_count // wide_count

    own_xt = inputs[0].reshape(token_shard // tokens, tokens, rows).swapaxes(1, 2)
    xt_parts = [own_xt] + [swap(own_xt, "zl", d) for d in range(1, zl_count)]
    xt = [lax.all_gather(x, "narrow", axis=0, tiled=True) for x in xt_parts]

    signs = []
    for d in range(zl_count):
        part = lax.dynamic_slice_in_dim(sign_bits[0], (zl ^ d) * col_dev, col_dev, axis=1)
        part = (2 * part - 1).astype(jnp.bfloat16)
        signs.append(part if d == 0 else swap(part, "zl", d))

    cut = prepare(out_cotangent[0, 0], zl_count, narrow_count, col_dev, CHUNKS)
    row_mix = jnp.asarray(hadamard(rows), jnp.bfloat16)
    place = jnp.stack([hi, zl, core]).astype(jnp.int32)
    blocks = []
    for index in range(CHUNKS):
        own = lax.all_to_all(cut[index], ("zl", "narrow"), 0, 0, tiled=True)
        cots = []
        for h in range(hi_count):
            piece = own if h == 0 else swap(own, "hi", h)
            cots += [piece, swap(piece, "core", 1)]
        cots = [c.reshape(zl_count, tokens, chunk) for c in cots]
        done = chunk_call(place, xt, cots, signs, row_mix, index, chunk, hi_count)
        blocks.append(done.reshape(chunk // LANES, zl_count * rows, LANES))

    row, col = row_pick[0], col_pick[0]
    block = (col // LANES) % (col_dev // LANES)
    row_in = (row // (2 * rows)) % zl_count * rows + row % rows
    position = block * (zl_count * rows) + row_in
    row_base = ((hi * zl_count + zl) * 2 + core) * rows
    col_base = narrow * col_shard + zl * col_dev
    lane = lax.broadcasted_iota(jnp.int32, (1, LANES), 1)
    fold = parity_sign((row & row_base)[:, None]) * parity_sign((col_base + lane) & col[:, None])
    picked = pick_call(position, blocks, fold.astype(jnp.bfloat16))

    devices = wide_count * narrow_count
    terms = lax.all_to_all(
        picked.reshape(devices, row.shape[0] // devices), ALL_AXES, 0, 0, tiled=True
    )
    total = jnp.sum(terms, axis=0) / jnp.sqrt(jnp.float32(row.shape[0]))
    return total.reshape(1, 1, -1)


def solution(mesh):
    wide, narrow = mesh.shape["wide"], mesh.shape["narrow"]
    sizes = (2, wide // 4, 2, narrow)
    split = Mesh(mesh.devices.reshape(sizes), ALL_AXES)
    wide_axes = ("hi", "zl", "core")
    return jax.shard_map(
        body,
        mesh=split,
        in_specs=(
            P(None, "narrow", wide_axes),
            P(None, None, ALL_AXES, None),
            P(None, wide_axes, "narrow"),
            P(),
            P(),
        ),
        out_specs=P(None, None, ALL_AXES),
        check_vma=False,
    )
```

```python
import functools

import jax
import jax.numpy as jnp
import numpy as np
from jax import lax
from jax.experimental import pallas as pl
from jax.experimental.pallas import tpu as pltpu
from jax.sharding import Mesh, PartitionSpec as P

LANES = 128
MOST_CHUNKS = 8
MIB = 1024 * 1024
ALL_AXES = ("hi", "zl", "core", "narrow")


def hadamard(length):
    h = np.ones((1, 1), np.float32)
    while h.shape[0] < length:
        h = np.block([[h, h], [h, -h]])
    return h


def butterfly(parts):
    step = 1
    while step < len(parts):
        parts = [
            parts[i] + parts[i ^ step] if not i & step else parts[i ^ step] - parts[i]
            for i in range(len(parts))
        ]
        step *= 2
    return parts


def prep_kernel(real_blocks, zl_count, chunk, in_ref, *out_refs):
    block = pl.program_id(1) * zl_count + pl.program_id(0)
    keep = block < real_blocks
    for c, out_ref in enumerate(out_refs):
        value = in_ref[:, c * chunk : (c + 1) * chunk]
        out_ref[0] = jnp.where(keep, value, jnp.zeros_like(value))


def prepare(cot, zl_count, narrow_count, col_dev, chunks):
    tokens, hidden = cot.shape
    real_blocks = hidden // col_dev
    chunk = col_dev // chunks
    return pl.pallas_call(
        functools.partial(prep_kernel, real_blocks, zl_count, chunk),
        grid=(zl_count, narrow_count),
        in_specs=[
            pl.BlockSpec(
                (tokens, col_dev),
                lambda z, n: (0, jnp.minimum(n * zl_count + z, real_blocks - 1)),
            )
        ],
        out_specs=[
            pl.BlockSpec((1, tokens, chunk), lambda z, n: (z * narrow_count + n, 0, 0))
            for _ in range(chunks)
        ],
        out_shape=[
            jax.ShapeDtypeStruct((zl_count * narrow_count, tokens, chunk), cot.dtype)
            for _ in range(chunks)
        ],
        compiler_params=pltpu.CompilerParams(vmem_limit_bytes=24 * MIB),
        cost_estimate=pl.CostEstimate(
            flops=0, bytes_accessed=4 * cot.size, transcendentals=0
        ),
        name="cut_columns",
    )(cot)


def chunk_kernel(hi_count, zl_count, place_ref, *refs):
    xt = refs[:zl_count]
    cots = refs[zl_count : zl_count + 2 * hi_count]
    signs = refs[zl_count + 2 * hi_count : 2 * zl_count + 2 * hi_count]
    row_mix = refs[-2]
    out_ref = refs[-1]
    hi, core = place_ref[0], place_ref[2]
    mixed = []
    for d in range(zl_count):
        total = None
        for h in range(hi_count):
            for c in range(2):
                for z in range(zl_count):
                    source = ((hi ^ h) * zl_count + z) * 2 + (core ^ c)
                    term = jnp.dot(
                        xt[d][source],
                        cots[h * 2 + c][z],
                        preferred_element_type=jnp.float32,
                    )
                    total = term if total is None else total + term
        value = total * signs[d][...].astype(jnp.float32)
        high = value.astype(jnp.bfloat16)
        low = (value - high.astype(jnp.float32)).astype(jnp.bfloat16)
        mixed.append(
            jnp.dot(row_mix[...], high, preferred_element_type=jnp.float32)
            + jnp.dot(row_mix[...], low, preferred_element_type=jnp.float32)
        )
    mixed = butterfly(mixed)
    for b in range(out_ref.shape[0]):
        for d in range(zl_count):
            out_ref[b, d] = mixed[d][:, b * LANES : (b + 1) * LANES]


def chunk_call(place, xt, cots, signs, row_mix, index, chunk, hi_count):
    zl_count = len(xt)
    sources, rows, tokens = xt[0].shape
    tile = min(256, chunk)
    steps = chunk // tile
    resident = pl.Buffered(1)
    return pl.pallas_call(
        functools.partial(chunk_kernel, hi_count, zl_count),
        grid_spec=pltpu.PrefetchScalarGridSpec(
            num_scalar_prefetch=1,
            grid=(steps,),
            in_specs=[
                pl.BlockSpec(
                    (sources, rows, tokens), lambda i, p: (0, 0, 0), pipeline_mode=resident
                )
                for _ in xt
            ]
            + [
                pl.BlockSpec((zl_count, tokens, tile), lambda i, p: (0, 0, i))
                for _ in cots
            ]
            + [
                pl.BlockSpec((rows, tile), lambda i, p: (0, index * steps + i))
                for _ in signs
            ]
            + [
                pl.BlockSpec((rows, rows), lambda i, p: (0, 0), pipeline_mode=resident)
            ],
            out_specs=pl.BlockSpec(
                (tile // LANES, zl_count, rows, LANES), lambda i, p: (i, 0, 0, 0)
            ),
        ),
        out_shape=jax.ShapeDtypeStruct(
            (chunk // LANES, zl_count, rows, LANES), jnp.float32
        ),
        compiler_params=pltpu.CompilerParams(vmem_limit_bytes=40 * MIB),
        cost_estimate=pl.CostEstimate(
            flops=zl_count * rows * chunk * tokens,
            bytes_accessed=4 * zl_count * rows * chunk,
            transcendentals=0,
        ),
        name="gradient_rows",
    )(place, *xt, *cots, *signs, row_mix)


def pick_kernel(parts, index_ref, *refs):
    blocks = refs[:parts]
    lane_signs, out_ref, mixed_ref, rows_ref = refs[parts:]
    per_part = blocks[0].shape[0]
    rows = blocks[0].shape[1]
    count = parts * per_part

    def mix(i, carry):
        spot = pl.ds(pl.multiple_of(i * 8, 8), 8)
        values = [blocks[b // per_part][b % per_part, spot, :] for b in range(count)]
        for b, value in enumerate(butterfly(values)):
            mixed_ref[pl.ds(pl.multiple_of(b * rows + i * 8, 8), 8), :] = value
        return carry

    lax.fori_loop(0, rows // 8, mix, 0)

    def group(g, carry):
        for j in range(LANES):
            row = index_ref[g * LANES + j]
            rows_ref[pl.ds(j, 1), :] = mixed_ref[pl.ds(row, 1), :]
        spot = pl.ds(pl.multiple_of(g * LANES, LANES), LANES)
        product = rows_ref[...] * lane_signs[spot, :].astype(jnp.float32)
        out_ref[pl.ds(g, 1), :] = jnp.sum(product.T, axis=0, keepdims=True)
        return carry

    lax.fori_loop(0, out_ref.shape[0], group, 0)


def pick_call(index, blocks, lane_signs):
    picks = index.shape[0]
    per_part, rows, _ = blocks[0].shape
    total = per_part * rows * len(blocks)
    return pl.pallas_call(
        functools.partial(pick_kernel, len(blocks)),
        grid_spec=pltpu.PrefetchScalarGridSpec(
            num_scalar_prefetch=1,
            grid=(1,),
            in_specs=[
                pl.BlockSpec(
                    (per_part, rows, LANES),
                    lambda i, p: (0, 0, 0),
                    pipeline_mode=pl.Buffered(1),
                )
                for _ in blocks
            ]
            + [
                pl.BlockSpec(
                    (picks, LANES), lambda i, p: (0, 0), pipeline_mode=pl.Buffered(1)
                )
            ],
            out_specs=pl.BlockSpec((picks // LANES, LANES), lambda i, p: (0, 0)),
            scratch_shapes=[
                pltpu.VMEM((total, LANES), jnp.float32),
                pltpu.VMEM((LANES, LANES), jnp.float32),
            ],
        ),
        out_shape=jax.ShapeDtypeStruct((picks // LANES, LANES), jnp.float32),
        compiler_params=pltpu.CompilerParams(vmem_limit_bytes=40 * MIB),
        cost_estimate=pl.CostEstimate(
            flops=8 * total * LANES, bytes_accessed=4 * total * LANES, transcendentals=0
        ),
        name="pick_samples",
    )(index, *blocks, lane_signs)


def parity_sign(bits):
    for shift in (16, 8, 4, 2, 1):
        bits = bits ^ (bits >> shift)
    return 1 - 2 * (bits & 1)


def swap(value, axis, offset):
    count = lax.axis_size(axis)
    return lax.ppermute(value, axis, [(i, i ^ offset) for i in range(count)])


def after(value, *others):
    return lax.optimization_barrier((value, *others))[0]


def after_all(values, *others):
    return list(lax.optimization_barrier((*values, *others)))[: len(values)]


def body(inputs, out_cotangent, sign_bits, row_pick, col_pick):
    hi_count = lax.axis_size("hi")
    zl_count = lax.axis_size("zl")
    narrow_count = lax.axis_size("narrow")
    hi, zl, core, narrow = [lax.axis_index(a) for a in ALL_AXES]
    wide_count = hi_count * zl_count * 2
    token_shard, rows = inputs.shape[1:]
    col_shard = sign_bits.shape[2]
    col_dev = col_shard // zl_count
    chunks = min(MOST_CHUNKS, col_dev // LANES)
    chunk = col_dev // chunks
    tokens = token_shard * narrow_count // wide_count
    cut = prepare(out_cotangent[0, 0], zl_count, narrow_count, col_dev, chunks)

    own, far = [], []
    for index in range(chunks):
        part = cut[index]
        if index == 1:
            part = after(part, own[0])
        elif index > 1:
            part = after(part, own[index - 1], far[index - 2][0])
        own.append(lax.all_to_all(part, ("zl", "narrow"), 0, 0, tiled=True))
        far.append([swap(own[index], "hi", h) for h in range(1, hi_count)])

    features = after(inputs[0], own[0])
    own_xt = features.reshape(token_shard // tokens, tokens, rows).swapaxes(1, 2)
    xt_parts = [own_xt] + [swap(own_xt, "zl", d) for d in range(1, zl_count)]
    xt = [lax.all_gather(x, "narrow", axis=0, tiled=True) for x in xt_parts]

    bits = after(sign_bits[0], own[1])
    signs = []
    for d in range(zl_count):
        part = lax.dynamic_slice_in_dim(bits, (zl ^ d) * col_dev, col_dev, axis=1)
        part = (2 * part - 1).astype(jnp.bfloat16)
        signs.append(part if d == 0 else swap(part, "zl", d))

    row_mix = jnp.asarray(hadamard(rows), jnp.bfloat16)
    place = jnp.stack([hi, zl, core]).astype(jnp.int32)
    blocks, swapped = [], []
    for index in range(chunks):
        if index == 0:
            place = after(place, own[max(chunks - 2, 0)])
        else:
            place = after(place, blocks[index - 1], own[min(index + chunks - 2, chunks - 1)])
        pieces = [own[index]] + far[index]
        if index > 1:
            pieces = after_all(pieces, blocks[index - 2])
        if index > 0:
            pieces = after_all(pieces, *swapped[index - 1])
        swapped.append([swap(piece, "core", 1) for piece in pieces])
        cots = [c for pair in zip(pieces, swapped[index]) for c in pair]
        cots = [c.reshape(zl_count, tokens, chunk) for c in cots]
        done = chunk_call(place, xt, cots, signs, row_mix, index, chunk, hi_count)
        blocks.append(done.reshape(chunk // LANES, zl_count * rows, LANES))

    row, col = row_pick[0], col_pick[0]
    block = (col // LANES) % (col_dev // LANES)
    row_in = (row // (2 * rows)) % zl_count * rows + row % rows
    position = block * (zl_count * rows) + row_in
    row_base = ((hi * zl_count + zl) * 2 + core) * rows
    col_base = narrow * col_shard + zl * col_dev
    lane = lax.broadcasted_iota(jnp.int32, (1, LANES), 1)
    fold = parity_sign((row & row_base)[:, None]) * parity_sign((col_base + lane) & col[:, None])
    picked = pick_call(position, blocks, fold.astype(jnp.bfloat16))

    devices = wide_count * narrow_count
    terms = lax.all_to_all(
        picked.reshape(devices, row.shape[0] // devices), ALL_AXES, 0, 0, tiled=True
    )
    total = jnp.sum(terms, axis=0) / jnp.sqrt(jnp.float32(row.shape[0]))
    return total.reshape(1, 1, -1)


def solution(mesh):
    wide, narrow = mesh.shape["wide"], mesh.shape["narrow"]
    sizes = (2, wide // 4, 2, narrow)
    split = Mesh(mesh.devices.reshape(sizes), ALL_AXES)
    wide_axes = ("hi", "zl", "core")
    return jax.shard_map(
        body,
        mesh=split,
        in_specs=(
            P(None, "narrow", wide_axes),
            P(None, None, ALL_AXES, None),
            P(None, wide_axes, "narrow"),
            P(),
            P(),
        ),
        out_specs=P(None, None, ALL_AXES),
        check_vma=False,
    )
```

```python
import functools

import jax
import jax.numpy as jnp
import numpy as np
from jax import lax
from jax.experimental import pallas as pl
from jax.experimental.pallas import tpu as pltpu
from jax.sharding import Mesh, PartitionSpec as P

LANES = 128
UNITS = 8
MIB = 1024 * 1024
ALL_AXES = ("hi", "zl", "core", "narrow")


def hadamard(length):
    h = np.ones((1, 1), np.float32)
    while h.shape[0] < length:
        h = np.block([[h, h], [h, -h]])
    return h


def butterfly(parts):
    step = 1
    while step < len(parts):
        parts = [
            parts[i] + parts[i ^ step] if not i & step else parts[i ^ step] - parts[i]
            for i in range(len(parts))
        ]
        step *= 2
    return parts


def plan_chunks(col_dev):
    tile = max(LANES, min(256, col_dev // UNITS))
    units = col_dev // tile
    middle = units - 2
    return tile, [1] + [2] * (middle // 2) + [1] * (middle % 2) + [1]


def prep_kernel(real_blocks, zl_count, widths, in_ref, *out_refs):
    block = pl.program_id(1) * zl_count + pl.program_id(0)
    keep = block < real_blocks
    start = 0
    for width, out_ref in zip(widths, out_refs):
        value = in_ref[:, start : start + width]
        out_ref[0] = jnp.where(keep, value, jnp.zeros_like(value))
        start += width


def prepare(cot, zl_count, narrow_count, widths):
    tokens, hidden = cot.shape
    col_dev = sum(widths)
    real_blocks = hidden // col_dev
    return pl.pallas_call(
        functools.partial(prep_kernel, real_blocks, zl_count, widths),
        grid=(zl_count, narrow_count),
        in_specs=[
            pl.BlockSpec(
                (tokens, col_dev),
                lambda z, n: (0, jnp.minimum(n * zl_count + z, real_blocks - 1)),
            )
        ],
        out_specs=[
            pl.BlockSpec((1, tokens, width), lambda z, n: (z * narrow_count + n, 0, 0))
            for width in widths
        ],
        out_shape=[
            jax.ShapeDtypeStruct((zl_count * narrow_count, tokens, width), cot.dtype)
            for width in widths
        ],
        compiler_params=pltpu.CompilerParams(vmem_limit_bytes=24 * MIB),
        cost_estimate=pl.CostEstimate(
            flops=0, bytes_accessed=4 * cot.size, transcendentals=0
        ),
        name="cut_columns",
    )(cot)


def chunk_kernel(zl_count, narrow_count, place_ref, *refs):
    features = zl_count * narrow_count
    xt = refs[:features]
    cots = refs[features : features + 2]
    signs = refs[features + 2 : features + 2 + zl_count]
    row_mix = refs[-2]
    out_ref = refs[-1]
    core, narrow = place_ref[0], place_ref[1]
    mixed = []
    for d in range(zl_count):
        total = None
        for e in range(narrow_count):
            group = narrow ^ e
            for c in range(2):
                term = jnp.dot(
                    xt[d * narrow_count + e][core ^ c],
                    cots[c][group],
                    preferred_element_type=jnp.float32,
                )
                total = term if total is None else total + term
        value = total * signs[d][...].astype(jnp.float32)
        high = value.astype(jnp.bfloat16)
        low = (value - high.astype(jnp.float32)).astype(jnp.bfloat16)
        mixed.append(
            jnp.dot(row_mix[...], high, preferred_element_type=jnp.float32)
            + jnp.dot(row_mix[...], low, preferred_element_type=jnp.float32)
        )
    mixed = butterfly(mixed)
    for b in range(out_ref.shape[0]):
        for d in range(zl_count):
            out_ref[b, d] = mixed[d][:, b * LANES : (b + 1) * LANES]


def chunk_call(place, xt, cots, signs, row_mix, tile, first, steps):
    zl_count, narrow_count = len(signs), len(xt) // len(signs)
    _, rows, tokens = xt[0].shape
    groups = cots[0].shape[0]
    resident = pl.Buffered(1)
    return pl.pallas_call(
        functools.partial(chunk_kernel, zl_count, narrow_count),
        grid_spec=pltpu.PrefetchScalarGridSpec(
            num_scalar_prefetch=1,
            grid=(steps,),
            in_specs=[
                pl.BlockSpec(
                    (2, rows, tokens), lambda i, p: (0, 0, 0), pipeline_mode=resident
                )
                for _ in xt
            ]
            + [pl.BlockSpec((groups, tokens, tile), lambda i, p: (0, 0, i)) for _ in cots]
            + [pl.BlockSpec((rows, tile), lambda i, p: (0, first + i)) for _ in signs]
            + [
                pl.BlockSpec((rows, rows), lambda i, p: (0, 0), pipeline_mode=resident)
            ],
            out_specs=pl.BlockSpec(
                (tile // LANES, zl_count, rows, LANES), lambda i, p: (i, 0, 0, 0)
            ),
        ),
        out_shape=jax.ShapeDtypeStruct(
            (steps * tile // LANES, zl_count, rows, LANES), jnp.float32
        ),
        compiler_params=pltpu.CompilerParams(vmem_limit_bytes=40 * MIB),
        cost_estimate=pl.CostEstimate(
            flops=2 * zl_count * rows * steps * tile * tokens,
            bytes_accessed=4 * zl_count * rows * steps * tile,
            transcendentals=0,
        ),
        name="gradient_rows",
    )(place, *xt, *cots, *signs, row_mix)


def pick_kernel(parts, index_ref, *refs):
    blocks = refs[:parts]
    lane_signs, out_ref, mixed_ref, rows_ref = refs[parts:]
    rows = blocks[0].shape[1]
    slabs = [(block, b) for block in blocks for b in range(block.shape[0])]

    def mix(i, carry):
        spot = pl.ds(pl.multiple_of(i * 8, 8), 8)
        values = [block[b, spot, :] for block, b in slabs]
        for b, value in enumerate(butterfly(values)):
            mixed_ref[pl.ds(pl.multiple_of(b * rows + i * 8, 8), 8), :] = value
        return carry

    lax.fori_loop(0, rows // 8, mix, 0)

    def group(g, carry):
        for j in range(LANES):
            row = index_ref[g * LANES + j]
            rows_ref[pl.ds(j, 1), :] = mixed_ref[pl.ds(row, 1), :]
        spot = pl.ds(pl.multiple_of(g * LANES, LANES), LANES)
        product = rows_ref[...] * lane_signs[spot, :].astype(jnp.float32)
        out_ref[pl.ds(g, 1), :] = jnp.sum(product.T, axis=0, keepdims=True)
        return carry

    lax.fori_loop(0, out_ref.shape[0], group, 0)


def pick_call(index, blocks, lane_signs):
    picks = index.shape[0]
    total = sum(block.shape[0] * block.shape[1] for block in blocks)
    return pl.pallas_call(
        functools.partial(pick_kernel, len(blocks)),
        grid_spec=pltpu.PrefetchScalarGridSpec(
            num_scalar_prefetch=1,
            grid=(1,),
            in_specs=[
                pl.BlockSpec(
                    block.shape, lambda i, p: (0, 0, 0), pipeline_mode=pl.Buffered(1)
                )
                for block in blocks
            ]
            + [
                pl.BlockSpec(
                    (picks, LANES), lambda i, p: (0, 0), pipeline_mode=pl.Buffered(1)
                )
            ],
            out_specs=pl.BlockSpec((picks // LANES, LANES), lambda i, p: (0, 0)),
            scratch_shapes=[
                pltpu.VMEM((total, LANES), jnp.float32),
                pltpu.VMEM((LANES, LANES), jnp.float32),
            ],
        ),
        out_shape=jax.ShapeDtypeStruct((picks // LANES, LANES), jnp.float32),
        compiler_params=pltpu.CompilerParams(vmem_limit_bytes=40 * MIB),
        cost_estimate=pl.CostEstimate(
            flops=8 * total * LANES, bytes_accessed=4 * total * LANES, transcendentals=0
        ),
        name="pick_samples",
    )(index, *blocks, lane_signs)


def parity_sign(bits):
    for shift in (16, 8, 4, 2, 1):
        bits = bits ^ (bits >> shift)
    return 1 - 2 * (bits & 1)


def swap(value, axis, offset):
    count = lax.axis_size(axis)
    return lax.ppermute(value, axis, [(i, i ^ offset) for i in range(count)])


def after(value, *others):
    return lax.optimization_barrier((value, *others))[0]


def body(inputs, out_cotangent, sign_bits, row_pick, col_pick):
    hi_count = lax.axis_size("hi")
    zl_count = lax.axis_size("zl")
    narrow_count = lax.axis_size("narrow")
    hi, zl, core, narrow = [lax.axis_index(a) for a in ALL_AXES]
    wide_count = hi_count * zl_count * 2
    token_shard, rows = inputs.shape[1:]
    col_shard = sign_bits.shape[2]
    col_dev = col_shard // zl_count
    tile, chunks = plan_chunks(col_dev)
    tokens = token_shard // 2
    cut = prepare(
        out_cotangent[0, 0], zl_count, narrow_count, [tile * steps for steps in chunks]
    )

    own, both = [], []
    for index, part in enumerate(cut):
        if index:
            part = after(part, own[index - 1])
        own.append(lax.all_to_all(part, ("zl", "narrow"), 0, 0, tiled=True))
        both.append(lax.all_gather(own[index], "hi", axis=0, tiled=True))

    features = after(inputs[0], own[0])
    own_xt = features.reshape(2, tokens, rows).swapaxes(1, 2)
    xt = []
    for d in range(zl_count):
        part = swap(own_xt, "zl", d) if d else own_xt
        xt += [part] + [swap(part, "narrow", e) for e in range(1, narrow_count)]

    bits = after(sign_bits[0], own[1])
    signs = []
    for d in range(zl_count):
        part = lax.dynamic_slice_in_dim(bits, (zl ^ d) * col_dev, col_dev, axis=1)
        part = (2 * part - 1).astype(jnp.bfloat16)
        signs.append(swap(part, "zl", d) if d else part)

    row_mix = jnp.asarray(hadamard(rows), jnp.bfloat16)
    place = after(jnp.stack([core, narrow]).astype(jnp.int32), own[-1])
    blocks, first = [], 0
    for index, steps in enumerate(chunks):
        piece = both[index]
        if index > 1:
            piece = after(piece, blocks[index - 2])
        other = swap(piece, "core", 1)
        shape = (hi_count * zl_count, tokens, tile * steps)
        cots = [piece.reshape(shape), other.reshape(shape)]
        if index:
            place = after(place, blocks[index - 1])
        done = chunk_call(place, xt, cots, signs, row_mix, tile, first, steps)
        blocks.append(done.reshape(-1, zl_count * rows, LANES))
        first += steps

    row, col = row_pick[0], col_pick[0]
    block = (col // LANES) % (col_dev // LANES)
    row_in = (row // (2 * rows)) % zl_count * rows + row % rows
    position = block * (zl_count * rows) + row_in
    row_base = ((hi * zl_count + zl) * 2 + core) * rows
    col_base = narrow * col_shard + zl * col_dev
    lane = lax.broadcasted_iota(jnp.int32, (1, LANES), 1)
    fold = parity_sign((row & row_base)[:, None]) * parity_sign((col_base + lane) & col[:, None])
    picked = pick_call(position, blocks, fold.astype(jnp.bfloat16))

    devices = wide_count * narrow_count
    terms = lax.all_to_all(
        picked.reshape(devices, row.shape[0] // devices), ALL_AXES, 0, 0, tiled=True
    )
    total = jnp.sum(terms, axis=0) / jnp.sqrt(jnp.float32(row.shape[0]))
    return total.reshape(1, 1, -1)


def solution(mesh):
    wide, narrow = mesh.shape["wide"], mesh.shape["narrow"]
    sizes = (2, wide // 4, 2, narrow)
    split = Mesh(mesh.devices.reshape(sizes), ALL_AXES)
    wide_axes = ("hi", "zl", "core")
    return jax.shard_map(
        body,
        mesh=split,
        in_specs=(
            P(None, "narrow", wide_axes),
            P(None, None, ALL_AXES, None),
            P(None, wide_axes, "narrow"),
            P(),
            P(),
        ),
        out_specs=P(None, None, ALL_AXES),
        check_vma=False,
    )
```

```python
import functools

import jax
import jax.numpy as jnp
import numpy as np
from jax import lax
from jax.experimental import pallas as pl
from jax.experimental.pallas import tpu as pltpu
from jax.sharding import Mesh, PartitionSpec as P

LANES = 128
UNITS = 8
MIB = 1024 * 1024
ALL_AXES = ("hi", "zl", "core", "narrow")


def hadamard(length):
    h = np.ones((1, 1), np.float32)
    while h.shape[0] < length:
        h = np.block([[h, h], [h, -h]])
    return h


def butterfly(parts):
    step = 1
    while step < len(parts):
        parts = [
            parts[i] + parts[i ^ step] if not i & step else parts[i ^ step] - parts[i]
            for i in range(len(parts))
        ]
        step *= 2
    return parts


def plan_chunks(col_dev):
    tile = max(LANES, min(256, col_dev // UNITS))
    units = col_dev // tile
    middle = units - 2
    return tile, [1] + [2] * (middle // 2) + [1] * (middle % 2) + [1]


def prep_kernel(real_blocks, zl_count, widths, in_ref, *out_refs):
    block = pl.program_id(1) * zl_count + pl.program_id(0)
    keep = block < real_blocks
    start = 0
    for width, out_ref in zip(widths, out_refs):
        value = in_ref[:, start : start + width]
        out_ref[0] = jnp.where(keep, value, jnp.zeros_like(value))
        start += width


def prepare(cot, zl_count, narrow_count, widths):
    tokens, hidden = cot.shape
    col_dev = sum(widths)
    real_blocks = hidden // col_dev
    return pl.pallas_call(
        functools.partial(prep_kernel, real_blocks, zl_count, widths),
        grid=(zl_count, narrow_count),
        in_specs=[
            pl.BlockSpec(
                (tokens, col_dev),
                lambda z, n: (0, jnp.minimum(n * zl_count + z, real_blocks - 1)),
            )
        ],
        out_specs=[
            pl.BlockSpec((1, tokens, width), lambda z, n: (z * narrow_count + n, 0, 0))
            for width in widths
        ],
        out_shape=[
            jax.ShapeDtypeStruct((zl_count * narrow_count, tokens, width), cot.dtype)
            for width in widths
        ],
        compiler_params=pltpu.CompilerParams(vmem_limit_bytes=60 * MIB),
        cost_estimate=pl.CostEstimate(
            flops=0, bytes_accessed=4 * cot.size, transcendentals=0
        ),
        name="cut_columns",
    )(cot)


def chunk_kernel(hi_count, zl_count, narrow_count, place_ref, *refs):
    features = zl_count * narrow_count
    xt = refs[:features]
    cots = refs[features : features + 2 * hi_count]
    signs = refs[features + 2 * hi_count : features + 2 * hi_count + zl_count]
    row_mix, out_ref, cot_ref = refs[-3:]
    hi, core, narrow = place_ref[0], place_ref[1], place_ref[2]
    for h in range(hi_count):
        for c in range(2):
            cot_ref[c, hi ^ h] = cots[2 * h + c][...]
    mixed = []
    for d in range(zl_count):
        total = None
        for e in range(narrow_count):
            group = narrow ^ e
            for c in range(2):
                term = jnp.dot(
                    xt[d * narrow_count + e][core ^ c],
                    cot_ref[c, group // zl_count, group % zl_count],
                    preferred_element_type=jnp.float32,
                )
                total = term if total is None else total + term
        value = total * signs[d][...].astype(jnp.float32)
        high = value.astype(jnp.bfloat16)
        low = (value - high.astype(jnp.float32)).astype(jnp.bfloat16)
        mixed.append(
            jnp.dot(row_mix[...], high, preferred_element_type=jnp.float32)
            + jnp.dot(row_mix[...], low, preferred_element_type=jnp.float32)
        )
    mixed = butterfly(mixed)
    for b in range(out_ref.shape[0]):
        for d in range(zl_count):
            out_ref[b, d] = mixed[d][:, b * LANES : (b + 1) * LANES]


def chunk_call(place, xt, cots, signs, row_mix, tile, steps):
    zl_count, narrow_count = len(signs), len(xt) // len(signs)
    hi_count = len(cots) // 2
    _, rows, tokens = xt[0].shape
    resident = pl.Buffered(1)
    return pl.pallas_call(
        functools.partial(chunk_kernel, hi_count, zl_count, narrow_count),
        grid_spec=pltpu.PrefetchScalarGridSpec(
            num_scalar_prefetch=1,
            grid=(steps,),
            in_specs=[
                pl.BlockSpec(
                    (2, rows, tokens), lambda i, p: (0, 0, 0), pipeline_mode=resident
                )
                for _ in xt
            ]
            + [
                pl.BlockSpec((zl_count, tokens, tile), lambda i, p: (0, 0, i))
                for _ in cots
            ]
            + [pl.BlockSpec((rows, tile), lambda i, p: (0, i)) for _ in signs]
            + [
                pl.BlockSpec((rows, rows), lambda i, p: (0, 0), pipeline_mode=resident)
            ],
            out_specs=pl.BlockSpec(
                (tile // LANES, zl_count, rows, LANES), lambda i, p: (i, 0, 0, 0)
            ),
            scratch_shapes=[
                pltpu.VMEM((2, hi_count, zl_count, tokens, tile), cots[0].dtype)
            ],
        ),
        out_shape=jax.ShapeDtypeStruct(
            (steps * tile // LANES, zl_count, rows, LANES), jnp.float32
        ),
        compiler_params=pltpu.CompilerParams(vmem_limit_bytes=60 * MIB),
        cost_estimate=pl.CostEstimate(
            flops=2 * zl_count * rows * steps * tile * tokens,
            bytes_accessed=4 * zl_count * rows * steps * tile,
            transcendentals=0,
        ),
        name="gradient_rows",
    )(place, *xt, *cots, *signs, row_mix)


def pick_kernel(parts, index_ref, *refs):
    blocks = refs[:parts]
    lane_signs, out_ref, mixed_ref, rows_ref = refs[parts:]
    rows = blocks[0].shape[1]
    slabs = [(block, b) for block in blocks for b in range(block.shape[0])]

    def mix(i, carry):
        spot = pl.ds(pl.multiple_of(i * 8, 8), 8)
        values = [block[b, spot, :] for block, b in slabs]
        for b, value in enumerate(butterfly(values)):
            mixed_ref[pl.ds(pl.multiple_of(b * rows + i * 8, 8), 8), :] = value
        return carry

    lax.fori_loop(0, rows // 8, mix, 0)

    def group(g, carry):
        for j in range(LANES):
            row = index_ref[g * LANES + j]
            rows_ref[pl.ds(j, 1), :] = mixed_ref[pl.ds(row, 1), :]
        spot = pl.ds(pl.multiple_of(g * LANES, LANES), LANES)
        product = rows_ref[...] * lane_signs[spot, :].astype(jnp.float32)
        out_ref[pl.ds(g, 1), :] = jnp.sum(product.T, axis=0, keepdims=True)
        return carry

    lax.fori_loop(0, out_ref.shape[0], group, 0)


def pick_call(index, blocks, lane_signs):
    picks = index.shape[0]
    total = sum(block.shape[0] * block.shape[1] for block in blocks)
    return pl.pallas_call(
        functools.partial(pick_kernel, len(blocks)),
        grid_spec=pltpu.PrefetchScalarGridSpec(
            num_scalar_prefetch=1,
            grid=(1,),
            in_specs=[
                pl.BlockSpec(
                    block.shape, lambda i, p: (0, 0, 0), pipeline_mode=pl.Buffered(1)
                )
                for block in blocks
            ]
            + [
                pl.BlockSpec(
                    (picks, LANES), lambda i, p: (0, 0), pipeline_mode=pl.Buffered(1)
                )
            ],
            out_specs=pl.BlockSpec((picks // LANES, LANES), lambda i, p: (0, 0)),
            scratch_shapes=[
                pltpu.VMEM((total, LANES), jnp.float32),
                pltpu.VMEM((LANES, LANES), jnp.float32),
            ],
        ),
        out_shape=jax.ShapeDtypeStruct((picks // LANES, LANES), jnp.float32),
        compiler_params=pltpu.CompilerParams(vmem_limit_bytes=60 * MIB),
        cost_estimate=pl.CostEstimate(
            flops=8 * total * LANES, bytes_accessed=4 * total * LANES, transcendentals=0
        ),
        name="pick_samples",
    )(index, *blocks, lane_signs)


def parity_sign(bits):
    for shift in (16, 8, 4, 2, 1):
        bits = bits ^ (bits >> shift)
    return 1 - 2 * (bits & 1)


def swap(value, axis, offset):
    count = lax.axis_size(axis)
    return lax.ppermute(value, axis, [(i, i ^ offset) for i in range(count)])


def after(value, *others):
    return lax.optimization_barrier((value, *others))[0]


def body(inputs, out_cotangent, sign_bits, row_pick, col_pick):
    hi_count = lax.axis_size("hi")
    zl_count = lax.axis_size("zl")
    narrow_count = lax.axis_size("narrow")
    hi, zl, core, narrow = [lax.axis_index(a) for a in ALL_AXES]
    wide_count = hi_count * zl_count * 2
    token_shard, rows = inputs.shape[1:]
    col_shard = sign_bits.shape[2]
    col_dev = col_shard // zl_count
    tile, chunks = plan_chunks(col_dev)
    tokens = token_shard // 2
    cut = prepare(
        out_cotangent[0, 0], zl_count, narrow_count, [tile * steps for steps in chunks]
    )

    own_xt = inputs[0].reshape(2, tokens, rows).swapaxes(1, 2)
    xt_parts = [swap(own_xt, "zl", d) if d else own_xt for d in range(zl_count)]

    own, far, signs = [], [], []
    first = 0
    for index, steps in enumerate(chunks):
        width = tile * steps
        part = cut[index]
        if index > 2:
            part = after(part, own[index - 1], *far[index - 3])
        elif index > 0:
            part = after(part, own[index - 1])
        own.append(lax.all_to_all(part, ("zl", "narrow"), 0, 0, tiled=True))
        earlier = far[index - 2] if index > 1 else [own[index]]
        ready = after(own[index], *earlier)
        far.append([swap(ready, "hi", h) for h in range(1, hi_count)])
        bits = after(sign_bits[0], *earlier)
        row_signs = []
        for d in range(zl_count):
            start = (zl ^ d) * col_dev + first
            part = lax.dynamic_slice_in_dim(bits, start, width, axis=1)
            part = (2 * part - 1).astype(jnp.bfloat16)
            row_signs.append(swap(part, "zl", d) if d else part)
        signs.append(row_signs)
        first += width

    xt = []
    for part in xt_parts:
        xt += [part] + [
            swap(after(part, own[0]), "narrow", e) for e in range(1, narrow_count)
        ]

    row_mix = jnp.asarray(hadamard(rows), jnp.bfloat16)
    place = after(jnp.stack([hi, core, narrow]).astype(jnp.int32), own[-1])
    blocks = []
    for index, steps in enumerate(chunks):
        pieces = [own[index]] + far[index]
        if index > 1:
            pieces = [after(piece, blocks[index - 2]) for piece in pieces]
        cots = []
        for piece in pieces:
            cots += [piece, swap(piece, "core", 1)]
        cots = [c.reshape(zl_count, tokens, tile * steps) for c in cots]
        if index:
            place = after(place, blocks[index - 1])
        done = chunk_call(place, xt, cots, signs[index], row_mix, tile, steps)
        blocks.append(done.reshape(-1, zl_count * rows, LANES))

    row, col = row_pick[0], col_pick[0]
    block = (col // LANES) % (col_dev // LANES)
    row_in = (row // (2 * rows)) % zl_count * rows + row % rows
    position = block * (zl_count * rows) + row_in
    row_base = ((hi * zl_count + zl) * 2 + core) * rows
    col_base = narrow * col_shard + zl * col_dev
    lane = lax.broadcasted_iota(jnp.int32, (1, LANES), 1)
    fold = parity_sign((row & row_base)[:, None]) * parity_sign((col_base + lane) & col[:, None])
    picked = pick_call(position, blocks, fold.astype(jnp.bfloat16))

    devices = wide_count * narrow_count
    terms = lax.all_to_all(
        picked.reshape(devices, row.shape[0] // devices), ALL_AXES, 0, 0, tiled=True
    )
    total = jnp.sum(terms, axis=0) / jnp.sqrt(jnp.float32(row.shape[0]))
    return total.reshape(1, 1, -1)


def solution(mesh):
    wide, narrow = mesh.shape["wide"], mesh.shape["narrow"]
    sizes = (2, wide // 4, 2, narrow)
    split = Mesh(mesh.devices.reshape(sizes), ALL_AXES)
    wide_axes = ("hi", "zl", "core")
    return jax.shard_map(
        body,
        mesh=split,
        in_specs=(
            P(None, "narrow", wide_axes),
            P(None, None, ALL_AXES, None),
            P(None, wide_axes, "narrow"),
            P(),
            P(),
        ),
        out_specs=P(None, None, ALL_AXES),
        check_vma=False,
    )
```

```python
import functools

import jax
import jax.numpy as jnp
import numpy as np
from jax import lax
from jax.experimental import pallas as pl
from jax.experimental.pallas import tpu as pltpu
from jax.sharding import Mesh, PartitionSpec as P

LANES = 128
UNITS = 8
MIB = 1024 * 1024
ALL_AXES = ("hi", "zl", "core", "narrow")


def hadamard(length):
    h = np.ones((1, 1), np.float32)
    while h.shape[0] < length:
        h = np.block([[h, h], [h, -h]])
    return h


def butterfly(parts):
    step = 1
    while step < len(parts):
        parts = [
            parts[i] + parts[i ^ step] if not i & step else parts[i ^ step] - parts[i]
            for i in range(len(parts))
        ]
        step *= 2
    return parts


def plan_chunks(col_dev):
    tile = max(LANES, min(256, col_dev // UNITS))
    units = col_dev // tile
    some = max(1, units // 4)
    last = max(1, some // 2)
    return tile, [some, some, units - 2 * some - last, last]


def prep_kernel(real_blocks, zl_count, spans, in_ref, *out_refs):
    block = pl.program_id(1) * zl_count + pl.program_id(0)
    keep = block < real_blocks
    for (start, stop), out_ref in zip(spans, out_refs):
        value = in_ref[:, start:stop]
        out_ref[0] = jnp.where(keep, value, jnp.zeros_like(value))


def prepare(cot, zl_count, narrow_count, col_dev, read, spans):
    tokens, hidden = cot.shape
    real_blocks = hidden // col_dev
    stride = col_dev // read
    return pl.pallas_call(
        functools.partial(prep_kernel, real_blocks, zl_count, spans),
        grid=(zl_count, narrow_count),
        in_specs=[
            pl.BlockSpec(
                (tokens, read),
                lambda z, n: (0, jnp.minimum(n * zl_count + z, real_blocks - 1) * stride),
            )
        ],
        out_specs=[
            pl.BlockSpec(
                (1, tokens, stop - start), lambda z, n: (z * narrow_count + n, 0, 0)
            )
            for start, stop in spans
        ],
        out_shape=[
            jax.ShapeDtypeStruct(
                (zl_count * narrow_count, tokens, stop - start), cot.dtype
            )
            for start, stop in spans
        ],
        compiler_params=pltpu.CompilerParams(vmem_limit_bytes=60 * MIB),
        cost_estimate=pl.CostEstimate(
            flops=0, bytes_accessed=4 * cot.size // stride, transcendentals=0
        ),
        name="cut_columns",
    )(cot)


def chunk_kernel(hi_count, zl_count, narrow_count, natural, place_ref, *refs):
    features = zl_count * narrow_count
    pieces = 2 if natural else 2 * hi_count
    xt = refs[:features]
    cots = refs[features : features + pieces]
    signs = refs[features + pieces : features + pieces + zl_count]
    row_mix, out_ref, cot_ref, xt_ref, sems = refs[-5:]
    hi, core, narrow = place_ref[0], place_ref[1], place_ref[2]
    token_shard = xt[0].shape[1]
    tokens = cots[0].shape[1]

    def feature_copy(d, e):
        spot = pl.ds(pl.multiple_of((narrow ^ e) * token_shard, token_shard), token_shard)
        k = d * narrow_count + e
        return pltpu.make_async_copy(xt[k], xt_ref.at[d, :, spot], sems.at[k])

    @pl.when(pl.program_id(0) == 0)
    def _():
        for d in range(zl_count):
            for e in range(narrow_count):
                feature_copy(d, e).start()

    for h in range(hi_count):
        for c in range(2):
            for z in range(zl_count):
                source = ((h if natural else hi ^ h) * zl_count + z) * 2 + (core ^ c)
                spot = pl.ds(pl.multiple_of(source * tokens, tokens), tokens)
                if natural:
                    cot_ref[spot, :] = cots[c][h * zl_count + z]
                else:
                    cot_ref[spot, :] = cots[2 * h + c][z]

    mixed = []
    for d in range(zl_count):

        @pl.when(pl.program_id(0) == 0)
        def _():
            for e in range(narrow_count):
                feature_copy(d, e).wait()

        value = jnp.dot(xt_ref[d], cot_ref[...], preferred_element_type=jnp.float32)
        value = value * signs[d][...].astype(jnp.float32)
        high = value.astype(jnp.bfloat16)
        low = (value - high.astype(jnp.float32)).astype(jnp.bfloat16)
        mixed.append(
            jnp.dot(row_mix[...], high, preferred_element_type=jnp.float32)
            + jnp.dot(row_mix[...], low, preferred_element_type=jnp.float32)
        )
    mixed = butterfly(mixed)
    for b in range(out_ref.shape[0]):
        for d in range(zl_count):
            out_ref[b, d] = mixed[d][:, b * LANES : (b + 1) * LANES]


def chunk_call(place, xt, cots, signs, row_mix, tile, start, steps, hi_count):
    zl_count, narrow_count = len(signs), len(xt) // len(signs)
    natural = len(cots) == 2
    rows, token_shard = xt[0].shape
    groups, tokens, _ = cots[0].shape
    total = token_shard * narrow_count
    return pl.pallas_call(
        functools.partial(chunk_kernel, hi_count, zl_count, narrow_count, natural),
        grid_spec=pltpu.PrefetchScalarGridSpec(
            num_scalar_prefetch=1,
            grid=(steps,),
            in_specs=[pl.BlockSpec(memory_space=pl.ANY) for _ in xt]
            + [
                pl.BlockSpec((groups, tokens, tile), lambda i, p: (0, 0, i)) for _ in cots
            ]
            + [pl.BlockSpec((rows, tile), lambda i, p: (0, start + i)) for _ in signs]
            + [
                pl.BlockSpec(
                    (rows, rows), lambda i, p: (0, 0), pipeline_mode=pl.Buffered(1)
                )
            ],
            out_specs=pl.BlockSpec(
                (tile // LANES, zl_count, rows, LANES), lambda i, p: (i, 0, 0, 0)
            ),
            scratch_shapes=[
                pltpu.VMEM((total, tile), cots[0].dtype),
                pltpu.VMEM((zl_count, rows, total), xt[0].dtype),
                pltpu.SemaphoreType.DMA((len(xt),)),
            ],
        ),
        out_shape=jax.ShapeDtypeStruct(
            (steps * tile // LANES, zl_count, rows, LANES), jnp.float32
        ),
        compiler_params=pltpu.CompilerParams(vmem_limit_bytes=60 * MIB),
        cost_estimate=pl.CostEstimate(
            flops=2 * zl_count * rows * steps * tile * token_shard,
            bytes_accessed=4 * zl_count * rows * steps * tile,
            transcendentals=0,
        ),
        name="gradient_rows",
    )(place, *xt, *cots, *signs, row_mix)


def pick_kernel(parts, index_ref, *refs):
    blocks = refs[:parts]
    lane_signs, out_ref, mixed_ref, rows_ref = refs[parts:]
    rows = blocks[0].shape[1]
    slabs = [(block, b) for block in blocks for b in range(block.shape[0])]

    def mix(i, carry):
        spot = pl.ds(pl.multiple_of(i * 8, 8), 8)
        values = [block[b, spot, :] for block, b in slabs]
        for b, value in enumerate(butterfly(values)):
            mixed_ref[pl.ds(pl.multiple_of(b * rows + i * 8, 8), 8), :] = value
        return carry

    lax.fori_loop(0, rows // 8, mix, 0)

    def group(g, carry):
        for j in range(LANES):
            row = index_ref[g * LANES + j]
            rows_ref[pl.ds(j, 1), :] = mixed_ref[pl.ds(row, 1), :]
        spot = pl.ds(pl.multiple_of(g * LANES, LANES), LANES)
        product = rows_ref[...] * lane_signs[spot, :].astype(jnp.float32)
        out_ref[pl.ds(g, 1), :] = jnp.sum(product.T, axis=0, keepdims=True)
        return carry

    lax.fori_loop(0, out_ref.shape[0], group, 0)


def pick_call(index, blocks, lane_signs):
    picks = index.shape[0]
    total = sum(block.shape[0] * block.shape[1] for block in blocks)
    return pl.pallas_call(
        functools.partial(pick_kernel, len(blocks)),
        grid_spec=pltpu.PrefetchScalarGridSpec(
            num_scalar_prefetch=1,
            grid=(1,),
            in_specs=[
                pl.BlockSpec(
                    block.shape, lambda i, p: (0, 0, 0), pipeline_mode=pl.Buffered(1)
                )
                for block in blocks
            ]
            + [
                pl.BlockSpec(
                    (picks, LANES), lambda i, p: (0, 0), pipeline_mode=pl.Buffered(1)
                )
            ],
            out_specs=pl.BlockSpec((picks // LANES, LANES), lambda i, p: (0, 0)),
            scratch_shapes=[
                pltpu.VMEM((total, LANES), jnp.float32),
                pltpu.VMEM((LANES, LANES), jnp.float32),
            ],
        ),
        out_shape=jax.ShapeDtypeStruct((picks // LANES, LANES), jnp.float32),
        compiler_params=pltpu.CompilerParams(vmem_limit_bytes=60 * MIB),
        cost_estimate=pl.CostEstimate(
            flops=8 * total * LANES, bytes_accessed=4 * total * LANES, transcendentals=0
        ),
        name="pick_samples",
    )(index, *blocks, lane_signs)


def parity_sign(bits):
    for shift in (16, 8, 4, 2, 1):
        bits = bits ^ (bits >> shift)
    return 1 - 2 * (bits & 1)


def swap(value, axis, offset):
    count = lax.axis_size(axis)
    return lax.ppermute(value, axis, [(i, i ^ offset) for i in range(count)])


def after(value, *others):
    return lax.optimization_barrier((value, *others))[0]


def body(inputs, out_cotangent, sign_bits, row_pick, col_pick):
    hi_count = lax.axis_size("hi")
    zl_count = lax.axis_size("zl")
    narrow_count = lax.axis_size("narrow")
    hi, zl, core, narrow = [lax.axis_index(a) for a in ALL_AXES]
    wide_count = hi_count * zl_count * 2
    token_shard, rows = inputs.shape[1:]
    col_shard = sign_bits.shape[2]
    col_dev = col_shard // zl_count
    tokens = token_shard * narrow_count // wide_count
    tile, chunks = plan_chunks(col_dev)
    edges = [tile * sum(chunks[:i]) for i in range(len(chunks) + 1)]
    spans = list(zip(edges, edges[1:]))
    cot = out_cotangent[0, 0]
    cut = list(prepare(cot, zl_count, narrow_count, col_dev, edges[1], spans[:1]))
    cut += prepare(
        after(cot, cut[0]), zl_count, narrow_count, col_dev, col_dev, spans[1:]
    )

    def spread(value):
        return lax.all_to_all(value, ("zl", "narrow"), 0, 0, tiled=True)

    def gather(value):
        return lax.all_gather(value, "hi", axis=0, tiled=True)

    own_0 = spread(cut[0])
    both_0 = gather(own_0)
    own_1 = spread(after(cut[1], own_0))
    far_1 = [swap(own_1, "hi", h) for h in range(1, hi_count)]

    own_xt = inputs[0].T
    xt_parts = [swap(own_xt, "zl", d) if d else own_xt for d in range(zl_count)]
    own_2 = spread(after(cut[2], own_1, *xt_parts))
    both_2 = gather(own_2)
    xt = []
    for part in xt_parts:
        xt += [part] + [
            swap(after(part, own_1), "narrow", e) for e in range(1, narrow_count)
        ]

    bits = after(sign_bits[0], own_1)
    signs = []
    for d in range(zl_count):
        part = lax.dynamic_slice_in_dim(bits, (zl ^ d) * col_dev, col_dev, axis=1)
        part = (2 * part - 1).astype(jnp.bfloat16)
        signs.append(swap(part, "zl", d) if d else part)
    own_3 = spread(after(cut[3], own_2, both_0, *far_1, *xt, *signs))
    both_3 = gather(own_3)

    row_mix = jnp.asarray(hadamard(rows), jnp.bfloat16)
    place = jnp.stack([hi, core, narrow]).astype(jnp.int32)
    blocks = [None] * len(chunks)
    parts = [[both_0], [own_1] + far_1, [both_2], [both_3]]
    order = (1, 0, 2, 3)
    for turn, index in enumerate(order):
        cots = []
        for piece in parts[index]:
            if turn > 1:
                piece = after(piece, blocks[order[1 if turn == 2 else turn - 2]])
            cots += [piece, swap(piece, "core", 1)]
        width = tile * chunks[index]
        cots = [c.reshape(-1, tokens, width) for c in cots]
        done = chunk_call(
            place, xt, cots, signs, row_mix, tile, edges[index] // tile, chunks[index], hi_count
        )
        place = after(place, done)
        blocks[index] = done.reshape(-1, zl_count * rows, LANES)

    row, col = row_pick[0], col_pick[0]
    block = (col // LANES) % (col_dev // LANES)
    row_in = (row // (2 * rows)) % zl_count * rows + row % rows
    position = block * (zl_count * rows) + row_in
    row_base = ((hi * zl_count + zl) * 2 + core) * rows
    col_base = narrow * col_shard + zl * col_dev
    lane = lax.broadcasted_iota(jnp.int32, (1, LANES), 1)
    fold = parity_sign((row & row_base)[:, None]) * parity_sign((col_base + lane) & col[:, None])
    picked = pick_call(position, blocks, fold.astype(jnp.bfloat16))

    devices = wide_count * narrow_count
    terms = lax.all_to_all(
        picked.reshape(devices, row.shape[0] // devices), ALL_AXES, 0, 0, tiled=True
    )
    total = jnp.sum(terms, axis=0) / jnp.sqrt(jnp.float32(row.shape[0]))
    return total.reshape(1, 1, -1)


def solution(mesh):
    wide, narrow = mesh.shape["wide"], mesh.shape["narrow"]
    sizes = (2, wide // 4, 2, narrow)
    split = Mesh(mesh.devices.reshape(sizes), ALL_AXES)
    wide_axes = ("hi", "zl", "core")
    return jax.shard_map(
        body,
        mesh=split,
        in_specs=(
            P(None, "narrow", wide_axes),
            P(None, None, ALL_AXES, None),
            P(None, wide_axes, "narrow"),
            P(),
            P(),
        ),
        out_specs=P(None, None, ALL_AXES),
        check_vma=False,
    )
```

```python
import functools

import jax
import jax.numpy as jnp
import numpy as np
from jax import lax
from jax.experimental import pallas as pl
from jax.experimental.pallas import tpu as pltpu
from jax.sharding import Mesh, PartitionSpec as P

LANES = 128
UNITS = 8
MIB = 1024 * 1024
ALL_AXES = ("hi", "zl", "core", "narrow")


def hadamard(length):
    h = np.ones((1, 1), np.float32)
    while h.shape[0] < length:
        h = np.block([[h, h], [h, -h]])
    return h


def butterfly(parts):
    step = 1
    while step < len(parts):
        parts = [
            parts[i] + parts[i ^ step] if not i & step else parts[i ^ step] - parts[i]
            for i in range(len(parts))
        ]
        step *= 2
    return parts


def plan_chunks(col_dev):
    tile = max(LANES, min(256, col_dev // UNITS))
    units = col_dev // tile
    first, last = max(1, units * 3 // UNITS), max(1, units // UNITS)
    return tile, [first, units - first - last, last]


def prep_kernel(real_blocks, zl_count, widths, in_ref, *out_refs):
    block = pl.program_id(1) * zl_count + pl.program_id(0)
    keep = block < real_blocks
    start = 0
    for width, out_ref in zip(widths, out_refs):
        value = in_ref[:, start : start + width]
        out_ref[0] = jnp.where(keep, value, jnp.zeros_like(value))
        start += width


def prepare(cot, zl_count, narrow_count, widths):
    tokens, hidden = cot.shape
    col_dev = sum(widths)
    real_blocks = hidden // col_dev
    return pl.pallas_call(
        functools.partial(prep_kernel, real_blocks, zl_count, widths),
        grid=(zl_count, narrow_count),
        in_specs=[
            pl.BlockSpec(
                (tokens, col_dev),
                lambda z, n: (0, jnp.minimum(n * zl_count + z, real_blocks - 1)),
            )
        ],
        out_specs=[
            pl.BlockSpec((1, tokens, width), lambda z, n: (z * narrow_count + n, 0, 0))
            for width in widths
        ],
        out_shape=[
            jax.ShapeDtypeStruct((zl_count * narrow_count, tokens, width), cot.dtype)
            for width in widths
        ],
        compiler_params=pltpu.CompilerParams(vmem_limit_bytes=24 * MIB),
        cost_estimate=pl.CostEstimate(
            flops=0, bytes_accessed=4 * cot.size, transcendentals=0
        ),
        name="cut_columns",
    )(cot)


def chunk_kernel(zl_count, narrow_count, place_ref, *refs):
    features = zl_count * narrow_count
    xt = refs[:features]
    cots = refs[features : features + 2]
    signs = refs[features + 2 : features + 2 + zl_count]
    row_mix = refs[-2]
    out_ref = refs[-1]
    core, narrow = place_ref[0], place_ref[1]
    mixed = []
    for d in range(zl_count):
        total = None
        for e in range(narrow_count):
            group = narrow ^ e
            for c in range(2):
                term = jnp.dot(
                    xt[d * narrow_count + e][core ^ c],
                    cots[c][group],
                    preferred_element_type=jnp.float32,
                )
                total = term if total is None else total + term
        value = total * signs[d][...].astype(jnp.float32)
        high = value.astype(jnp.bfloat16)
        low = (value - high.astype(jnp.float32)).astype(jnp.bfloat16)
        mixed.append(
            jnp.dot(row_mix[...], high, preferred_element_type=jnp.float32)
            + jnp.dot(row_mix[...], low, preferred_element_type=jnp.float32)
        )
    mixed = butterfly(mixed)
    for b in range(out_ref.shape[0]):
        for d in range(zl_count):
            out_ref[b, d] = mixed[d][:, b * LANES : (b + 1) * LANES]


def chunk_call(place, xt, cots, signs, row_mix, tile, first, steps):
    zl_count, narrow_count = len(signs), len(xt) // len(signs)
    _, rows, tokens = xt[0].shape
    groups = cots[0].shape[0]
    resident = pl.Buffered(1)
    return pl.pallas_call(
        functools.partial(chunk_kernel, zl_count, narrow_count),
        grid_spec=pltpu.PrefetchScalarGridSpec(
            num_scalar_prefetch=1,
            grid=(steps,),
            in_specs=[
                pl.BlockSpec(
                    (2, rows, tokens), lambda i, p: (0, 0, 0), pipeline_mode=resident
                )
                for _ in xt
            ]
            + [pl.BlockSpec((groups, tokens, tile), lambda i, p: (0, 0, i)) for _ in cots]
            + [pl.BlockSpec((rows, tile), lambda i, p: (0, first + i)) for _ in signs]
            + [
                pl.BlockSpec((rows, rows), lambda i, p: (0, 0), pipeline_mode=resident)
            ],
            out_specs=pl.BlockSpec(
                (tile // LANES, zl_count, rows, LANES), lambda i, p: (i, 0, 0, 0)
            ),
        ),
        out_shape=jax.ShapeDtypeStruct(
            (steps * tile // LANES, zl_count, rows, LANES), jnp.float32
        ),
        compiler_params=pltpu.CompilerParams(vmem_limit_bytes=40 * MIB),
        cost_estimate=pl.CostEstimate(
            flops=2 * zl_count * rows * steps * tile * tokens,
            bytes_accessed=4 * zl_count * rows * steps * tile,
            transcendentals=0,
        ),
        name="gradient_rows",
    )(place, *xt, *cots, *signs, row_mix)


def pick_kernel(parts, index_ref, *refs):
    blocks = refs[:parts]
    lane_signs, out_ref, mixed_ref, rows_ref = refs[parts:]
    rows = blocks[0].shape[1]
    slabs = [(block, b) for block in blocks for b in range(block.shape[0])]

    def mix(i, carry):
        spot = pl.ds(pl.multiple_of(i * 8, 8), 8)
        values = [block[b, spot, :] for block, b in slabs]
        for b, value in enumerate(butterfly(values)):
            mixed_ref[pl.ds(pl.multiple_of(b * rows + i * 8, 8), 8), :] = value
        return carry

    lax.fori_loop(0, rows // 8, mix, 0)

    def group(g, carry):
        for j in range(LANES):
            row = index_ref[g * LANES + j]
            rows_ref[pl.ds(j, 1), :] = mixed_ref[pl.ds(row, 1), :]
        spot = pl.ds(pl.multiple_of(g * LANES, LANES), LANES)
        product = rows_ref[...] * lane_signs[spot, :].astype(jnp.float32)
        out_ref[pl.ds(g, 1), :] = jnp.sum(product.T, axis=0, keepdims=True)
        return carry

    lax.fori_loop(0, out_ref.shape[0], group, 0)


def pick_call(index, blocks, lane_signs):
    picks = index.shape[0]
    total = sum(block.shape[0] * block.shape[1] for block in blocks)
    return pl.pallas_call(
        functools.partial(pick_kernel, len(blocks)),
        grid_spec=pltpu.PrefetchScalarGridSpec(
            num_scalar_prefetch=1,
            grid=(1,),
            in_specs=[
                pl.BlockSpec(
                    block.shape, lambda i, p: (0, 0, 0), pipeline_mode=pl.Buffered(1)
                )
                for block in blocks
            ]
            + [
                pl.BlockSpec(
                    (picks, LANES), lambda i, p: (0, 0), pipeline_mode=pl.Buffered(1)
                )
            ],
            out_specs=pl.BlockSpec((picks // LANES, LANES), lambda i, p: (0, 0)),
            scratch_shapes=[
                pltpu.VMEM((total, LANES), jnp.float32),
                pltpu.VMEM((LANES, LANES), jnp.float32),
            ],
        ),
        out_shape=jax.ShapeDtypeStruct((picks // LANES, LANES), jnp.float32),
        compiler_params=pltpu.CompilerParams(vmem_limit_bytes=40 * MIB),
        cost_estimate=pl.CostEstimate(
            flops=8 * total * LANES, bytes_accessed=4 * total * LANES, transcendentals=0
        ),
        name="pick_samples",
    )(index, *blocks, lane_signs)


def parity_sign(bits):
    for shift in (16, 8, 4, 2, 1):
        bits = bits ^ (bits >> shift)
    return 1 - 2 * (bits & 1)


def swap(value, axis, offset):
    count = lax.axis_size(axis)
    return lax.ppermute(value, axis, [(i, i ^ offset) for i in range(count)])


def after(value, *others):
    return lax.optimization_barrier((value, *others))[0]


def body(inputs, out_cotangent, sign_bits, row_pick, col_pick):
    hi_count = lax.axis_size("hi")
    zl_count = lax.axis_size("zl")
    narrow_count = lax.axis_size("narrow")
    hi, zl, core, narrow = [lax.axis_index(a) for a in ALL_AXES]
    wide_count = hi_count * zl_count * 2
    token_shard, rows = inputs.shape[1:]
    col_shard = sign_bits.shape[2]
    col_dev = col_shard // zl_count
    tile, chunks = plan_chunks(col_dev)
    tokens = token_shard // 2
    cut = prepare(
        out_cotangent[0, 0], zl_count, narrow_count, [tile * steps for steps in chunks]
    )

    own, both = [], []
    for index, part in enumerate(cut):
        if index:
            part = after(part, own[index - 1])
        own.append(lax.all_to_all(part, ("zl", "narrow"), 0, 0, tiled=True))
        both.append(lax.all_gather(own[index], "hi", axis=0, tiled=True))

    features = after(inputs[0], own[0])
    own_xt = features.reshape(2, tokens, rows).swapaxes(1, 2)
    xt = []
    for d in range(zl_count):
        part = swap(own_xt, "zl", d) if d else own_xt
        xt += [part] + [swap(part, "narrow", e) for e in range(1, narrow_count)]

    bits = after(sign_bits[0], own[1])
    signs = []
    for d in range(zl_count):
        part = lax.dynamic_slice_in_dim(bits, (zl ^ d) * col_dev, col_dev, axis=1)
        part = (2 * part - 1).astype(jnp.bfloat16)
        signs.append(swap(part, "zl", d) if d else part)

    row_mix = jnp.asarray(hadamard(rows), jnp.bfloat16)
    place = after(jnp.stack([core, narrow]).astype(jnp.int32), own[-1])
    blocks, first = [], 0
    for index, steps in enumerate(chunks):
        piece = both[index]
        if index > 1:
            piece = after(piece, blocks[index - 2])
        other = swap(piece, "core", 1)
        shape = (hi_count * zl_count, tokens, tile * steps)
        cots = [piece.reshape(shape), other.reshape(shape)]
        if index:
            place = after(place, blocks[index - 1])
        done = chunk_call(place, xt, cots, signs, row_mix, tile, first, steps)
        blocks.append(done.reshape(-1, zl_count * rows, LANES))
        first += steps

    row, col = row_pick[0], col_pick[0]
    block = (col // LANES) % (col_dev // LANES)
    row_in = (row // (2 * rows)) % zl_count * rows + row % rows
    position = block * (zl_count * rows) + row_in
    row_base = ((hi * zl_count + zl) * 2 + core) * rows
    col_base = narrow * col_shard + zl * col_dev
    lane = lax.broadcasted_iota(jnp.int32, (1, LANES), 1)
    fold = parity_sign((row & row_base)[:, None]) * parity_sign((col_base + lane) & col[:, None])
    picked = pick_call(position, blocks, fold.astype(jnp.bfloat16))

    devices = wide_count * narrow_count
    terms = lax.all_to_all(
        picked.reshape(devices, row.shape[0] // devices), ALL_AXES, 0, 0, tiled=True
    )
    total = jnp.sum(terms, axis=0) / jnp.sqrt(jnp.float32(row.shape[0]))
    return total.reshape(1, 1, -1)


def solution(mesh):
    wide, narrow = mesh.shape["wide"], mesh.shape["narrow"]
    sizes = (2, wide // 4, 2, narrow)
    split = Mesh(mesh.devices.reshape(sizes), ALL_AXES)
    wide_axes = ("hi", "zl", "core")
    return jax.shard_map(
        body,
        mesh=split,
        in_specs=(
            P(None, "narrow", wide_axes),
            P(None, None, ALL_AXES, None),
            P(None, wide_axes, "narrow"),
            P(),
            P(),
        ),
        out_specs=P(None, None, ALL_AXES),
        check_vma=False,
    )
```

```python
import functools

import jax
import jax.numpy as jnp
import numpy as np
from jax import lax
from jax.experimental import pallas as pl
from jax.experimental.pallas import tpu as pltpu
from jax.sharding import Mesh, PartitionSpec as P

LANES = 128
UNITS = 8
MIB = 1024 * 1024
ALL_AXES = ("hi", "zl", "core", "narrow")


def hadamard(length):
    h = np.ones((1, 1), np.float32)
    while h.shape[0] < length:
        h = np.block([[h, h], [h, -h]])
    return h


def butterfly(parts):
    step = 1
    while step < len(parts):
        parts = [
            parts[i] + parts[i ^ step] if not i & step else parts[i ^ step] - parts[i]
            for i in range(len(parts))
        ]
        step *= 2
    return parts


def plan_chunks(col_dev):
    tile = max(LANES, min(256, col_dev // UNITS))
    units = col_dev // tile
    some = max(1, units // 4)
    return tile, [units - 2 * some, some, some]


def prep_kernel(real_blocks, zl_count, spans, in_ref, *out_refs):
    block = pl.program_id(1) * zl_count + pl.program_id(0)
    keep = block < real_blocks
    for (start, stop), out_ref in zip(spans, out_refs):
        value = in_ref[:, start:stop]
        out_ref[0] = jnp.where(keep, value, jnp.zeros_like(value))


def prepare(cot, zl_count, narrow_count, col_dev, read, spans):
    tokens, hidden = cot.shape
    real_blocks = hidden // col_dev
    stride = col_dev // read
    return pl.pallas_call(
        functools.partial(prep_kernel, real_blocks, zl_count, spans),
        grid=(zl_count, narrow_count),
        in_specs=[
            pl.BlockSpec(
                (tokens, read),
                lambda z, n: (0, jnp.minimum(n * zl_count + z, real_blocks - 1) * stride),
            )
        ],
        out_specs=[
            pl.BlockSpec(
                (1, tokens, stop - start), lambda z, n: (z * narrow_count + n, 0, 0)
            )
            for start, stop in spans
        ],
        out_shape=[
            jax.ShapeDtypeStruct(
                (zl_count * narrow_count, tokens, stop - start), cot.dtype
            )
            for start, stop in spans
        ],
        compiler_params=pltpu.CompilerParams(vmem_limit_bytes=24 * MIB),
        cost_estimate=pl.CostEstimate(
            flops=0, bytes_accessed=4 * cot.size // stride, transcendentals=0
        ),
        name="cut_columns",
    )(cot)


def chunk_kernel(hi_count, zl_count, narrow_count, natural, place_ref, *refs):
    features = zl_count * narrow_count
    pieces = 2 if natural else 2 * hi_count
    xt = refs[:features]
    cots = refs[features : features + pieces]
    signs = refs[features + pieces : features + pieces + zl_count]
    row_mix, out_ref, cot_ref, xt_ref, sems = refs[-5:]
    hi, core, narrow = place_ref[0], place_ref[1], place_ref[2]
    token_shard = xt[0].shape[1]
    tokens = cots[0].shape[1]

    def feature_copy(d, e):
        spot = pl.ds(pl.multiple_of((narrow ^ e) * token_shard, token_shard), token_shard)
        k = d * narrow_count + e
        return pltpu.make_async_copy(xt[k], xt_ref.at[d, :, spot], sems.at[k])

    @pl.when(pl.program_id(0) == 0)
    def _():
        for d in range(zl_count):
            for e in range(narrow_count):
                feature_copy(d, e).start()

    for h in range(hi_count):
        for c in range(2):
            for z in range(zl_count):
                source = ((h if natural else hi ^ h) * zl_count + z) * 2 + (core ^ c)
                spot = pl.ds(pl.multiple_of(source * tokens, tokens), tokens)
                if natural:
                    cot_ref[spot, :] = cots[c][h * zl_count + z]
                else:
                    cot_ref[spot, :] = cots[2 * h + c][z]

    mixed = []
    for d in range(zl_count):

        @pl.when(pl.program_id(0) == 0)
        def _():
            for e in range(narrow_count):
                feature_copy(d, e).wait()

        value = jnp.dot(xt_ref[d], cot_ref[...], preferred_element_type=jnp.float32)
        value = value * signs[d][...].astype(jnp.float32)
        high = value.astype(jnp.bfloat16)
        low = (value - high.astype(jnp.float32)).astype(jnp.bfloat16)
        mixed.append(
            jnp.dot(row_mix[...], high, preferred_element_type=jnp.float32)
            + jnp.dot(row_mix[...], low, preferred_element_type=jnp.float32)
        )
    mixed = butterfly(mixed)
    for b in range(out_ref.shape[0]):
        for d in range(zl_count):
            out_ref[b, d] = mixed[d][:, b * LANES : (b + 1) * LANES]


def chunk_call(place, xt, cots, signs, row_mix, tile, start, steps, hi_count):
    zl_count, narrow_count = len(signs), len(xt) // len(signs)
    natural = len(cots) == 2
    rows, token_shard = xt[0].shape
    groups, tokens, _ = cots[0].shape
    total = token_shard * narrow_count
    return pl.pallas_call(
        functools.partial(chunk_kernel, hi_count, zl_count, narrow_count, natural),
        grid_spec=pltpu.PrefetchScalarGridSpec(
            num_scalar_prefetch=1,
            grid=(steps,),
            in_specs=[pl.BlockSpec(memory_space=pl.ANY) for _ in xt]
            + [
                pl.BlockSpec((groups, tokens, tile), lambda i, p: (0, 0, i)) for _ in cots
            ]
            + [pl.BlockSpec((rows, tile), lambda i, p: (0, start + i)) for _ in signs]
            + [
                pl.BlockSpec(
                    (rows, rows), lambda i, p: (0, 0), pipeline_mode=pl.Buffered(1)
                )
            ],
            out_specs=pl.BlockSpec(
                (tile // LANES, zl_count, rows, LANES), lambda i, p: (i, 0, 0, 0)
            ),
            scratch_shapes=[
                pltpu.VMEM((total, tile), cots[0].dtype),
                pltpu.VMEM((zl_count, rows, total), xt[0].dtype),
                pltpu.SemaphoreType.DMA((len(xt),)),
            ],
        ),
        out_shape=jax.ShapeDtypeStruct(
            (steps * tile // LANES, zl_count, rows, LANES), jnp.float32
        ),
        compiler_params=pltpu.CompilerParams(vmem_limit_bytes=40 * MIB),
        cost_estimate=pl.CostEstimate(
            flops=2 * zl_count * rows * steps * tile * token_shard,
            bytes_accessed=4 * zl_count * rows * steps * tile,
            transcendentals=0,
        ),
        name="gradient_rows",
    )(place, *xt, *cots, *signs, row_mix)


def pick_kernel(parts, index_ref, *refs):
    blocks = refs[:parts]
    lane_signs, out_ref, mixed_ref, rows_ref = refs[parts:]
    rows = blocks[0].shape[1]
    slabs = [(block, b) for block in blocks for b in range(block.shape[0])]

    def mix(i, carry):
        spot = pl.ds(pl.multiple_of(i * 8, 8), 8)
        values = [block[b, spot, :] for block, b in slabs]
        for b, value in enumerate(butterfly(values)):
            mixed_ref[pl.ds(pl.multiple_of(b * rows + i * 8, 8), 8), :] = value
        return carry

    lax.fori_loop(0, rows // 8, mix, 0)

    def group(g, carry):
        for j in range(LANES):
            row = index_ref[g * LANES + j]
            rows_ref[pl.ds(j, 1), :] = mixed_ref[pl.ds(row, 1), :]
        spot = pl.ds(pl.multiple_of(g * LANES, LANES), LANES)
        product = rows_ref[...] * lane_signs[spot, :].astype(jnp.float32)
        out_ref[pl.ds(g, 1), :] = jnp.sum(product.T, axis=0, keepdims=True)
        return carry

    lax.fori_loop(0, out_ref.shape[0], group, 0)


def pick_call(index, blocks, lane_signs):
    picks = index.shape[0]
    total = sum(block.shape[0] * block.shape[1] for block in blocks)
    return pl.pallas_call(
        functools.partial(pick_kernel, len(blocks)),
        grid_spec=pltpu.PrefetchScalarGridSpec(
            num_scalar_prefetch=1,
            grid=(1,),
            in_specs=[
                pl.BlockSpec(
                    block.shape, lambda i, p: (0, 0, 0), pipeline_mode=pl.Buffered(1)
                )
                for block in blocks
            ]
            + [
                pl.BlockSpec(
                    (picks, LANES), lambda i, p: (0, 0), pipeline_mode=pl.Buffered(1)
                )
            ],
            out_specs=pl.BlockSpec((picks // LANES, LANES), lambda i, p: (0, 0)),
            scratch_shapes=[
                pltpu.VMEM((total, LANES), jnp.float32),
                pltpu.VMEM((LANES, LANES), jnp.float32),
            ],
        ),
        out_shape=jax.ShapeDtypeStruct((picks // LANES, LANES), jnp.float32),
        compiler_params=pltpu.CompilerParams(vmem_limit_bytes=40 * MIB),
        cost_estimate=pl.CostEstimate(
            flops=8 * total * LANES, bytes_accessed=4 * total * LANES, transcendentals=0
        ),
        name="pick_samples",
    )(index, *blocks, lane_signs)


def parity_sign(bits):
    for shift in (16, 8, 4, 2, 1):
        bits = bits ^ (bits >> shift)
    return 1 - 2 * (bits & 1)


def swap(value, axis, offset):
    count = lax.axis_size(axis)
    return lax.ppermute(value, axis, [(i, i ^ offset) for i in range(count)])


def after(value, *others):
    return lax.optimization_barrier((value, *others))[0]


def body(inputs, out_cotangent, sign_bits, row_pick, col_pick):
    hi_count = lax.axis_size("hi")
    zl_count = lax.axis_size("zl")
    narrow_count = lax.axis_size("narrow")
    hi, zl, core, narrow = [lax.axis_index(a) for a in ALL_AXES]
    wide_count = hi_count * zl_count * 2
    token_shard, rows = inputs.shape[1:]
    col_shard = sign_bits.shape[2]
    col_dev = col_shard // zl_count
    tokens = token_shard * narrow_count // wide_count
    tile, chunks = plan_chunks(col_dev)
    edges = [tile * sum(chunks[:i]) for i in range(len(chunks) + 1)]
    spans = list(zip(edges, edges[1:]))
    cot = out_cotangent[0, 0]
    cut = prepare(cot, zl_count, narrow_count, col_dev, col_dev, spans)

    def spread(value):
        return lax.all_to_all(value, ("zl", "narrow"), 0, 0, tiled=True)

    def gather(value):
        return lax.all_gather(value, "hi", axis=0, tiled=True)

    own_0 = spread(cut[0])
    both_0 = gather(own_0)
    own_1 = spread(after(cut[1], own_0))
    far_1 = [swap(own_1, "hi", h) for h in range(1, hi_count)]

    own_xt = after(inputs[0], own_0).T
    xt_parts = [swap(own_xt, "zl", d) if d else own_xt for d in range(zl_count)]
    own_2 = spread(after(cut[2], own_1, *far_1, *xt_parts))
    both_2 = gather(own_2)
    xt = []
    for part in xt_parts:
        xt += [part] + [swap(part, "narrow", e) for e in range(1, narrow_count)]

    bits = after(sign_bits[0], own_0)
    signs = []
    for d in range(zl_count):
        part = lax.dynamic_slice_in_dim(bits, (zl ^ d) * col_dev, col_dev, axis=1)
        part = (2 * part - 1).astype(jnp.bfloat16)
        signs.append(swap(part, "zl", d) if d else part)

    row_mix = jnp.asarray(hadamard(rows), jnp.bfloat16)
    place = after(jnp.stack([hi, core, narrow]).astype(jnp.int32), own_2)
    blocks = [None] * len(chunks)
    parts = [[both_0], [own_1] + far_1, [both_2]]
    for index in (1, 0, 2):
        ready = {0: [own_2, *xt, *signs], 1: [], 2: [blocks[0]]}[index]
        cots = []
        for piece in parts[index]:
            piece = after(piece, *ready) if ready else piece
            cots += [piece, swap(piece, "core", 1)]
        width = tile * chunks[index]
        cots = [c.reshape(-1, tokens, width) for c in cots]
        done = chunk_call(
            place, xt, cots, signs, row_mix, tile, edges[index] // tile, chunks[index], hi_count
        )
        place = after(place, done)
        blocks[index] = done.reshape(-1, zl_count * rows, LANES)

    row, col = row_pick[0], col_pick[0]
    block = (col // LANES) % (col_dev // LANES)
    row_in = (row // (2 * rows)) % zl_count * rows + row % rows
    position = block * (zl_count * rows) + row_in
    row_base = ((hi * zl_count + zl) * 2 + core) * rows
    col_base = narrow * col_shard + zl * col_dev
    lane = lax.broadcasted_iota(jnp.int32, (1, LANES), 1)
    fold = parity_sign((row & row_base)[:, None]) * parity_sign((col_base + lane) & col[:, None])
    picked = pick_call(position, blocks, fold.astype(jnp.bfloat16))

    devices = wide_count * narrow_count
    terms = lax.all_to_all(
        picked.reshape(devices, row.shape[0] // devices), ALL_AXES, 0, 0, tiled=True
    )
    total = jnp.sum(terms, axis=0) / jnp.sqrt(jnp.float32(row.shape[0]))
    return total.reshape(1, 1, -1)


def solution(mesh):
    wide, narrow = mesh.shape["wide"], mesh.shape["narrow"]
    sizes = (2, wide // 4, 2, narrow)
    split = Mesh(mesh.devices.reshape(sizes), ALL_AXES)
    wide_axes = ("hi", "zl", "core")
    return jax.shard_map(
        body,
        mesh=split,
        in_specs=(
            P(None, "narrow", wide_axes),
            P(None, None, ALL_AXES, None),
            P(None, wide_axes, "narrow"),
            P(),
            P(),
        ),
        out_specs=P(None, None, ALL_AXES),
        check_vma=False,
    )
```

```python
import functools

import jax
import jax.numpy as jnp
import numpy as np
from jax import lax
from jax.experimental import pallas as pl
from jax.experimental.pallas import tpu as pltpu
from jax.sharding import Mesh, PartitionSpec as P

LANES = 128
UNITS = 8
MIB = 1024 * 1024
ALL_AXES = ("hi", "zl", "core", "narrow")


def hadamard(length):
    h = np.ones((1, 1), np.float32)
    while h.shape[0] < length:
        h = np.block([[h, h], [h, -h]])
    return h


def butterfly(parts):
    step = 1
    while step < len(parts):
        parts = [
            parts[i] + parts[i ^ step] if not i & step else parts[i ^ step] - parts[i]
            for i in range(len(parts))
        ]
        step *= 2
    return parts


def plan_chunks(col_dev):
    tile = max(LANES, min(256, col_dev // UNITS))
    units = col_dev // tile
    middle = units - 2
    return tile, [1] + [2] * (middle // 2) + [1] * (middle % 2) + [1]


def prep_kernel(real_blocks, zl_count, widths, in_ref, *out_refs):
    block = pl.program_id(1) * zl_count + pl.program_id(0)
    keep = block < real_blocks
    start = 0
    for width, out_ref in zip(widths, out_refs):
        value = in_ref[:, start : start + width]
        out_ref[0] = jnp.where(keep, value, jnp.zeros_like(value))
        start += width


def prepare(cot, zl_count, narrow_count, widths):
    tokens, hidden = cot.shape
    col_dev = sum(widths)
    real_blocks = hidden // col_dev
    return pl.pallas_call(
        functools.partial(prep_kernel, real_blocks, zl_count, widths),
        grid=(zl_count, narrow_count),
        in_specs=[
            pl.BlockSpec(
                (tokens, col_dev),
                lambda z, n: (0, jnp.minimum(n * zl_count + z, real_blocks - 1)),
            )
        ],
        out_specs=[
            pl.BlockSpec((1, tokens, width), lambda z, n: (z * narrow_count + n, 0, 0))
            for width in widths
        ],
        out_shape=[
            jax.ShapeDtypeStruct((zl_count * narrow_count, tokens, width), cot.dtype)
            for width in widths
        ],
        compiler_params=pltpu.CompilerParams(vmem_limit_bytes=24 * MIB),
        cost_estimate=pl.CostEstimate(
            flops=0, bytes_accessed=4 * cot.size, transcendentals=0
        ),
        name="cut_columns",
    )(cot)


def chunk_kernel(hi_count, zl_count, place_ref, *refs):
    xt = refs[:zl_count]
    cots = refs[zl_count : zl_count + 2 * hi_count]
    signs = refs[zl_count + 2 * hi_count : 2 * zl_count + 2 * hi_count]
    row_mix = refs[-2]
    out_ref = refs[-1]
    hi, core = place_ref[0], place_ref[2]
    mixed = []
    for d in range(zl_count):
        total = None
        for h in range(hi_count):
            for c in range(2):
                for z in range(zl_count):
                    source = ((hi ^ h) * zl_count + z) * 2 + (core ^ c)
                    term = jnp.dot(
                        xt[d][source],
                        cots[h * 2 + c][z],
                        preferred_element_type=jnp.float32,
                    )
                    total = term if total is None else total + term
        value = total * signs[d][...].astype(jnp.float32)
        high = value.astype(jnp.bfloat16)
        low = (value - high.astype(jnp.float32)).astype(jnp.bfloat16)
        mixed.append(
            jnp.dot(row_mix[...], high, preferred_element_type=jnp.float32)
            + jnp.dot(row_mix[...], low, preferred_element_type=jnp.float32)
        )
    mixed = butterfly(mixed)
    for b in range(out_ref.shape[0]):
        for d in range(zl_count):
            out_ref[b, d] = mixed[d][:, b * LANES : (b + 1) * LANES]


def chunk_call(place, xt, cots, signs, row_mix, tile, steps, hi_count):
    zl_count = len(xt)
    sources, rows, tokens = xt[0].shape
    chunk = tile * steps
    resident = pl.Buffered(1)
    return pl.pallas_call(
        functools.partial(chunk_kernel, hi_count, zl_count),
        grid_spec=pltpu.PrefetchScalarGridSpec(
            num_scalar_prefetch=1,
            grid=(steps,),
            in_specs=[
                pl.BlockSpec(
                    (sources, rows, tokens), lambda i, p: (0, 0, 0), pipeline_mode=resident
                )
                for _ in xt
            ]
            + [
                pl.BlockSpec((zl_count, tokens, tile), lambda i, p: (0, 0, i))
                for _ in cots
            ]
            + [
                pl.BlockSpec((rows, tile), lambda i, p: (0, i))
                for _ in signs
            ]
            + [
                pl.BlockSpec((rows, rows), lambda i, p: (0, 0), pipeline_mode=resident)
            ],
            out_specs=pl.BlockSpec(
                (tile // LANES, zl_count, rows, LANES), lambda i, p: (i, 0, 0, 0)
            ),
        ),
        out_shape=jax.ShapeDtypeStruct(
            (chunk // LANES, zl_count, rows, LANES), jnp.float32
        ),
        compiler_params=pltpu.CompilerParams(vmem_limit_bytes=40 * MIB),
        cost_estimate=pl.CostEstimate(
            flops=zl_count * rows * chunk * tokens,
            bytes_accessed=4 * zl_count * rows * chunk,
            transcendentals=0,
        ),
        name="gradient_rows",
    )(place, *xt, *cots, *signs, row_mix)


def pick_kernel(parts, index_ref, *refs):
    blocks = refs[:parts]
    lane_signs, out_ref, mixed_ref, rows_ref = refs[parts:]
    rows = blocks[0].shape[1]
    slabs = [(block, b) for block in blocks for b in range(block.shape[0])]

    def mix(i, carry):
        spot = pl.ds(pl.multiple_of(i * 8, 8), 8)
        values = [block[b, spot, :] for block, b in slabs]
        for b, value in enumerate(butterfly(values)):
            mixed_ref[pl.ds(pl.multiple_of(b * rows + i * 8, 8), 8), :] = value
        return carry

    lax.fori_loop(0, rows // 8, mix, 0)

    def group(g, carry):
        for j in range(LANES):
            row = index_ref[g * LANES + j]
            rows_ref[pl.ds(j, 1), :] = mixed_ref[pl.ds(row, 1), :]
        spot = pl.ds(pl.multiple_of(g * LANES, LANES), LANES)
        product = rows_ref[...] * lane_signs[spot, :].astype(jnp.float32)
        out_ref[pl.ds(g, 1), :] = jnp.sum(product.T, axis=0, keepdims=True)
        return carry

    lax.fori_loop(0, out_ref.shape[0], group, 0)


def pick_call(index, blocks, lane_signs):
    picks = index.shape[0]
    total = sum(block.shape[0] * block.shape[1] for block in blocks)
    return pl.pallas_call(
        functools.partial(pick_kernel, len(blocks)),
        grid_spec=pltpu.PrefetchScalarGridSpec(
            num_scalar_prefetch=1,
            grid=(1,),
            in_specs=[
                pl.BlockSpec(
                    block.shape, lambda i, p: (0, 0, 0), pipeline_mode=pl.Buffered(1)
                )
                for block in blocks
            ]
            + [
                pl.BlockSpec(
                    (picks, LANES), lambda i, p: (0, 0), pipeline_mode=pl.Buffered(1)
                )
            ],
            out_specs=pl.BlockSpec((picks // LANES, LANES), lambda i, p: (0, 0)),
            scratch_shapes=[
                pltpu.VMEM((total, LANES), jnp.float32),
                pltpu.VMEM((LANES, LANES), jnp.float32),
            ],
        ),
        out_shape=jax.ShapeDtypeStruct((picks // LANES, LANES), jnp.float32),
        compiler_params=pltpu.CompilerParams(vmem_limit_bytes=40 * MIB),
        cost_estimate=pl.CostEstimate(
            flops=8 * total * LANES, bytes_accessed=4 * total * LANES, transcendentals=0
        ),
        name="pick_samples",
    )(index, *blocks, lane_signs)


def parity_sign(bits):
    for shift in (16, 8, 4, 2, 1):
        bits = bits ^ (bits >> shift)
    return 1 - 2 * (bits & 1)


def swap(value, axis, offset):
    count = lax.axis_size(axis)
    return lax.ppermute(value, axis, [(i, i ^ offset) for i in range(count)])


def after(value, *others):
    return lax.optimization_barrier((value, *others))[0]


def body(inputs, out_cotangent, sign_bits, row_pick, col_pick):
    hi_count = lax.axis_size("hi")
    zl_count = lax.axis_size("zl")
    narrow_count = lax.axis_size("narrow")
    hi, zl, core, narrow = [lax.axis_index(a) for a in ALL_AXES]
    wide_count = hi_count * zl_count * 2
    token_shard, rows = inputs.shape[1:]
    col_shard = sign_bits.shape[2]
    col_dev = col_shard // zl_count
    tile, chunks = plan_chunks(col_dev)
    tokens = token_shard * narrow_count // wide_count
    cut = prepare(
        out_cotangent[0, 0], zl_count, narrow_count, [tile * steps for steps in chunks]
    )

    own_xt = inputs[0].reshape(token_shard // tokens, tokens, rows).swapaxes(1, 2)
    xt_parts = [swap(own_xt, "zl", d) if d else own_xt for d in range(zl_count)]

    row_mix = jnp.asarray(hadamard(rows), jnp.bfloat16)
    place = jnp.stack([hi, zl, core]).astype(jnp.int32)
    edges = [tile * sum(chunks[:i]) for i in range(len(chunks) + 1)]
    count = len(chunks)
    own, far, signs, swapped = {}, {}, {}, {}
    blocks, xt = [], None
    cut = list(cut)
    bits = sign_bits[0]

    def sign_block(d, index):
        start = (zl ^ d) * col_dev + edges[index]
        part = lax.dynamic_slice_in_dim(bits, start, tile * chunks[index], axis=1)
        return (2 * part - 1).astype(jnp.bfloat16)

    for stage in range(count + 2):
        if stage < count:
            own[stage] = lax.all_to_all(cut[stage], ("zl", "narrow"), 0, 0, tiled=True)
            signs[stage] = [sign_block(d, stage) for d in range(zl_count)]
        if 1 <= stage <= count:
            c = stage - 1
            far[c] = [swap(own[c], "hi", h) for h in range(1, hi_count)]
            signs[c] = [swap(x, "zl", d) if d else x for d, x in enumerate(signs[c])]
        if stage >= 2:
            c = stage - 2
            swapped[c] = [swap(x, "core", 1) for x in [own[c]] + far[c]]
        ready = {count - 1: range(count - 3), count: [count - 3], count + 1: [count - 2]}
        for c in ready.get(stage, []):
            pairs = zip([own[c]] + far[c], swapped[c])
            cots = [
                x.reshape(zl_count, tokens, tile * chunks[c]) for pair in pairs for x in pair
            ]
            done = chunk_call(
                place, xt, cots, signs[c], row_mix, tile, chunks[c], hi_count
            )
            blocks.append(done.reshape(-1, zl_count * rows, LANES))
            place = after(place, done)
        state = (cut, own, far, signs, swapped, blocks, bits, place, xt_parts)
        state = lax.optimization_barrier(state)
        cut, own, far, signs, swapped, blocks, bits, place, xt_parts = state
        if stage == 0:
            xt = [lax.all_gather(x, "narrow", axis=0, tiled=True) for x in [own_xt] + xt_parts[1:]]
    c = count - 1
    pairs = zip([own[c]] + far[c], swapped[c])
    cots = [x.reshape(zl_count, tokens, tile * chunks[c]) for pair in pairs for x in pair]
    done = chunk_call(place, xt, cots, signs[c], row_mix, tile, chunks[c], hi_count)
    blocks.append(done.reshape(-1, zl_count * rows, LANES))

    row, col = row_pick[0], col_pick[0]
    block = (col // LANES) % (col_dev // LANES)
    row_in = (row // (2 * rows)) % zl_count * rows + row % rows
    position = block * (zl_count * rows) + row_in
    row_base = ((hi * zl_count + zl) * 2 + core) * rows
    col_base = narrow * col_shard + zl * col_dev
    lane = lax.broadcasted_iota(jnp.int32, (1, LANES), 1)
    fold = parity_sign((row & row_base)[:, None]) * parity_sign((col_base + lane) & col[:, None])
    picked = pick_call(position, blocks, fold.astype(jnp.bfloat16))

    devices = wide_count * narrow_count
    terms = lax.all_to_all(
        picked.reshape(devices, row.shape[0] // devices), ALL_AXES, 0, 0, tiled=True
    )
    total = jnp.sum(terms, axis=0) / jnp.sqrt(jnp.float32(row.shape[0]))
    return total.reshape(1, 1, -1)


def solution(mesh):
    wide, narrow = mesh.shape["wide"], mesh.shape["narrow"]
    sizes = (2, wide // 4, 2, narrow)
    split = Mesh(mesh.devices.reshape(sizes), ALL_AXES)
    wide_axes = ("hi", "zl", "core")
    return jax.shard_map(
        body,
        mesh=split,
        in_specs=(
            P(None, "narrow", wide_axes),
            P(None, None, ALL_AXES, None),
            P(None, wide_axes, "narrow"),
            P(),
            P(),
        ),
        out_specs=P(None, None, ALL_AXES),
        check_vma=False,
    )
```

```python
import functools

import jax
import jax.numpy as jnp
import numpy as np
from jax import lax
from jax.experimental import pallas as pl
from jax.experimental.pallas import tpu as pltpu
from jax.sharding import Mesh, PartitionSpec as P

LANES = 128
UNITS = 8
MIB = 1024 * 1024
ALL_AXES = ("hi", "zl", "core", "narrow")


def hadamard(length):
    h = np.ones((1, 1), np.float32)
    while h.shape[0] < length:
        h = np.block([[h, h], [h, -h]])
    return h


def butterfly(parts):
    step = 1
    while step < len(parts):
        parts = [
            parts[i] + parts[i ^ step] if not i & step else parts[i ^ step] - parts[i]
            for i in range(len(parts))
        ]
        step *= 2
    return parts


def plan_chunks(col_dev):
    tile = max(LANES, min(256, col_dev // UNITS))
    units = col_dev // tile
    middle = (units - 2) // 2
    return tile, [1, units - 2 - middle, middle, 1]


def prep_kernel(real_blocks, zl_count, widths, in_ref, *out_refs):
    block = pl.program_id(1) * zl_count + pl.program_id(0)
    keep = block < real_blocks
    start = 0
    for width, out_ref in zip(widths, out_refs):
        value = in_ref[:, start : start + width]
        out_ref[0] = jnp.where(keep, value, jnp.zeros_like(value))
        start += width


def prepare(cot, zl_count, narrow_count, widths):
    tokens, hidden = cot.shape
    col_dev = sum(widths)
    real_blocks = hidden // col_dev
    return pl.pallas_call(
        functools.partial(prep_kernel, real_blocks, zl_count, widths),
        grid=(zl_count, narrow_count),
        in_specs=[
            pl.BlockSpec(
                (tokens, col_dev),
                lambda z, n: (0, jnp.minimum(n * zl_count + z, real_blocks - 1)),
            )
        ],
        out_specs=[
            pl.BlockSpec((1, tokens, width), lambda z, n: (z * narrow_count + n, 0, 0))
            for width in widths
        ],
        out_shape=[
            jax.ShapeDtypeStruct((zl_count * narrow_count, tokens, width), cot.dtype)
            for width in widths
        ],
        compiler_params=pltpu.CompilerParams(vmem_limit_bytes=24 * MIB),
        cost_estimate=pl.CostEstimate(
            flops=0, bytes_accessed=4 * cot.size, transcendentals=0
        ),
        name="cut_columns",
    )(cot)


def chunk_kernel(hi_count, zl_count, place_ref, *refs):
    xt = refs[:zl_count]
    cots = refs[zl_count : zl_count + 2 * hi_count]
    signs = refs[zl_count + 2 * hi_count : 2 * zl_count + 2 * hi_count]
    row_mix = refs[-2]
    out_ref = refs[-1]
    hi, core = place_ref[0], place_ref[2]
    mixed = []
    for d in range(zl_count):
        total = None
        for h in range(hi_count):
            for c in range(2):
                for z in range(zl_count):
                    source = ((hi ^ h) * zl_count + z) * 2 + (core ^ c)
                    term = jnp.dot(
                        xt[d][source],
                        cots[h * 2 + c][z],
                        preferred_element_type=jnp.float32,
                    )
                    total = term if total is None else total + term
        value = total * signs[d][...].astype(jnp.float32)
        high = value.astype(jnp.bfloat16)
        low = (value - high.astype(jnp.float32)).astype(jnp.bfloat16)
        mixed.append(
            jnp.dot(row_mix[...], high, preferred_element_type=jnp.float32)
            + jnp.dot(row_mix[...], low, preferred_element_type=jnp.float32)
        )
    mixed = butterfly(mixed)
    for b in range(out_ref.shape[0]):
        for d in range(zl_count):
            out_ref[b, d] = mixed[d][:, b * LANES : (b + 1) * LANES]


def chunk_call(place, xt, cots, signs, row_mix, tile, steps, hi_count):
    zl_count = len(xt)
    sources, rows, tokens = xt[0].shape
    chunk = tile * steps
    resident = pl.Buffered(1)
    return pl.pallas_call(
        functools.partial(chunk_kernel, hi_count, zl_count),
        grid_spec=pltpu.PrefetchScalarGridSpec(
            num_scalar_prefetch=1,
            grid=(steps,),
            in_specs=[
                pl.BlockSpec(
                    (sources, rows, tokens), lambda i, p: (0, 0, 0), pipeline_mode=resident
                )
                for _ in xt
            ]
            + [
                pl.BlockSpec((zl_count, tokens, tile), lambda i, p: (0, 0, i))
                for _ in cots
            ]
            + [
                pl.BlockSpec((rows, tile), lambda i, p: (0, i))
                for _ in signs
            ]
            + [
                pl.BlockSpec((rows, rows), lambda i, p: (0, 0), pipeline_mode=resident)
            ],
            out_specs=pl.BlockSpec(
                (tile // LANES, zl_count, rows, LANES), lambda i, p: (i, 0, 0, 0)
            ),
        ),
        out_shape=jax.ShapeDtypeStruct(
            (chunk // LANES, zl_count, rows, LANES), jnp.float32
        ),
        compiler_params=pltpu.CompilerParams(vmem_limit_bytes=40 * MIB),
        cost_estimate=pl.CostEstimate(
            flops=zl_count * rows * chunk * tokens,
            bytes_accessed=4 * zl_count * rows * chunk,
            transcendentals=0,
        ),
        name="gradient_rows",
    )(place, *xt, *cots, *signs, row_mix)


def pick_kernel(parts, index_ref, *refs):
    blocks = refs[:parts]
    lane_signs, out_ref, mixed_ref, rows_ref = refs[parts:]
    rows = blocks[0].shape[1]
    slabs = [(block, b) for block in blocks for b in range(block.shape[0])]

    def mix(i, carry):
        spot = pl.ds(pl.multiple_of(i * 8, 8), 8)
        values = [block[b, spot, :] for block, b in slabs]
        for b, value in enumerate(butterfly(values)):
            mixed_ref[pl.ds(pl.multiple_of(b * rows + i * 8, 8), 8), :] = value
        return carry

    lax.fori_loop(0, rows // 8, mix, 0)

    def group(g, carry):
        for j in range(LANES):
            row = index_ref[g * LANES + j]
            rows_ref[pl.ds(j, 1), :] = mixed_ref[pl.ds(row, 1), :]
        spot = pl.ds(pl.multiple_of(g * LANES, LANES), LANES)
        product = rows_ref[...] * lane_signs[spot, :].astype(jnp.float32)
        out_ref[pl.ds(g, 1), :] = jnp.sum(product.T, axis=0, keepdims=True)
        return carry

    lax.fori_loop(0, out_ref.shape[0], group, 0)


def pick_call(index, blocks, lane_signs):
    picks = index.shape[0]
    total = sum(block.shape[0] * block.shape[1] for block in blocks)
    return pl.pallas_call(
        functools.partial(pick_kernel, len(blocks)),
        grid_spec=pltpu.PrefetchScalarGridSpec(
            num_scalar_prefetch=1,
            grid=(1,),
            in_specs=[
                pl.BlockSpec(
                    block.shape, lambda i, p: (0, 0, 0), pipeline_mode=pl.Buffered(1)
                )
                for block in blocks
            ]
            + [
                pl.BlockSpec(
                    (picks, LANES), lambda i, p: (0, 0), pipeline_mode=pl.Buffered(1)
                )
            ],
            out_specs=pl.BlockSpec((picks // LANES, LANES), lambda i, p: (0, 0)),
            scratch_shapes=[
                pltpu.VMEM((total, LANES), jnp.float32),
                pltpu.VMEM((LANES, LANES), jnp.float32),
            ],
        ),
        out_shape=jax.ShapeDtypeStruct((picks // LANES, LANES), jnp.float32),
        compiler_params=pltpu.CompilerParams(vmem_limit_bytes=40 * MIB),
        cost_estimate=pl.CostEstimate(
            flops=8 * total * LANES, bytes_accessed=4 * total * LANES, transcendentals=0
        ),
        name="pick_samples",
    )(index, *blocks, lane_signs)


def parity_sign(bits):
    for shift in (16, 8, 4, 2, 1):
        bits = bits ^ (bits >> shift)
    return 1 - 2 * (bits & 1)


def swap(value, axis, offset):
    count = lax.axis_size(axis)
    return lax.ppermute(value, axis, [(i, i ^ offset) for i in range(count)])


def after(value, *others):
    return lax.optimization_barrier((value, *others))[0]


def body(inputs, out_cotangent, sign_bits, row_pick, col_pick):
    hi_count = lax.axis_size("hi")
    zl_count = lax.axis_size("zl")
    narrow_count = lax.axis_size("narrow")
    hi, zl, core, narrow = [lax.axis_index(a) for a in ALL_AXES]
    wide_count = hi_count * zl_count * 2
    token_shard, rows = inputs.shape[1:]
    col_shard = sign_bits.shape[2]
    col_dev = col_shard // zl_count
    tile, chunks = plan_chunks(col_dev)
    tokens = token_shard * narrow_count // wide_count
    cut = prepare(
        out_cotangent[0, 0], zl_count, narrow_count, [tile * steps for steps in chunks]
    )

    own_xt = inputs[0].reshape(token_shard // tokens, tokens, rows).swapaxes(1, 2)
    xt_parts = [swap(own_xt, "zl", d) if d else own_xt for d in range(zl_count)]

    row_mix = jnp.asarray(hadamard(rows), jnp.bfloat16)
    place = jnp.stack([hi, zl, core]).astype(jnp.int32)
    edges = [tile * sum(chunks[:i]) for i in range(len(chunks) + 1)]
    count = len(chunks)
    own, far, signs, swapped = {}, {}, {}, {}
    blocks, xt = [], None
    cut = list(cut)
    bits = sign_bits[0]
    samples = (row_pick[0], col_pick[0])

    def sign_block(d, index):
        start = (zl ^ d) * col_dev + edges[index]
        part = lax.dynamic_slice_in_dim(bits, start, tile * chunks[index], axis=1)
        return (2 * part - 1).astype(jnp.bfloat16)

    for stage in range(count + 2):
        if stage < count:
            own[stage] = lax.all_to_all(cut[stage], ("zl", "narrow"), 0, 0, tiled=True)
            signs[stage] = [sign_block(d, stage) for d in range(zl_count)]
        if 1 <= stage <= count:
            c = stage - 1
            far[c] = [swap(own[c], "hi", h) for h in range(1, hi_count)]
            swapped[c] = [swap(own[c], "core", 1)]
            signs[c] = [swap(x, "zl", d) if d else x for d, x in enumerate(signs[c])]
        if stage >= 2:
            c = stage - 2
            swapped[c] += [swap(x, "core", 1) for x in far[c]]
        ready = {count - 1: range(count - 2), count: [count - 2], count + 1: [count - 1]}
        for c in ready.get(stage, []):
            pairs = zip([own[c]] + far[c], swapped[c])
            cots = [
                x.reshape(zl_count, tokens, tile * chunks[c]) for pair in pairs for x in pair
            ]
            done = chunk_call(
                place, xt, cots, signs[c], row_mix, tile, chunks[c], hi_count
            )
            blocks.append(done.reshape(-1, zl_count * rows, LANES))
            place = after(place, done)
        if stage == 2:
            row, col = samples
            block = (col // LANES) % (col_dev // LANES)
            row_in = (row // (2 * rows)) % zl_count * rows + row % rows
            position = block * (zl_count * rows) + row_in
            row_base = ((hi * zl_count + zl) * 2 + core) * rows
            col_base = narrow * col_shard + zl * col_dev
            lane = lax.broadcasted_iota(jnp.int32, (1, LANES), 1)
            fold = parity_sign((row & row_base)[:, None]) * parity_sign((col_base + lane) & col[:, None])
            samples = (position, fold.astype(jnp.bfloat16))
        state = (cut, own, far, signs, swapped, blocks, bits, place, xt_parts, samples)
        state = lax.optimization_barrier(state)
        cut, own, far, signs, swapped, blocks, bits, place, xt_parts, samples = state
        if stage == 0:
            xt = [lax.all_gather(x, "narrow", axis=0, tiled=True) for x in [own_xt] + xt_parts[1:]]
    position, lane_signs = samples
    picked = pick_call(position, blocks, lane_signs)

    devices = wide_count * narrow_count
    terms = lax.all_to_all(
        picked.reshape(devices, position.shape[0] // devices), ALL_AXES, 0, 0, tiled=True
    )
    total = jnp.sum(terms, axis=0) / jnp.sqrt(jnp.float32(position.shape[0]))
    return total.reshape(1, 1, -1)


def solution(mesh):
    wide, narrow = mesh.shape["wide"], mesh.shape["narrow"]
    sizes = (2, wide // 4, 2, narrow)
    split = Mesh(mesh.devices.reshape(sizes), ALL_AXES)
    wide_axes = ("hi", "zl", "core")
    return jax.shard_map(
        body,
        mesh=split,
        in_specs=(
            P(None, "narrow", wide_axes),
            P(None, None, ALL_AXES, None),
            P(None, wide_axes, "narrow"),
            P(),
            P(),
        ),
        out_specs=P(None, None, ALL_AXES),
        check_vma=False,
    )
```

```python
import functools

import jax
import jax.numpy as jnp
import numpy as np
from jax import lax
from jax.experimental import pallas as pl
from jax.experimental.pallas import tpu as pltpu
from jax.sharding import Mesh, PartitionSpec as P

LANES = 128
UNITS = 8
MIB = 1024 * 1024
ALL_AXES = ("hi", "zl", "core", "narrow")


def hadamard(length):
    h = np.ones((1, 1), np.float32)
    while h.shape[0] < length:
        h = np.block([[h, h], [h, -h]])
    return h


def butterfly(parts):
    step = 1
    while step < len(parts):
        parts = [
            parts[i] + parts[i ^ step] if not i & step else parts[i ^ step] - parts[i]
            for i in range(len(parts))
        ]
        step *= 2
    return parts


def plan_chunks(col_dev):
    tile = max(LANES, min(256, col_dev // UNITS))
    units = col_dev // tile
    first, second, last = max(1, units // 4), max(1, units * 3 // 8), max(1, units // 8)
    return tile, [first, second, units - first - second - last, last]


def prep_kernel(real_blocks, zl_count, widths, in_ref, *out_refs):
    block = pl.program_id(1) * zl_count + pl.program_id(0)
    keep = block < real_blocks
    start = 0
    for width, out_ref in zip(widths, out_refs):
        value = in_ref[:, start : start + width]
        out_ref[0] = jnp.where(keep, value, jnp.zeros_like(value))
        start += width


def prepare(cot, zl_count, narrow_count, widths):
    tokens, hidden = cot.shape
    col_dev = sum(widths)
    real_blocks = hidden // col_dev
    return pl.pallas_call(
        functools.partial(prep_kernel, real_blocks, zl_count, widths),
        grid=(zl_count, narrow_count),
        in_specs=[
            pl.BlockSpec(
                (tokens, col_dev),
                lambda z, n: (0, jnp.minimum(n * zl_count + z, real_blocks - 1)),
            )
        ],
        out_specs=[
            pl.BlockSpec((1, tokens, width), lambda z, n: (z * narrow_count + n, 0, 0))
            for width in widths
        ],
        out_shape=[
            jax.ShapeDtypeStruct((zl_count * narrow_count, tokens, width), cot.dtype)
            for width in widths
        ],
        compiler_params=pltpu.CompilerParams(vmem_limit_bytes=24 * MIB),
        cost_estimate=pl.CostEstimate(
            flops=0, bytes_accessed=4 * cot.size, transcendentals=0
        ),
        name="cut_columns",
    )(cot)


def chunk_kernel(hi_count, zl_count, place_ref, *refs):
    xt = refs[:zl_count]
    cots = refs[zl_count : zl_count + 2 * hi_count]
    signs = refs[zl_count + 2 * hi_count : 2 * zl_count + 2 * hi_count]
    row_mix = refs[-2]
    out_ref = refs[-1]
    hi, core = place_ref[0], place_ref[2]
    mixed = []
    for d in range(zl_count):
        total = None
        for h in range(hi_count):
            for c in range(2):
                for z in range(zl_count):
                    source = ((hi ^ h) * zl_count + z) * 2 + (core ^ c)
                    term = jnp.dot(
                        xt[d][source],
                        cots[h * 2 + c][z],
                        preferred_element_type=jnp.float32,
                    )
                    total = term if total is None else total + term
        value = total * signs[d][...].astype(jnp.float32)
        high = value.astype(jnp.bfloat16)
        low = (value - high.astype(jnp.float32)).astype(jnp.bfloat16)
        mixed.append(
            jnp.dot(row_mix[...], high, preferred_element_type=jnp.float32)
            + jnp.dot(row_mix[...], low, preferred_element_type=jnp.float32)
        )
    mixed = butterfly(mixed)
    for b in range(out_ref.shape[0]):
        for d in range(zl_count):
            out_ref[b, d] = mixed[d][:, b * LANES : (b + 1) * LANES]


def chunk_call(place, xt, cots, signs, row_mix, tile, steps, hi_count):
    zl_count = len(xt)
    sources, rows, tokens = xt[0].shape
    chunk = tile * steps
    resident = pl.Buffered(1)
    return pl.pallas_call(
        functools.partial(chunk_kernel, hi_count, zl_count),
        grid_spec=pltpu.PrefetchScalarGridSpec(
            num_scalar_prefetch=1,
            grid=(steps,),
            in_specs=[
                pl.BlockSpec(
                    (sources, rows, tokens), lambda i, p: (0, 0, 0), pipeline_mode=resident
                )
                for _ in xt
            ]
            + [
                pl.BlockSpec((zl_count, tokens, tile), lambda i, p: (0, 0, i))
                for _ in cots
            ]
            + [
                pl.BlockSpec((rows, tile), lambda i, p: (0, i))
                for _ in signs
            ]
            + [
                pl.BlockSpec((rows, rows), lambda i, p: (0, 0), pipeline_mode=resident)
            ],
            out_specs=pl.BlockSpec(
                (tile // LANES, zl_count, rows, LANES), lambda i, p: (i, 0, 0, 0)
            ),
        ),
        out_shape=jax.ShapeDtypeStruct(
            (chunk // LANES, zl_count, rows, LANES), jnp.float32
        ),
        compiler_params=pltpu.CompilerParams(vmem_limit_bytes=40 * MIB),
        cost_estimate=pl.CostEstimate(
            flops=zl_count * rows * chunk * tokens,
            bytes_accessed=4 * zl_count * rows * chunk,
            transcendentals=0,
        ),
        name="gradient_rows",
    )(place, *xt, *cots, *signs, row_mix)


def pick_kernel(parts, index_ref, *refs):
    blocks = refs[:parts]
    lane_signs, out_ref, mixed_ref, rows_ref = refs[parts:]
    rows = blocks[0].shape[1]
    slabs = [(block, b) for block in blocks for b in range(block.shape[0])]

    def mix(i, carry):
        spot = pl.ds(pl.multiple_of(i * 8, 8), 8)
        values = [block[b, spot, :] for block, b in slabs]
        for b, value in enumerate(butterfly(values)):
            mixed_ref[pl.ds(pl.multiple_of(b * rows + i * 8, 8), 8), :] = value
        return carry

    lax.fori_loop(0, rows // 8, mix, 0)

    def group(g, carry):
        for j in range(LANES):
            row = index_ref[g * LANES + j]
            rows_ref[pl.ds(j, 1), :] = mixed_ref[pl.ds(row, 1), :]
        spot = pl.ds(pl.multiple_of(g * LANES, LANES), LANES)
        product = rows_ref[...] * lane_signs[spot, :].astype(jnp.float32)
        out_ref[pl.ds(g, 1), :] = jnp.sum(product.T, axis=0, keepdims=True)
        return carry

    lax.fori_loop(0, out_ref.shape[0], group, 0)


def pick_call(index, blocks, lane_signs):
    picks = index.shape[0]
    total = sum(block.shape[0] * block.shape[1] for block in blocks)
    return pl.pallas_call(
        functools.partial(pick_kernel, len(blocks)),
        grid_spec=pltpu.PrefetchScalarGridSpec(
            num_scalar_prefetch=1,
            grid=(1,),
            in_specs=[
                pl.BlockSpec(
                    block.shape, lambda i, p: (0, 0, 0), pipeline_mode=pl.Buffered(1)
                )
                for block in blocks
            ]
            + [
                pl.BlockSpec(
                    (picks, LANES), lambda i, p: (0, 0), pipeline_mode=pl.Buffered(1)
                )
            ],
            out_specs=pl.BlockSpec((picks // LANES, LANES), lambda i, p: (0, 0)),
            scratch_shapes=[
                pltpu.VMEM((total, LANES), jnp.float32),
                pltpu.VMEM((LANES, LANES), jnp.float32),
            ],
        ),
        out_shape=jax.ShapeDtypeStruct((picks // LANES, LANES), jnp.float32),
        compiler_params=pltpu.CompilerParams(vmem_limit_bytes=40 * MIB),
        cost_estimate=pl.CostEstimate(
            flops=8 * total * LANES, bytes_accessed=4 * total * LANES, transcendentals=0
        ),
        name="pick_samples",
    )(index, *blocks, lane_signs)


def parity_sign(bits):
    for shift in (16, 8, 4, 2, 1):
        bits = bits ^ (bits >> shift)
    return 1 - 2 * (bits & 1)


def swap(value, axis, offset):
    count = lax.axis_size(axis)
    return lax.ppermute(value, axis, [(i, i ^ offset) for i in range(count)])


def after(value, *others):
    return lax.optimization_barrier((value, *others))[0]


def body(inputs, out_cotangent, sign_bits, row_pick, col_pick):
    hi_count = lax.axis_size("hi")
    zl_count = lax.axis_size("zl")
    narrow_count = lax.axis_size("narrow")
    hi, zl, core, narrow = [lax.axis_index(a) for a in ALL_AXES]
    wide_count = hi_count * zl_count * 2
    token_shard, rows = inputs.shape[1:]
    col_shard = sign_bits.shape[2]
    col_dev = col_shard // zl_count
    tile, chunks = plan_chunks(col_dev)
    tokens = token_shard * narrow_count // wide_count
    cut = prepare(
        out_cotangent[0, 0], zl_count, narrow_count, [tile * steps for steps in chunks]
    )

    features = after(inputs[0], cut[0])
    own_xt = features.reshape(token_shard // tokens, tokens, rows).swapaxes(1, 2)
    xt_parts = [swap(own_xt, "zl", d) if d else own_xt for d in range(zl_count)]

    row_mix = jnp.asarray(hadamard(rows), jnp.bfloat16)
    place = jnp.stack([hi, zl, core]).astype(jnp.int32)
    edges = [tile * sum(chunks[:i]) for i in range(len(chunks) + 1)]
    count = len(chunks)
    own, far, signs, swapped = {}, {}, {}, {}
    blocks, xt = [], None
    cut = list(cut)
    bits = sign_bits[0]
    samples = (row_pick[0], col_pick[0])

    def sign_block(d, index):
        start = (zl ^ d) * col_dev + edges[index]
        part = lax.dynamic_slice_in_dim(bits, start, tile * chunks[index], axis=1)
        return (2 * part - 1).astype(jnp.bfloat16)

    for stage in range(count + 2):
        if stage < count:
            signs[stage] = [sign_block(d, stage) for d in range(zl_count)]
            part = after(cut[stage], *signs[stage]) if stage else cut[stage]
            own[stage] = lax.all_to_all(part, ("zl", "narrow"), 0, 0, tiled=True)
        if 1 <= stage <= count:
            c = stage - 1
            far[c] = [swap(own[c], "hi", h) for h in range(1, hi_count)]
            swapped[c] = [swap(own[c], "core", 1)]
            signs[c] = [swap(x, "zl", d) if d else x for d, x in enumerate(signs[c])]
        if stage >= 2:
            c = stage - 2
            swapped[c] += [swap(x, "core", 1) for x in far[c]]
        ready = {count - 1: range(count - 2), count: [count - 2], count + 1: [count - 1]}
        for c in ready.get(stage, []):
            pairs = zip([own[c]] + far[c], swapped[c])
            cots = [
                x.reshape(zl_count, tokens, tile * chunks[c]) for pair in pairs for x in pair
            ]
            done = chunk_call(
                place, xt, cots, signs[c], row_mix, tile, chunks[c], hi_count
            )
            blocks.append(done.reshape(-1, zl_count * rows, LANES))
            place = after(place, done)
        if stage == 2:
            row, col = samples
            block = (col // LANES) % (col_dev // LANES)
            row_in = (row // (2 * rows)) % zl_count * rows + row % rows
            position = block * (zl_count * rows) + row_in
            row_base = ((hi * zl_count + zl) * 2 + core) * rows
            col_base = narrow * col_shard + zl * col_dev
            lane = lax.broadcasted_iota(jnp.int32, (1, LANES), 1)
            fold = parity_sign((row & row_base)[:, None]) * parity_sign((col_base + lane) & col[:, None])
            samples = (position, fold.astype(jnp.bfloat16))
        state = (cut, own, far, signs, swapped, blocks, bits, place, xt_parts, samples)
        state = lax.optimization_barrier(state)
        cut, own, far, signs, swapped, blocks, bits, place, xt_parts, samples = state
        if stage == 0:
            xt = [lax.all_gather(x, "narrow", axis=0, tiled=True) for x in [own_xt] + xt_parts[1:]]
    position, lane_signs = samples
    picked = pick_call(position, blocks, lane_signs)

    devices = wide_count * narrow_count
    terms = lax.all_to_all(
        picked.reshape(devices, position.shape[0] // devices), ALL_AXES, 0, 0, tiled=True
    )
    total = jnp.sum(terms, axis=0) / jnp.sqrt(jnp.float32(position.shape[0]))
    return total.reshape(1, 1, -1)


def solution(mesh):
    wide, narrow = mesh.shape["wide"], mesh.shape["narrow"]
    sizes = (2, wide // 4, 2, narrow)
    split = Mesh(mesh.devices.reshape(sizes), ALL_AXES)
    wide_axes = ("hi", "zl", "core")
    return jax.shard_map(
        body,
        mesh=split,
        in_specs=(
            P(None, "narrow", wide_axes),
            P(None, None, ALL_AXES, None),
            P(None, wide_axes, "narrow"),
            P(),
            P(),
        ),
        out_specs=P(None, None, ALL_AXES),
        check_vma=False,
    )
```

```python
import functools

import jax
import jax.numpy as jnp
import numpy as np
from jax import lax
from jax.experimental import pallas as pl
from jax.experimental.pallas import tpu as pltpu
from jax.sharding import Mesh, PartitionSpec as P

LANES = 128
UNITS = 8
MIB = 1024 * 1024
ALL_AXES = ("hi", "zl", "core", "narrow")


def hadamard(length):
    h = np.ones((1, 1), np.float32)
    while h.shape[0] < length:
        h = np.block([[h, h], [h, -h]])
    return h


def butterfly(parts):
    step = 1
    while step < len(parts):
        parts = [
            parts[i] + parts[i ^ step] if not i & step else parts[i ^ step] - parts[i]
            for i in range(len(parts))
        ]
        step *= 2
    return parts


def plan_chunks(col_dev):
    tile = max(LANES, min(256, col_dev // UNITS))
    units = col_dev // tile
    first, third = max(1, units // 8), max(1, units // 4)
    return tile, [first, units - 2 * first - third, third, first]


def prep_kernel(real_blocks, zl_count, widths, in_ref, *out_refs):
    block = pl.program_id(1) * zl_count + pl.program_id(0)
    keep = block < real_blocks
    start = 0
    for width, out_ref in zip(widths, out_refs):
        value = in_ref[:, start : start + width]
        out_ref[0] = jnp.where(keep, value, jnp.zeros_like(value))
        start += width


def prepare(cot, zl_count, narrow_count, widths):
    tokens, hidden = cot.shape
    col_dev = sum(widths)
    real_blocks = hidden // col_dev
    return pl.pallas_call(
        functools.partial(prep_kernel, real_blocks, zl_count, widths),
        grid=(zl_count, narrow_count),
        in_specs=[
            pl.BlockSpec(
                (tokens, col_dev),
                lambda z, n: (0, jnp.minimum(n * zl_count + z, real_blocks - 1)),
            )
        ],
        out_specs=[
            pl.BlockSpec((1, tokens, width), lambda z, n: (z * narrow_count + n, 0, 0))
            for width in widths
        ],
        out_shape=[
            jax.ShapeDtypeStruct((zl_count * narrow_count, tokens, width), cot.dtype)
            for width in widths
        ],
        compiler_params=pltpu.CompilerParams(vmem_limit_bytes=24 * MIB),
        cost_estimate=pl.CostEstimate(
            flops=0, bytes_accessed=4 * cot.size, transcendentals=0
        ),
        name="cut_columns",
    )(cot)


def chunk_kernel(hi_count, zl_count, place_ref, *refs):
    xt = refs[:zl_count]
    cots = refs[zl_count : zl_count + 2 * hi_count]
    signs = refs[zl_count + 2 * hi_count : 2 * zl_count + 2 * hi_count]
    row_mix = refs[-2]
    out_ref = refs[-1]
    hi, core = place_ref[0], place_ref[2]
    mixed = []
    for d in range(zl_count):
        total = None
        for h in range(hi_count):
            for c in range(2):
                for z in range(zl_count):
                    source = ((hi ^ h) * zl_count + z) * 2 + (core ^ c)
                    term = jnp.dot(
                        xt[d][source],
                        cots[h * 2 + c][z],
                        preferred_element_type=jnp.float32,
                    )
                    total = term if total is None else total + term
        value = total * signs[d][...].astype(jnp.float32)
        high = value.astype(jnp.bfloat16)
        low = (value - high.astype(jnp.float32)).astype(jnp.bfloat16)
        mixed.append(
            jnp.dot(row_mix[...], high, preferred_element_type=jnp.float32)
            + jnp.dot(row_mix[...], low, preferred_element_type=jnp.float32)
        )
    mixed = butterfly(mixed)
    for b in range(out_ref.shape[0]):
        for d in range(zl_count):
            out_ref[b, d] = mixed[d][:, b * LANES : (b + 1) * LANES]


def chunk_call(place, xt, cots, signs, row_mix, tile, steps, hi_count):
    zl_count = len(xt)
    sources, rows, tokens = xt[0].shape
    chunk = tile * steps
    resident = pl.Buffered(1)
    return pl.pallas_call(
        functools.partial(chunk_kernel, hi_count, zl_count),
        grid_spec=pltpu.PrefetchScalarGridSpec(
            num_scalar_prefetch=1,
            grid=(steps,),
            in_specs=[
                pl.BlockSpec(
                    (sources, rows, tokens), lambda i, p: (0, 0, 0), pipeline_mode=resident
                )
                for _ in xt
            ]
            + [
                pl.BlockSpec((zl_count, tokens, tile), lambda i, p: (0, 0, i))
                for _ in cots
            ]
            + [
                pl.BlockSpec((rows, tile), lambda i, p: (0, i))
                for _ in signs
            ]
            + [
                pl.BlockSpec((rows, rows), lambda i, p: (0, 0), pipeline_mode=resident)
            ],
            out_specs=pl.BlockSpec(
                (tile // LANES, zl_count, rows, LANES), lambda i, p: (i, 0, 0, 0)
            ),
        ),
        out_shape=jax.ShapeDtypeStruct(
            (chunk // LANES, zl_count, rows, LANES), jnp.float32
        ),
        compiler_params=pltpu.CompilerParams(vmem_limit_bytes=40 * MIB),
        cost_estimate=pl.CostEstimate(
            flops=zl_count * rows * chunk * tokens,
            bytes_accessed=4 * zl_count * rows * chunk,
            transcendentals=0,
        ),
        name="gradient_rows",
    )(place, *xt, *cots, *signs, row_mix)


def pick_kernel(parts, index_ref, *refs):
    blocks = refs[:parts]
    lane_signs, out_ref, mixed_ref, rows_ref = refs[parts:]
    rows = blocks[0].shape[1]
    slabs = [(block, b) for block in blocks for b in range(block.shape[0])]

    def mix(i, carry):
        spot = pl.ds(pl.multiple_of(i * 8, 8), 8)
        values = [block[b, spot, :] for block, b in slabs]
        for b, value in enumerate(butterfly(values)):
            mixed_ref[pl.ds(pl.multiple_of(b * rows + i * 8, 8), 8), :] = value
        return carry

    lax.fori_loop(0, rows // 8, mix, 0)

    def group(g, carry):
        for j in range(LANES):
            row = index_ref[g * LANES + j]
            rows_ref[pl.ds(j, 1), :] = mixed_ref[pl.ds(row, 1), :]
        spot = pl.ds(pl.multiple_of(g * LANES, LANES), LANES)
        product = rows_ref[...] * lane_signs[spot, :].astype(jnp.float32)
        out_ref[pl.ds(g, 1), :] = jnp.sum(product.T, axis=0, keepdims=True)
        return carry

    lax.fori_loop(0, out_ref.shape[0], group, 0)


def pick_call(index, blocks, lane_signs):
    picks = index.shape[0]
    total = sum(block.shape[0] * block.shape[1] for block in blocks)
    return pl.pallas_call(
        functools.partial(pick_kernel, len(blocks)),
        grid_spec=pltpu.PrefetchScalarGridSpec(
            num_scalar_prefetch=1,
            grid=(1,),
            in_specs=[
                pl.BlockSpec(
                    block.shape, lambda i, p: (0, 0, 0), pipeline_mode=pl.Buffered(1)
                )
                for block in blocks
            ]
            + [
                pl.BlockSpec(
                    (picks, LANES), lambda i, p: (0, 0), pipeline_mode=pl.Buffered(1)
                )
            ],
            out_specs=pl.BlockSpec((picks // LANES, LANES), lambda i, p: (0, 0)),
            scratch_shapes=[
                pltpu.VMEM((total, LANES), jnp.float32),
                pltpu.VMEM((LANES, LANES), jnp.float32),
            ],
        ),
        out_shape=jax.ShapeDtypeStruct((picks // LANES, LANES), jnp.float32),
        compiler_params=pltpu.CompilerParams(vmem_limit_bytes=40 * MIB),
        cost_estimate=pl.CostEstimate(
            flops=8 * total * LANES, bytes_accessed=4 * total * LANES, transcendentals=0
        ),
        name="pick_samples",
    )(index, *blocks, lane_signs)


def parity_sign(bits):
    for shift in (16, 8, 4, 2, 1):
        bits = bits ^ (bits >> shift)
    return 1 - 2 * (bits & 1)


def swap(value, axis, offset):
    count = lax.axis_size(axis)
    return lax.ppermute(value, axis, [(i, i ^ offset) for i in range(count)])


def after(value, *others):
    return lax.optimization_barrier((value, *others))[0]


def body(inputs, out_cotangent, sign_bits, row_pick, col_pick):
    hi_count = lax.axis_size("hi")
    zl_count = lax.axis_size("zl")
    narrow_count = lax.axis_size("narrow")
    hi, zl, core, narrow = [lax.axis_index(a) for a in ALL_AXES]
    wide_count = hi_count * zl_count * 2
    token_shard, rows = inputs.shape[1:]
    col_shard = sign_bits.shape[2]
    col_dev = col_shard // zl_count
    tile, chunks = plan_chunks(col_dev)
    tokens = token_shard * narrow_count // wide_count
    cut = prepare(
        out_cotangent[0, 0], zl_count, narrow_count, [tile * steps for steps in chunks]
    )

    features = after(inputs[0], cut[0])
    own_xt = features.reshape(token_shard // tokens, tokens, rows).swapaxes(1, 2)
    xt_parts = [swap(own_xt, "zl", d) if d else own_xt for d in range(zl_count)]

    row_mix = jnp.asarray(hadamard(rows), jnp.bfloat16)
    place = jnp.stack([hi, zl, core]).astype(jnp.int32)
    edges = [tile * sum(chunks[:i]) for i in range(len(chunks) + 1)]
    count = len(chunks)
    own, far, signs, swapped = {}, {}, {}, {}
    blocks, xt = [], None
    cut = list(cut)
    bits = sign_bits[0]
    samples = (row_pick[0], col_pick[0])

    def sign_block(d, index):
        start = (zl ^ d) * col_dev + edges[index]
        part = lax.dynamic_slice_in_dim(bits, start, tile * chunks[index], axis=1)
        return (2 * part - 1).astype(jnp.bfloat16)

    for stage in range(count + 2):
        if stage < count:
            signs[stage] = [sign_block(d, stage) for d in range(zl_count)]
            part = after(cut[stage], *signs[stage]) if stage else cut[stage]
            own[stage] = lax.all_to_all(part, ("zl", "narrow"), 0, 0, tiled=True)
        if 1 <= stage <= count:
            c = stage - 1
            far[c] = [swap(own[c], "hi", h) for h in range(1, hi_count)]
            swapped[c] = [swap(own[c], "core", 1)]
            signs[c] = [swap(x, "zl", d) if d else x for d, x in enumerate(signs[c])]
        if stage >= 2:
            c = stage - 2
            swapped[c] += [swap(x, "core", 1) for x in far[c]]
            pairs = zip([own[c]] + far[c], swapped[c])
            cots = [
                x.reshape(zl_count, tokens, tile * chunks[c]) for pair in pairs for x in pair
            ]
            done = chunk_call(
                place, xt, cots, signs[c], row_mix, tile, chunks[c], hi_count
            )
            blocks.append(done.reshape(-1, zl_count * rows, LANES))
            place = after(place, done)
        if stage == 2:
            row, col = samples
            block = (col // LANES) % (col_dev // LANES)
            row_in = (row // (2 * rows)) % zl_count * rows + row % rows
            position = block * (zl_count * rows) + row_in
            row_base = ((hi * zl_count + zl) * 2 + core) * rows
            col_base = narrow * col_shard + zl * col_dev
            lane = lax.broadcasted_iota(jnp.int32, (1, LANES), 1)
            fold = parity_sign((row & row_base)[:, None]) * parity_sign((col_base + lane) & col[:, None])
            samples = (position, fold.astype(jnp.bfloat16))
        state = (cut, own, far, signs, swapped, blocks, bits, place, xt_parts, samples)
        state = lax.optimization_barrier(state)
        cut, own, far, signs, swapped, blocks, bits, place, xt_parts, samples = state
        if stage == 0:
            xt = [lax.all_gather(x, "narrow", axis=0, tiled=True) for x in [own_xt] + xt_parts[1:]]
    position, lane_signs = samples
    picked = pick_call(position, blocks, lane_signs)

    devices = wide_count * narrow_count
    terms = lax.all_to_all(
        picked.reshape(devices, position.shape[0] // devices), ALL_AXES, 0, 0, tiled=True
    )
    total = jnp.sum(terms, axis=0) / jnp.sqrt(jnp.float32(position.shape[0]))
    return total.reshape(1, 1, -1)


def solution(mesh):
    wide, narrow = mesh.shape["wide"], mesh.shape["narrow"]
    sizes = (2, wide // 4, 2, narrow)
    split = Mesh(mesh.devices.reshape(sizes), ALL_AXES)
    wide_axes = ("hi", "zl", "core")
    return jax.shard_map(
        body,
        mesh=split,
        in_specs=(
            P(None, "narrow", wide_axes),
            P(None, None, ALL_AXES, None),
            P(None, wide_axes, "narrow"),
            P(),
            P(),
        ),
        out_specs=P(None, None, ALL_AXES),
        check_vma=False,
    )
```

```python
import functools

import jax
import jax.numpy as jnp
import numpy as np
from jax import lax
from jax.experimental import pallas as pl
from jax.experimental.pallas import tpu as pltpu
from jax.sharding import Mesh, PartitionSpec as P

LANES = 128
UNITS = 8
MIB = 1024 * 1024
ALL_AXES = ("hi", "zl", "core", "narrow")


def hadamard(length):
    h = np.ones((1, 1), np.float32)
    while h.shape[0] < length:
        h = np.block([[h, h], [h, -h]])
    return h


def butterfly(parts):
    step = 1
    while step < len(parts):
        parts = [
            parts[i] + parts[i ^ step] if not i & step else parts[i ^ step] - parts[i]
            for i in range(len(parts))
        ]
        step *= 2
    return parts


def plan_chunks(col_dev):
    tile = max(LANES, min(256, col_dev // UNITS))
    units = col_dev // tile
    middle = (units - 2) // 2
    return tile, [1, units - 2 - middle, middle, 1]


def prep_kernel(real_blocks, zl_count, widths, in_ref, *out_refs):
    block = pl.program_id(1) * zl_count + pl.program_id(0)
    keep = block < real_blocks
    start = 0
    for width, out_ref in zip(widths, out_refs):
        value = in_ref[:, start : start + width]
        out_ref[0] = jnp.where(keep, value, jnp.zeros_like(value))
        start += width


def prepare(cot, zl_count, narrow_count, widths):
    tokens, hidden = cot.shape
    col_dev = sum(widths)
    real_blocks = hidden // col_dev
    return pl.pallas_call(
        functools.partial(prep_kernel, real_blocks, zl_count, widths),
        grid=(zl_count, narrow_count),
        in_specs=[
            pl.BlockSpec(
                (tokens, col_dev),
                lambda z, n: (0, jnp.minimum(n * zl_count + z, real_blocks - 1)),
            )
        ],
        out_specs=[
            pl.BlockSpec((1, tokens, width), lambda z, n: (z * narrow_count + n, 0, 0))
            for width in widths
        ],
        out_shape=[
            jax.ShapeDtypeStruct((zl_count * narrow_count, tokens, width), cot.dtype)
            for width in widths
        ],
        compiler_params=pltpu.CompilerParams(vmem_limit_bytes=60 * MIB),
        cost_estimate=pl.CostEstimate(
            flops=0, bytes_accessed=4 * cot.size, transcendentals=0
        ),
        name="cut_columns",
    )(cot)


def chunk_kernel(hi_count, zl_count, place_ref, *refs):
    xt = refs[:zl_count]
    cots = refs[zl_count : zl_count + 2 * hi_count]
    signs = refs[zl_count + 2 * hi_count : 2 * zl_count + 2 * hi_count]
    row_mix = refs[-2]
    out_ref = refs[-1]
    hi, core = place_ref[0], place_ref[2]
    mixed = []
    for d in range(zl_count):
        total = None
        for h in range(hi_count):
            for c in range(2):
                for z in range(zl_count):
                    source = ((hi ^ h) * zl_count + z) * 2 + (core ^ c)
                    term = jnp.dot(
                        xt[d][source],
                        cots[h * 2 + c][z],
                        preferred_element_type=jnp.float32,
                    )
                    total = term if total is None else total + term
        value = total * signs[d][...].astype(jnp.float32)
        high = value.astype(jnp.bfloat16)
        low = (value - high.astype(jnp.float32)).astype(jnp.bfloat16)
        mixed.append(
            jnp.dot(row_mix[...], high, preferred_element_type=jnp.float32)
            + jnp.dot(row_mix[...], low, preferred_element_type=jnp.float32)
        )
    mixed = butterfly(mixed)
    for b in range(out_ref.shape[0]):
        for d in range(zl_count):
            out_ref[b, d] = mixed[d][:, b * LANES : (b + 1) * LANES]


def chunk_call(place, xt, cots, signs, row_mix, tile, steps, hi_count):
    zl_count = len(xt)
    sources, rows, tokens = xt[0].shape
    chunk = tile * steps
    resident = pl.Buffered(1)
    return pl.pallas_call(
        functools.partial(chunk_kernel, hi_count, zl_count),
        grid_spec=pltpu.PrefetchScalarGridSpec(
            num_scalar_prefetch=1,
            grid=(steps,),
            in_specs=[
                pl.BlockSpec(
                    (sources, rows, tokens), lambda i, p: (0, 0, 0), pipeline_mode=resident
                )
                for _ in xt
            ]
            + [
                pl.BlockSpec((zl_count, tokens, tile), lambda i, p: (0, 0, i))
                for _ in cots
            ]
            + [
                pl.BlockSpec((rows, tile), lambda i, p: (0, i))
                for _ in signs
            ]
            + [
                pl.BlockSpec((rows, rows), lambda i, p: (0, 0), pipeline_mode=resident)
            ],
            out_specs=pl.BlockSpec(
                (tile // LANES, zl_count, rows, LANES), lambda i, p: (i, 0, 0, 0)
            ),
        ),
        out_shape=jax.ShapeDtypeStruct(
            (chunk // LANES, zl_count, rows, LANES), jnp.float32
        ),
        compiler_params=pltpu.CompilerParams(vmem_limit_bytes=40 * MIB),
        cost_estimate=pl.CostEstimate(
            flops=zl_count * rows * chunk * tokens,
            bytes_accessed=4 * zl_count * rows * chunk,
            transcendentals=0,
        ),
        name="gradient_rows",
    )(place, *xt, *cots, *signs, row_mix)


def pick_kernel(parts, index_ref, *refs):
    blocks = refs[:parts]
    lane_signs, out_ref, mixed_ref, rows_ref = refs[parts:]
    rows = blocks[0].shape[1]
    slabs = [(block, b) for block in blocks for b in range(block.shape[0])]

    def mix(i, carry):
        spot = pl.ds(pl.multiple_of(i * 8, 8), 8)
        values = [block[b, spot, :] for block, b in slabs]
        for b, value in enumerate(butterfly(values)):
            mixed_ref[pl.ds(pl.multiple_of(b * rows + i * 8, 8), 8), :] = value
        return carry

    lax.fori_loop(0, rows // 8, mix, 0)

    def gather(g, carry):
        for j in range(LANES):
            row = index_ref[g * LANES + j]
            rows_ref[g, j : j + 1, :] = mixed_ref[pl.ds(row, 1), :]
        return carry

    groups = out_ref.shape[0]
    lax.fori_loop(0, groups, gather, 0)
    side = 4 if groups % 4 == 0 else 1

    def reduce(i, carry):
        for q in range(side):
            g = i * side + q
            spot = pl.ds(pl.multiple_of(g * LANES, LANES), LANES)
            product = rows_ref[g] * lane_signs[spot, :].astype(jnp.float32)
            out_ref[pl.ds(g, 1), :] = jnp.sum(product.T, axis=0, keepdims=True)
        return carry

    lax.fori_loop(0, groups // side, reduce, 0)


def pick_call(index, blocks, lane_signs):
    picks = index.shape[0]
    total = sum(block.shape[0] * block.shape[1] for block in blocks)
    return pl.pallas_call(
        functools.partial(pick_kernel, len(blocks)),
        grid_spec=pltpu.PrefetchScalarGridSpec(
            num_scalar_prefetch=1,
            grid=(1,),
            in_specs=[
                pl.BlockSpec(
                    block.shape, lambda i, p: (0, 0, 0), pipeline_mode=pl.Buffered(1)
                )
                for block in blocks
            ]
            + [
                pl.BlockSpec(
                    (picks, LANES), lambda i, p: (0, 0), pipeline_mode=pl.Buffered(1)
                )
            ],
            out_specs=pl.BlockSpec((picks // LANES, LANES), lambda i, p: (0, 0)),
            scratch_shapes=[
                pltpu.VMEM((total, LANES), jnp.float32),
                pltpu.VMEM((picks // LANES, LANES, LANES), jnp.float32),
            ],
        ),
        out_shape=jax.ShapeDtypeStruct((picks // LANES, LANES), jnp.float32),
        compiler_params=pltpu.CompilerParams(vmem_limit_bytes=40 * MIB),
        cost_estimate=pl.CostEstimate(
            flops=8 * total * LANES, bytes_accessed=4 * total * LANES, transcendentals=0
        ),
        name="pick_samples",
    )(index, *blocks, lane_signs)


def parity_sign(bits):
    for shift in (16, 8, 4, 2, 1):
        bits = bits ^ (bits >> shift)
    return 1 - 2 * (bits & 1)


def swap(value, axis, offset):
    count = lax.axis_size(axis)
    return lax.ppermute(value, axis, [(i, i ^ offset) for i in range(count)])


def after(value, *others):
    return lax.optimization_barrier((value, *others))[0]


def body(inputs, out_cotangent, sign_bits, row_pick, col_pick):
    hi_count = lax.axis_size("hi")
    zl_count = lax.axis_size("zl")
    narrow_count = lax.axis_size("narrow")
    hi, zl, core, narrow = [lax.axis_index(a) for a in ALL_AXES]
    wide_count = hi_count * zl_count * 2
    token_shard, rows = inputs.shape[1:]
    col_shard = sign_bits.shape[2]
    col_dev = col_shard // zl_count
    tile, chunks = plan_chunks(col_dev)
    tokens = token_shard * narrow_count // wide_count
    cut = prepare(
        out_cotangent[0, 0], zl_count, narrow_count, [tile * steps for steps in chunks]
    )

    own_xt = inputs[0].reshape(token_shard // tokens, tokens, rows).swapaxes(1, 2)
    xt_parts = [swap(own_xt, "zl", d) if d else own_xt for d in range(zl_count)]

    row_mix = jnp.asarray(hadamard(rows), jnp.bfloat16)
    place = jnp.stack([hi, zl, core]).astype(jnp.int32)
    edges = [tile * sum(chunks[:i]) for i in range(len(chunks) + 1)]
    count = len(chunks)
    own, far, signs, swapped = {}, {}, {}, {}
    blocks, xt = [], None
    cut = list(cut)
    bits = sign_bits[0]
    samples = (row_pick[0], col_pick[0])

    def sign_block(d, index):
        start = (zl ^ d) * col_dev + edges[index]
        part = lax.dynamic_slice_in_dim(bits, start, tile * chunks[index], axis=1)
        return (2 * part - 1).astype(jnp.bfloat16)

    for stage in range(count + 2):
        if stage < count:
            signs[stage] = [sign_block(d, stage) for d in range(zl_count)]
            part = after(cut[stage], *signs[stage]) if stage > 1 else cut[stage]
            own[stage] = lax.all_to_all(part, ("zl", "narrow"), 0, 0, tiled=True)
        if 1 <= stage <= count:
            c = stage - 1
            far[c] = [swap(own[c], "hi", h) for h in range(1, hi_count)]
            swapped[c] = [swap(own[c], "core", 1)]
            signs[c] = [swap(x, "zl", d) if d else x for d, x in enumerate(signs[c])]
        if stage >= 2:
            c = stage - 2
            swapped[c] += [swap(x, "core", 1) for x in far[c]]
        ready = {count - 1: range(count - 2), count: [count - 2], count + 1: [count - 1]}
        for c in ready.get(stage, []):
            pairs = zip([own[c]] + far[c], swapped[c])
            cots = [
                x.reshape(zl_count, tokens, tile * chunks[c]) for pair in pairs for x in pair
            ]
            done = chunk_call(
                place, xt, cots, signs[c], row_mix, tile, chunks[c], hi_count
            )
            blocks.append(done.reshape(-1, zl_count * rows, LANES))
            place = after(place, done)
        if stage == 2:
            row, col = samples
            block = (col // LANES) % (col_dev // LANES)
            row_in = (row // (2 * rows)) % zl_count * rows + row % rows
            position = block * (zl_count * rows) + row_in
            row_base = ((hi * zl_count + zl) * 2 + core) * rows
            col_base = narrow * col_shard + zl * col_dev
            lane = lax.broadcasted_iota(jnp.int32, (1, LANES), 1)
            fold = parity_sign((row & row_base)[:, None]) * parity_sign((col_base + lane) & col[:, None])
            samples = (position, fold.astype(jnp.bfloat16))
        state = (cut, own, far, signs, swapped, blocks, bits, place, xt_parts, samples)
        state = lax.optimization_barrier(state)
        cut, own, far, signs, swapped, blocks, bits, place, xt_parts, samples = state
        if stage == 0:
            xt = [lax.all_gather(x, "narrow", axis=0, tiled=True) for x in [own_xt] + xt_parts[1:]]
    position, lane_signs = samples
    picked = pick_call(position, blocks, lane_signs)

    devices = wide_count * narrow_count
    terms = lax.all_to_all(
        picked.reshape(devices, position.shape[0] // devices), ALL_AXES, 0, 0, tiled=True
    )
    total = jnp.sum(terms, axis=0) / jnp.sqrt(jnp.float32(position.shape[0]))
    return total.reshape(1, 1, -1)


def solution(mesh):
    wide, narrow = mesh.shape["wide"], mesh.shape["narrow"]
    sizes = (2, wide // 4, 2, narrow)
    split = Mesh(mesh.devices.reshape(sizes), ALL_AXES)
    wide_axes = ("hi", "zl", "core")
    return jax.shard_map(
        body,
        mesh=split,
        in_specs=(
            P(None, "narrow", wide_axes),
            P(None, None, ALL_AXES, None),
            P(None, wide_axes, "narrow"),
            P(),
            P(),
        ),
        out_specs=P(None, None, ALL_AXES),
        check_vma=False,
    )
```

```python
import functools

import jax
import jax.numpy as jnp
import numpy as np
from jax import lax
from jax.experimental import pallas as pl
from jax.experimental.pallas import tpu as pltpu
from jax.sharding import Mesh, PartitionSpec as P

LANES = 128
UNITS = 8
MIB = 1024 * 1024
ALL_AXES = ("hi", "zl", "core", "narrow")


def hadamard(length):
    h = np.ones((1, 1), np.float32)
    while h.shape[0] < length:
        h = np.block([[h, h], [h, -h]])
    return h


def butterfly(parts):
    step = 1
    while step < len(parts):
        parts = [
            parts[i] + parts[i ^ step] if not i & step else parts[i ^ step] - parts[i]
            for i in range(len(parts))
        ]
        step *= 2
    return parts


def plan_chunks(col_dev):
    tile = max(LANES, min(256, col_dev // UNITS))
    units = col_dev // tile
    middle = (units - 2) // 2
    return tile, [1, units - 2 - middle, middle, 1]


def prep_kernel(real_blocks, zl_count, spans, in_ref, *out_refs):
    block = pl.program_id(1) * zl_count + pl.program_id(0)
    keep = block < real_blocks
    for (start, stop), out_ref in zip(spans, out_refs):
        value = in_ref[:, start:stop]
        out_ref[0] = jnp.where(keep, value, jnp.zeros_like(value))


def prepare(cot, zl_count, narrow_count, col_dev, read, spans):
    tokens, hidden = cot.shape
    real_blocks = hidden // col_dev
    stride = col_dev // read
    return pl.pallas_call(
        functools.partial(prep_kernel, real_blocks, zl_count, spans),
        grid=(zl_count, narrow_count),
        in_specs=[
            pl.BlockSpec(
                (tokens, read),
                lambda z, n: (0, jnp.minimum(n * zl_count + z, real_blocks - 1) * stride),
            )
        ],
        out_specs=[
            pl.BlockSpec(
                (1, tokens, stop - start), lambda z, n: (z * narrow_count + n, 0, 0)
            )
            for start, stop in spans
        ],
        out_shape=[
            jax.ShapeDtypeStruct(
                (zl_count * narrow_count, tokens, stop - start), cot.dtype
            )
            for start, stop in spans
        ],
        compiler_params=pltpu.CompilerParams(vmem_limit_bytes=60 * MIB),
        cost_estimate=pl.CostEstimate(
            flops=0, bytes_accessed=4 * cot.size // stride, transcendentals=0
        ),
        name="cut_columns",
    )(cot)


def chunk_kernel(hi_count, zl_count, place_ref, *refs):
    xt = refs[:zl_count]
    cots = refs[zl_count : zl_count + 2 * hi_count]
    signs = refs[zl_count + 2 * hi_count : 2 * zl_count + 2 * hi_count]
    row_mix = refs[-2]
    out_ref = refs[-1]
    hi, core = place_ref[0], place_ref[2]
    mixed = []
    for d in range(zl_count):
        total = None
        for h in range(hi_count):
            for c in range(2):
                for z in range(zl_count):
                    source = ((hi ^ h) * zl_count + z) * 2 + (core ^ c)
                    term = jnp.dot(
                        xt[d][source],
                        cots[h * 2 + c][z],
                        preferred_element_type=jnp.float32,
                    )
                    total = term if total is None else total + term
        value = total * signs[d][...].astype(jnp.float32)
        high = value.astype(jnp.bfloat16)
        low = (value - high.astype(jnp.float32)).astype(jnp.bfloat16)
        mixed.append(
            jnp.dot(row_mix[...], high, preferred_element_type=jnp.float32)
            + jnp.dot(row_mix[...], low, preferred_element_type=jnp.float32)
        )
    mixed = butterfly(mixed)
    for b in range(out_ref.shape[0]):
        for d in range(zl_count):
            out_ref[b, d] = mixed[d][:, b * LANES : (b + 1) * LANES]


def chunk_call(place, xt, cots, signs, row_mix, tile, steps, hi_count):
    zl_count = len(xt)
    sources, rows, tokens = xt[0].shape
    chunk = tile * steps
    resident = pl.Buffered(1)
    return pl.pallas_call(
        functools.partial(chunk_kernel, hi_count, zl_count),
        grid_spec=pltpu.PrefetchScalarGridSpec(
            num_scalar_prefetch=1,
            grid=(steps,),
            in_specs=[
                pl.BlockSpec(
                    (sources, rows, tokens), lambda i, p: (0, 0, 0), pipeline_mode=resident
                )
                for _ in xt
            ]
            + [
                pl.BlockSpec((zl_count, tokens, tile), lambda i, p: (0, 0, i))
                for _ in cots
            ]
            + [
                pl.BlockSpec((rows, tile), lambda i, p: (0, i))
                for _ in signs
            ]
            + [
                pl.BlockSpec((rows, rows), lambda i, p: (0, 0), pipeline_mode=resident)
            ],
            out_specs=pl.BlockSpec(
                (tile // LANES, zl_count, rows, LANES), lambda i, p: (i, 0, 0, 0)
            ),
        ),
        out_shape=jax.ShapeDtypeStruct(
            (chunk // LANES, zl_count, rows, LANES), jnp.float32
        ),
        compiler_params=pltpu.CompilerParams(vmem_limit_bytes=40 * MIB),
        cost_estimate=pl.CostEstimate(
            flops=zl_count * rows * chunk * tokens,
            bytes_accessed=4 * zl_count * rows * chunk,
            transcendentals=0,
        ),
        name="gradient_rows",
    )(place, *xt, *cots, *signs, row_mix)


def pick_kernel(parts, index_ref, *refs):
    blocks = refs[:parts]
    lane_signs, out_ref, mixed_ref, rows_ref = refs[parts:]
    rows = blocks[0].shape[1]
    slabs = [(block, b) for block in blocks for b in range(block.shape[0])]

    def mix(i, carry):
        spot = pl.ds(pl.multiple_of(i * 8, 8), 8)
        values = [block[b, spot, :] for block, b in slabs]
        for b, value in enumerate(butterfly(values)):
            mixed_ref[pl.ds(pl.multiple_of(b * rows + i * 8, 8), 8), :] = value
        return carry

    lax.fori_loop(0, rows // 8, mix, 0)

    def gather(g, carry):
        for j in range(LANES):
            row = index_ref[g * LANES + j]
            rows_ref[g, j : j + 1, :] = mixed_ref[pl.ds(row, 1), :]
        return carry

    groups = out_ref.shape[0]
    lax.fori_loop(0, groups, gather, 0)
    side = 4 if groups % 4 == 0 else 1

    def reduce(i, carry):
        for q in range(side):
            g = i * side + q
            spot = pl.ds(pl.multiple_of(g * LANES, LANES), LANES)
            product = rows_ref[g] * lane_signs[spot, :].astype(jnp.float32)
            out_ref[pl.ds(g, 1), :] = jnp.sum(product.T, axis=0, keepdims=True)
        return carry

    lax.fori_loop(0, groups // side, reduce, 0)


def pick_call(index, blocks, lane_signs):
    picks = index.shape[0]
    total = sum(block.shape[0] * block.shape[1] for block in blocks)
    return pl.pallas_call(
        functools.partial(pick_kernel, len(blocks)),
        grid_spec=pltpu.PrefetchScalarGridSpec(
            num_scalar_prefetch=1,
            grid=(1,),
            in_specs=[
                pl.BlockSpec(
                    block.shape, lambda i, p: (0, 0, 0), pipeline_mode=pl.Buffered(1)
                )
                for block in blocks
            ]
            + [
                pl.BlockSpec(
                    (picks, LANES), lambda i, p: (0, 0), pipeline_mode=pl.Buffered(1)
                )
            ],
            out_specs=pl.BlockSpec((picks // LANES, LANES), lambda i, p: (0, 0)),
            scratch_shapes=[
                pltpu.VMEM((total, LANES), jnp.float32),
                pltpu.VMEM((picks // LANES, LANES, LANES), jnp.float32),
            ],
        ),
        out_shape=jax.ShapeDtypeStruct((picks // LANES, LANES), jnp.float32),
        compiler_params=pltpu.CompilerParams(vmem_limit_bytes=40 * MIB),
        cost_estimate=pl.CostEstimate(
            flops=8 * total * LANES, bytes_accessed=4 * total * LANES, transcendentals=0
        ),
        name="pick_samples",
    )(index, *blocks, lane_signs)


def parity_sign(bits):
    for shift in (16, 8, 4, 2, 1):
        bits = bits ^ (bits >> shift)
    return 1 - 2 * (bits & 1)


def swap(value, axis, offset):
    count = lax.axis_size(axis)
    return lax.ppermute(value, axis, [(i, i ^ offset) for i in range(count)])


def after(value, *others):
    return lax.optimization_barrier((value, *others))[0]


def body(inputs, out_cotangent, sign_bits, row_pick, col_pick):
    hi_count = lax.axis_size("hi")
    zl_count = lax.axis_size("zl")
    narrow_count = lax.axis_size("narrow")
    hi, zl, core, narrow = [lax.axis_index(a) for a in ALL_AXES]
    wide_count = hi_count * zl_count * 2
    token_shard, rows = inputs.shape[1:]
    col_shard = sign_bits.shape[2]
    col_dev = col_shard // zl_count
    tile, chunks = plan_chunks(col_dev)
    tokens = token_shard * narrow_count // wide_count
    edges = [tile * sum(chunks[:i]) for i in range(len(chunks) + 1)]
    spans = list(zip(edges, edges[1:]))
    cot = out_cotangent[0, 0]
    cut = list(prepare(cot, zl_count, narrow_count, col_dev, edges[1], spans[:1]))
    cut += prepare(
        after(cot, cut[0]), zl_count, narrow_count, col_dev, col_dev, spans[1:]
    )

    own_xt = inputs[0].reshape(token_shard // tokens, tokens, rows).swapaxes(1, 2)
    xt_parts = [swap(own_xt, "zl", d) if d else own_xt for d in range(zl_count)]

    row_mix = jnp.asarray(hadamard(rows), jnp.bfloat16)
    place = jnp.stack([hi, zl, core]).astype(jnp.int32)
    count = len(chunks)
    own, far, signs, swapped = {}, {}, {}, {}
    blocks, xt = [], None
    bits = sign_bits[0]
    samples = (row_pick[0], col_pick[0])

    def sign_block(d, index):
        start = (zl ^ d) * col_dev + edges[index]
        part = lax.dynamic_slice_in_dim(bits, start, tile * chunks[index], axis=1)
        return (2 * part - 1).astype(jnp.bfloat16)

    for stage in range(count + 2):
        if stage < count:
            signs[stage] = [sign_block(d, stage) for d in range(zl_count)]
            own[stage] = lax.all_to_all(cut[stage], ("zl", "narrow"), 0, 0, tiled=True)
        if 1 <= stage <= count:
            c = stage - 1
            far[c] = [swap(own[c], "hi", h) for h in range(1, hi_count)]
            swapped[c] = [swap(own[c], "core", 1)]
            signs[c] = [swap(x, "zl", d) if d else x for d, x in enumerate(signs[c])]
        if stage >= 2:
            c = stage - 2
            swapped[c] += [swap(x, "core", 1) for x in far[c]]
        ready = {count - 1: range(count - 2), count: [count - 2], count + 1: [count - 1]}
        for c in ready.get(stage, []):
            pairs = zip([own[c]] + far[c], swapped[c])
            cots = [
                x.reshape(zl_count, tokens, tile * chunks[c]) for pair in pairs for x in pair
            ]
            done = chunk_call(
                place, xt, cots, signs[c], row_mix, tile, chunks[c], hi_count
            )
            blocks.append(done.reshape(-1, zl_count * rows, LANES))
            place = after(place, done)
        if stage == 3:
            row, col = samples
            block = (col // LANES) % (col_dev // LANES)
            row_in = (row // (2 * rows)) % zl_count * rows + row % rows
            position = block * (zl_count * rows) + row_in
            row_base = ((hi * zl_count + zl) * 2 + core) * rows
            col_base = narrow * col_shard + zl * col_dev
            lane = lax.broadcasted_iota(jnp.int32, (1, LANES), 1)
            fold = parity_sign((row & row_base)[:, None]) * parity_sign((col_base + lane) & col[:, None])
            samples = (position, fold.astype(jnp.bfloat16))
        state = (cut, own, far, signs, swapped, blocks, bits, place, xt_parts, samples)
        state = lax.optimization_barrier(state)
        cut, own, far, signs, swapped, blocks, bits, place, xt_parts, samples = state
        if stage == 0:
            xt = [lax.all_gather(x, "narrow", axis=0, tiled=True) for x in [own_xt] + xt_parts[1:]]
    position, lane_signs = samples
    picked = pick_call(position, blocks, lane_signs)

    devices = wide_count * narrow_count
    terms = lax.all_to_all(
        picked.reshape(devices, position.shape[0] // devices), ALL_AXES, 0, 0, tiled=True
    )
    total = jnp.sum(terms, axis=0) / jnp.sqrt(jnp.float32(position.shape[0]))
    return total.reshape(1, 1, -1)


def solution(mesh):
    wide, narrow = mesh.shape["wide"], mesh.shape["narrow"]
    sizes = (2, wide // 4, 2, narrow)
    split = Mesh(mesh.devices.reshape(sizes), ALL_AXES)
    wide_axes = ("hi", "zl", "core")
    return jax.shard_map(
        body,
        mesh=split,
        in_specs=(
            P(None, "narrow", wide_axes),
            P(None, None, ALL_AXES, None),
            P(None, wide_axes, "narrow"),
            P(),
            P(),
        ),
        out_specs=P(None, None, ALL_AXES),
        check_vma=False,
    )
```

```python
import functools

import jax
import jax.numpy as jnp
import numpy as np
from jax import lax
from jax.experimental import pallas as pl
from jax.experimental.pallas import tpu as pltpu
from jax.sharding import Mesh, PartitionSpec as P

LANES = 128
UNITS = 8
MIB = 1024 * 1024
ALL_AXES = ("hi", "zl", "core", "narrow")


def hadamard(length):
    h = np.ones((1, 1), np.float32)
    while h.shape[0] < length:
        h = np.block([[h, h], [h, -h]])
    return h


def butterfly(parts):
    step = 1
    while step < len(parts):
        parts = [
            parts[i] + parts[i ^ step] if not i & step else parts[i ^ step] - parts[i]
            for i in range(len(parts))
        ]
        step *= 2
    return parts


def plan_chunks(col_dev):
    tile = max(LANES, min(256, col_dev // UNITS))
    units = col_dev // tile
    first, third = max(1, units // 8), max(1, units // 4)
    return tile, [first, units - 2 * first - third, third, first]


def prep_kernel(real_blocks, zl_count, spans, in_ref, *out_refs):
    block = pl.program_id(1) * zl_count + pl.program_id(0)
    keep = block < real_blocks
    for (start, stop), out_ref in zip(spans, out_refs):
        value = in_ref[:, start:stop]
        out_ref[0] = jnp.where(keep, value, jnp.zeros_like(value))


def prepare(cot, zl_count, narrow_count, col_dev, read, spans):
    tokens, hidden = cot.shape
    real_blocks = hidden // col_dev
    stride = col_dev // read
    return pl.pallas_call(
        functools.partial(prep_kernel, real_blocks, zl_count, spans),
        grid=(zl_count, narrow_count),
        in_specs=[
            pl.BlockSpec(
                (tokens, read),
                lambda z, n: (0, jnp.minimum(n * zl_count + z, real_blocks - 1) * stride),
            )
        ],
        out_specs=[
            pl.BlockSpec(
                (1, tokens, stop - start), lambda z, n: (z * narrow_count + n, 0, 0)
            )
            for start, stop in spans
        ],
        out_shape=[
            jax.ShapeDtypeStruct(
                (zl_count * narrow_count, tokens, stop - start), cot.dtype
            )
            for start, stop in spans
        ],
        compiler_params=pltpu.CompilerParams(vmem_limit_bytes=60 * MIB),
        cost_estimate=pl.CostEstimate(
            flops=0, bytes_accessed=4 * cot.size // stride, transcendentals=0
        ),
        name="cut_columns",
    )(cot)


def chunk_kernel(hi_count, zl_count, place_ref, *refs):
    xt = refs[:zl_count]
    cots = refs[zl_count : zl_count + 2 * hi_count]
    signs = refs[zl_count + 2 * hi_count : 2 * zl_count + 2 * hi_count]
    row_mix = refs[-2]
    out_ref = refs[-1]
    hi, core = place_ref[0], place_ref[2]
    mixed = []
    for d in range(zl_count):
        total = None
        for h in range(hi_count):
            for c in range(2):
                for z in range(zl_count):
                    source = ((hi ^ h) * zl_count + z) * 2 + (core ^ c)
                    term = jnp.dot(
                        xt[d][source],
                        cots[h * 2 + c][z],
                        preferred_element_type=jnp.float32,
                    )
                    total = term if total is None else total + term
        value = total * signs[d][...].astype(jnp.float32)
        high = value.astype(jnp.bfloat16)
        low = (value - high.astype(jnp.float32)).astype(jnp.bfloat16)
        mixed.append(
            jnp.dot(row_mix[...], high, preferred_element_type=jnp.float32)
            + jnp.dot(row_mix[...], low, preferred_element_type=jnp.float32)
        )
    mixed = butterfly(mixed)
    for b in range(out_ref.shape[0]):
        for d in range(zl_count):
            out_ref[b, d] = mixed[d][:, b * LANES : (b + 1) * LANES]


def chunk_call(place, xt, cots, signs, row_mix, tile, steps, hi_count):
    zl_count = len(xt)
    sources, rows, tokens = xt[0].shape
    chunk = tile * steps
    resident = pl.Buffered(1)
    return pl.pallas_call(
        functools.partial(chunk_kernel, hi_count, zl_count),
        grid_spec=pltpu.PrefetchScalarGridSpec(
            num_scalar_prefetch=1,
            grid=(steps,),
            in_specs=[
                pl.BlockSpec(
                    (sources, rows, tokens), lambda i, p: (0, 0, 0), pipeline_mode=resident
                )
                for _ in xt
            ]
            + [
                pl.BlockSpec((zl_count, tokens, tile), lambda i, p: (0, 0, i))
                for _ in cots
            ]
            + [
                pl.BlockSpec((rows, tile), lambda i, p: (0, i))
                for _ in signs
            ]
            + [
                pl.BlockSpec((rows, rows), lambda i, p: (0, 0), pipeline_mode=resident)
            ],
            out_specs=pl.BlockSpec(
                (tile // LANES, zl_count, rows, LANES), lambda i, p: (i, 0, 0, 0)
            ),
        ),
        out_shape=jax.ShapeDtypeStruct(
            (chunk // LANES, zl_count, rows, LANES), jnp.float32
        ),
        compiler_params=pltpu.CompilerParams(vmem_limit_bytes=40 * MIB),
        cost_estimate=pl.CostEstimate(
            flops=zl_count * rows * chunk * tokens,
            bytes_accessed=4 * zl_count * rows * chunk,
            transcendentals=0,
        ),
        name="gradient_rows",
    )(place, *xt, *cots, *signs, row_mix)


def pick_kernel(parts, index_ref, *refs):
    blocks = refs[:parts]
    lane_signs, out_ref, mixed_ref, rows_ref = refs[parts:]
    rows = blocks[0].shape[1]
    slabs = [(block, b) for block in blocks for b in range(block.shape[0])]

    def mix(i, carry):
        spot = pl.ds(pl.multiple_of(i * 8, 8), 8)
        values = [block[b, spot, :] for block, b in slabs]
        for b, value in enumerate(butterfly(values)):
            mixed_ref[pl.ds(pl.multiple_of(b * rows + i * 8, 8), 8), :] = value
        return carry

    lax.fori_loop(0, rows // 8, mix, 0)

    def gather(g, carry):
        for j in range(LANES):
            row = index_ref[g * LANES + j]
            rows_ref[g, j : j + 1, :] = mixed_ref[pl.ds(row, 1), :]
        return carry

    groups = out_ref.shape[0]
    lax.fori_loop(0, groups, gather, 0)
    side = 4 if groups % 4 == 0 else 1

    def reduce(i, carry):
        for q in range(side):
            g = i * side + q
            spot = pl.ds(pl.multiple_of(g * LANES, LANES), LANES)
            product = rows_ref[g] * lane_signs[spot, :].astype(jnp.float32)
            out_ref[pl.ds(g, 1), :] = jnp.sum(product.T, axis=0, keepdims=True)
        return carry

    lax.fori_loop(0, groups // side, reduce, 0)


def pick_call(index, blocks, lane_signs):
    picks = index.shape[0]
    total = sum(block.shape[0] * block.shape[1] for block in blocks)
    return pl.pallas_call(
        functools.partial(pick_kernel, len(blocks)),
        grid_spec=pltpu.PrefetchScalarGridSpec(
            num_scalar_prefetch=1,
            grid=(1,),
            in_specs=[
                pl.BlockSpec(
                    block.shape, lambda i, p: (0, 0, 0), pipeline_mode=pl.Buffered(1)
                )
                for block in blocks
            ]
            + [
                pl.BlockSpec(
                    (picks, LANES), lambda i, p: (0, 0), pipeline_mode=pl.Buffered(1)
                )
            ],
            out_specs=pl.BlockSpec((picks // LANES, LANES), lambda i, p: (0, 0)),
            scratch_shapes=[
                pltpu.VMEM((total, LANES), jnp.float32),
                pltpu.VMEM((picks // LANES, LANES, LANES), jnp.float32),
            ],
        ),
        out_shape=jax.ShapeDtypeStruct((picks // LANES, LANES), jnp.float32),
        compiler_params=pltpu.CompilerParams(vmem_limit_bytes=40 * MIB),
        cost_estimate=pl.CostEstimate(
            flops=8 * total * LANES, bytes_accessed=4 * total * LANES, transcendentals=0
        ),
        name="pick_samples",
    )(index, *blocks, lane_signs)


def parity_sign(bits):
    for shift in (16, 8, 4, 2, 1):
        bits = bits ^ (bits >> shift)
    return 1 - 2 * (bits & 1)


def swap(value, axis, offset):
    count = lax.axis_size(axis)
    return lax.ppermute(value, axis, [(i, i ^ offset) for i in range(count)])


def after(value, *others):
    return lax.optimization_barrier((value, *others))[0]


def body(inputs, out_cotangent, sign_bits, row_pick, col_pick):
    hi_count = lax.axis_size("hi")
    zl_count = lax.axis_size("zl")
    narrow_count = lax.axis_size("narrow")
    hi, zl, core, narrow = [lax.axis_index(a) for a in ALL_AXES]
    wide_count = hi_count * zl_count * 2
    token_shard, rows = inputs.shape[1:]
    col_shard = sign_bits.shape[2]
    col_dev = col_shard // zl_count
    tile, chunks = plan_chunks(col_dev)
    tokens = token_shard * narrow_count // wide_count
    edges = [tile * sum(chunks[:i]) for i in range(len(chunks) + 1)]
    spans = list(zip(edges, edges[1:]))
    cot = out_cotangent[0, 0]
    cut = list(prepare(cot, zl_count, narrow_count, col_dev, edges[1], spans[:1]))
    cut += prepare(
        after(cot, cut[0]), zl_count, narrow_count, col_dev, col_dev, spans[1:]
    )

    own_xt = inputs[0].reshape(token_shard // tokens, tokens, rows).swapaxes(1, 2)
    xt_parts = [swap(own_xt, "zl", d) if d else own_xt for d in range(zl_count)]

    row_mix = jnp.asarray(hadamard(rows), jnp.bfloat16)
    place = jnp.stack([hi, zl, core]).astype(jnp.int32)
    count = len(chunks)
    own, far, signs, swapped = {}, {}, {}, {}
    blocks, xt = [], None
    bits = sign_bits[0]
    samples = (row_pick[0], col_pick[0])

    def sign_block(d, index):
        start = (zl ^ d) * col_dev + edges[index]
        part = lax.dynamic_slice_in_dim(bits, start, tile * chunks[index], axis=1)
        return (2 * part - 1).astype(jnp.bfloat16)

    for stage in range(count + 2):
        if stage < count:
            signs[stage] = [sign_block(d, stage) for d in range(zl_count)]
            own[stage] = lax.all_to_all(cut[stage], ("zl", "narrow"), 0, 0, tiled=True)
        if 1 <= stage <= count:
            c = stage - 1
            far[c] = [swap(own[c], "hi", h) for h in range(1, hi_count)]
            swapped[c] = [swap(own[c], "core", 1)]
            signs[c] = [swap(x, "zl", d) if d else x for d, x in enumerate(signs[c])]
        if stage >= 2:
            c = stage - 2
            swapped[c] += [swap(x, "core", 1) for x in far[c]]
            pairs = zip([own[c]] + far[c], swapped[c])
            cots = [
                x.reshape(zl_count, tokens, tile * chunks[c]) for pair in pairs for x in pair
            ]
            done = chunk_call(
                place, xt, cots, signs[c], row_mix, tile, chunks[c], hi_count
            )
            blocks.append(done.reshape(-1, zl_count * rows, LANES))
            place = after(place, done)
        if stage == 2:
            row, col = samples
            block = (col // LANES) % (col_dev // LANES)
            row_in = (row // (2 * rows)) % zl_count * rows + row % rows
            position = block * (zl_count * rows) + row_in
            row_base = ((hi * zl_count + zl) * 2 + core) * rows
            col_base = narrow * col_shard + zl * col_dev
            lane = lax.broadcasted_iota(jnp.int32, (1, LANES), 1)
            fold = parity_sign((row & row_base)[:, None]) * parity_sign((col_base + lane) & col[:, None])
            samples = (position, fold.astype(jnp.bfloat16))
        state = (cut, own, far, signs, swapped, blocks, bits, place, xt_parts, samples)
        state = lax.optimization_barrier(state)
        cut, own, far, signs, swapped, blocks, bits, place, xt_parts, samples = state
        if stage == 0:
            xt = [lax.all_gather(x, "narrow", axis=0, tiled=True) for x in [own_xt] + xt_parts[1:]]
    position, lane_signs = samples
    picked = pick_call(position, blocks, lane_signs)

    devices = wide_count * narrow_count
    terms = lax.all_to_all(
        picked.reshape(devices, position.shape[0] // devices), ALL_AXES, 0, 0, tiled=True
    )
    total = jnp.sum(terms, axis=0) / jnp.sqrt(jnp.float32(position.shape[0]))
    return total.reshape(1, 1, -1)


def solution(mesh):
    wide, narrow = mesh.shape["wide"], mesh.shape["narrow"]
    sizes = (2, wide // 4, 2, narrow)
    split = Mesh(mesh.devices.reshape(sizes), ALL_AXES)
    wide_axes = ("hi", "zl", "core")
    return jax.shard_map(
        body,
        mesh=split,
        in_specs=(
            P(None, "narrow", wide_axes),
            P(None, None, ALL_AXES, None),
            P(None, wide_axes, "narrow"),
            P(),
            P(),
        ),
        out_specs=P(None, None, ALL_AXES),
        check_vma=False,
    )
```

```python
import functools

import jax
import jax.numpy as jnp
import numpy as np
from jax import lax
from jax.experimental import pallas as pl
from jax.experimental.pallas import tpu as pltpu
from jax.sharding import Mesh, PartitionSpec as P

LANES = 128
UNITS = 8
SLABS = 4
MIB = 1024 * 1024
ALL_AXES = ("hi", "zl", "core", "narrow")


def hadamard(length):
    h = np.ones((1, 1), np.float32)
    while h.shape[0] < length:
        h = np.block([[h, h], [h, -h]])
    return h


def butterfly(parts):
    step = 1
    while step < len(parts):
        parts = [
            parts[i] + parts[i ^ step] if not i & step else parts[i ^ step] - parts[i]
            for i in range(len(parts))
        ]
        step *= 2
    return parts


def plan_chunks(col_dev):
    tile = max(LANES, min(256, col_dev // UNITS))
    units = col_dev // tile
    first, third = max(1, units // 8), max(1, units // 4)
    return tile, [first, units - 2 * first - third, third, first]


def prep_kernel(real_blocks, zl_count, spans, in_ref, *out_refs):
    block = pl.program_id(1) * zl_count + pl.program_id(0)
    keep = block < real_blocks
    for (start, stop), out_ref in zip(spans, out_refs):
        value = in_ref[:, start:stop]
        out_ref[0] = jnp.where(keep, value, jnp.zeros_like(value))


def prepare(cot, zl_count, narrow_count, col_dev, read, spans):
    tokens, hidden = cot.shape
    real_blocks = hidden // col_dev
    stride = col_dev // read
    return pl.pallas_call(
        functools.partial(prep_kernel, real_blocks, zl_count, spans),
        grid=(zl_count, narrow_count),
        in_specs=[
            pl.BlockSpec(
                (tokens, read),
                lambda z, n: (0, jnp.minimum(n * zl_count + z, real_blocks - 1) * stride),
            )
        ],
        out_specs=[
            pl.BlockSpec(
                (1, tokens, stop - start), lambda z, n: (z * narrow_count + n, 0, 0)
            )
            for start, stop in spans
        ],
        out_shape=[
            jax.ShapeDtypeStruct(
                (zl_count * narrow_count, tokens, stop - start), cot.dtype
            )
            for start, stop in spans
        ],
        compiler_params=pltpu.CompilerParams(vmem_limit_bytes=60 * MIB),
        cost_estimate=pl.CostEstimate(
            flops=0, bytes_accessed=4 * cot.size // stride, transcendentals=0
        ),
        name="cut_columns",
    )(cot)


def chunk_kernel(hi_count, zl_count, place_ref, *refs):
    xt = refs[:zl_count]
    cots = refs[zl_count : zl_count + 2 * hi_count]
    signs = refs[zl_count + 2 * hi_count : 2 * zl_count + 2 * hi_count]
    row_mix = refs[-2]
    out_ref = refs[-1]
    hi, core = place_ref[0], place_ref[2]
    mixed = []
    for d in range(zl_count):
        total = None
        for h in range(hi_count):
            for c in range(2):
                for z in range(zl_count):
                    source = ((hi ^ h) * zl_count + z) * 2 + (core ^ c)
                    term = jnp.dot(
                        xt[d][source],
                        cots[h * 2 + c][z],
                        preferred_element_type=jnp.float32,
                    )
                    total = term if total is None else total + term
        value = total * signs[d][...].astype(jnp.float32)
        high = value.astype(jnp.bfloat16)
        low = (value - high.astype(jnp.float32)).astype(jnp.bfloat16)
        mixed.append(
            jnp.dot(row_mix[...], high, preferred_element_type=jnp.float32)
            + jnp.dot(row_mix[...], low, preferred_element_type=jnp.float32)
        )
    mixed = butterfly(mixed)
    for b in range(out_ref.shape[0]):
        for d in range(zl_count):
            out_ref[b, d] = mixed[d][:, b * LANES : (b + 1) * LANES]


def chunk_call(place, xt, cots, signs, row_mix, tile, steps, hi_count):
    zl_count = len(xt)
    sources, rows, tokens = xt[0].shape
    chunk = tile * steps
    resident = pl.Buffered(1)
    return pl.pallas_call(
        functools.partial(chunk_kernel, hi_count, zl_count),
        grid_spec=pltpu.PrefetchScalarGridSpec(
            num_scalar_prefetch=1,
            grid=(steps,),
            in_specs=[
                pl.BlockSpec(
                    (sources, rows, tokens), lambda i, p: (0, 0, 0), pipeline_mode=resident
                )
                for _ in xt
            ]
            + [
                pl.BlockSpec((zl_count, tokens, tile), lambda i, p: (0, 0, i))
                for _ in cots
            ]
            + [
                pl.BlockSpec((rows, tile), lambda i, p: (0, i))
                for _ in signs
            ]
            + [
                pl.BlockSpec((rows, rows), lambda i, p: (0, 0), pipeline_mode=resident)
            ],
            out_specs=pl.BlockSpec(
                (tile // LANES, zl_count, rows, LANES), lambda i, p: (i, 0, 0, 0)
            ),
        ),
        out_shape=jax.ShapeDtypeStruct(
            (chunk // LANES, zl_count, rows, LANES), jnp.float32
        ),
        compiler_params=pltpu.CompilerParams(vmem_limit_bytes=40 * MIB),
        cost_estimate=pl.CostEstimate(
            flops=zl_count * rows * chunk * tokens,
            bytes_accessed=4 * zl_count * rows * chunk,
            transcendentals=0,
        ),
        name="gradient_rows",
    )(place, *xt, *cots, *signs, row_mix)


def pick_kernel(parts, index_ref, *refs):
    blocks = refs[:parts]
    lane_any, out_ref, mixed_ref, rows_ref, *held, lane_signs, sems = refs[parts:]
    rows = blocks[0].shape[1]
    slab = rows // SLABS
    slabs = [(block, b) for block in held for b in range(block.shape[0])]

    def block_copy(k, part):
        spot = pl.ds(k * slab, slab)
        return pltpu.make_async_copy(
            blocks[part].at[:, spot, :], held[part].at[:, spot, :], sems.at[k * parts + part]
        )

    sign_copy = pltpu.make_async_copy(lane_any, lane_signs, sems.at[SLABS * parts])
    for k in range(SLABS):
        for part in range(parts):
            block_copy(k, part).start()
    sign_copy.start()

    def mix(i, carry):
        spot = pl.ds(pl.multiple_of(i * 8, 8), 8)
        values = [block[b, spot, :] for block, b in slabs]
        for b, value in enumerate(butterfly(values)):
            mixed_ref[pl.ds(pl.multiple_of(b * rows + i * 8, 8), 8), :] = value
        return carry

    for k in range(SLABS):
        for part in range(parts):
            block_copy(k, part).wait()
        lax.fori_loop(k * slab // 8, (k + 1) * slab // 8, mix, 0)

    def gather(g, carry):
        for j in range(LANES):
            row = index_ref[g * LANES + j]
            rows_ref[g, j : j + 1, :] = mixed_ref[pl.ds(row, 1), :]
        return carry

    groups = out_ref.shape[0]
    lax.fori_loop(0, groups, gather, 0)
    sign_copy.wait()
    side = 4 if groups % 4 == 0 else 1

    def reduce(i, carry):
        for q in range(side):
            g = i * side + q
            spot = pl.ds(pl.multiple_of(g * LANES, LANES), LANES)
            product = rows_ref[g] * lane_signs[spot, :].astype(jnp.float32)
            out_ref[pl.ds(g, 1), :] = jnp.sum(product.T, axis=0, keepdims=True)
        return carry

    lax.fori_loop(0, groups // side, reduce, 0)


def pick_call(index, blocks, lane_signs):
    picks = index.shape[0]
    total = sum(block.shape[0] * block.shape[1] for block in blocks)
    return pl.pallas_call(
        functools.partial(pick_kernel, len(blocks)),
        grid_spec=pltpu.PrefetchScalarGridSpec(
            num_scalar_prefetch=1,
            grid=(1,),
            in_specs=[pl.BlockSpec(memory_space=pl.ANY)] * (len(blocks) + 1),
            out_specs=pl.BlockSpec((picks // LANES, LANES), lambda i, p: (0, 0)),
            scratch_shapes=[
                pltpu.VMEM((total, LANES), jnp.float32),
                pltpu.VMEM((picks // LANES, LANES, LANES), jnp.float32),
                *[pltpu.VMEM(block.shape, jnp.float32) for block in blocks],
                pltpu.VMEM(lane_signs.shape, lane_signs.dtype),
                pltpu.SemaphoreType.DMA((SLABS * len(blocks) + 1,)),
            ],
        ),
        out_shape=jax.ShapeDtypeStruct((picks // LANES, LANES), jnp.float32),
        compiler_params=pltpu.CompilerParams(vmem_limit_bytes=40 * MIB),
        cost_estimate=pl.CostEstimate(
            flops=8 * total * LANES, bytes_accessed=4 * total * LANES, transcendentals=0
        ),
        name="pick_samples",
    )(index, *blocks, lane_signs)


def parity_sign(bits):
    for shift in (16, 8, 4, 2, 1):
        bits = bits ^ (bits >> shift)
    return 1 - 2 * (bits & 1)


def swap(value, axis, offset):
    count = lax.axis_size(axis)
    return lax.ppermute(value, axis, [(i, i ^ offset) for i in range(count)])


def after(value, *others):
    return lax.optimization_barrier((value, *others))[0]


def body(inputs, out_cotangent, sign_bits, row_pick, col_pick):
    hi_count = lax.axis_size("hi")
    zl_count = lax.axis_size("zl")
    narrow_count = lax.axis_size("narrow")
    hi, zl, core, narrow = [lax.axis_index(a) for a in ALL_AXES]
    wide_count = hi_count * zl_count * 2
    token_shard, rows = inputs.shape[1:]
    col_shard = sign_bits.shape[2]
    col_dev = col_shard // zl_count
    tile, chunks = plan_chunks(col_dev)
    tokens = token_shard * narrow_count // wide_count
    edges = [tile * sum(chunks[:i]) for i in range(len(chunks) + 1)]
    spans = list(zip(edges, edges[1:]))
    cot = out_cotangent[0, 0]
    cut = list(prepare(cot, zl_count, narrow_count, col_dev, edges[1], spans[:1]))
    cut += prepare(
        after(cot, cut[0]), zl_count, narrow_count, col_dev, col_dev, spans[1:]
    )

    own_xt = inputs[0].reshape(token_shard // tokens, tokens, rows).swapaxes(1, 2)
    xt_parts = [swap(own_xt, "zl", d) if d else own_xt for d in range(zl_count)]

    row_mix = jnp.asarray(hadamard(rows), jnp.bfloat16)
    place = jnp.stack([hi, zl, core]).astype(jnp.int32)
    count = len(chunks)
    own, far, signs, swapped = {}, {}, {}, {}
    blocks, xt = [], None
    bits = sign_bits[0]
    samples = (row_pick[0], col_pick[0])

    def sign_block(d, index):
        start = (zl ^ d) * col_dev + edges[index]
        part = lax.dynamic_slice_in_dim(bits, start, tile * chunks[index], axis=1)
        return (2 * part - 1).astype(jnp.bfloat16)

    for stage in range(count + 2):
        if stage < count:
            signs[stage] = [sign_block(d, stage) for d in range(zl_count)]
            own[stage] = lax.all_to_all(cut[stage], ("zl", "narrow"), 0, 0, tiled=True)
        if 1 <= stage <= count:
            c = stage - 1
            far[c] = [swap(own[c], "hi", h) for h in range(1, hi_count)]
            swapped[c] = [swap(own[c], "core", 1)]
            signs[c] = [swap(x, "zl", d) if d else x for d, x in enumerate(signs[c])]
        if stage >= 2:
            c = stage - 2
            swapped[c] += [swap(x, "core", 1) for x in far[c]]
            pairs = zip([own[c]] + far[c], swapped[c])
            cots = [
                x.reshape(zl_count, tokens, tile * chunks[c]) for pair in pairs for x in pair
            ]
            done = chunk_call(
                place, xt, cots, signs[c], row_mix, tile, chunks[c], hi_count
            )
            blocks.append(done.reshape(-1, zl_count * rows, LANES))
            place = after(place, done)
        if stage == 2:
            row, col = samples
            block = (col // LANES) % (col_dev // LANES)
            row_in = (row // (2 * rows)) % zl_count * rows + row % rows
            position = block * (zl_count * rows) + row_in
            row_base = ((hi * zl_count + zl) * 2 + core) * rows
            col_base = narrow * col_shard + zl * col_dev
            lane = lax.broadcasted_iota(jnp.int32, (1, LANES), 1)
            fold = parity_sign((row & row_base)[:, None]) * parity_sign((col_base + lane) & col[:, None])
            samples = (position, fold.astype(jnp.bfloat16))
        state = (cut, own, far, signs, swapped, blocks, bits, place, xt_parts, samples)
        state = lax.optimization_barrier(state)
        cut, own, far, signs, swapped, blocks, bits, place, xt_parts, samples = state
        if stage == 0:
            xt = [lax.all_gather(x, "narrow", axis=0, tiled=True) for x in [own_xt] + xt_parts[1:]]
    position, lane_signs = samples
    picked = pick_call(position, blocks, lane_signs)

    devices = wide_count * narrow_count
    terms = lax.all_to_all(
        picked.reshape(devices, position.shape[0] // devices), ALL_AXES, 0, 0, tiled=True
    )
    total = jnp.sum(terms, axis=0) / jnp.sqrt(jnp.float32(position.shape[0]))
    return total.reshape(1, 1, -1)


def solution(mesh):
    wide, narrow = mesh.shape["wide"], mesh.shape["narrow"]
    sizes = (2, wide // 4, 2, narrow)
    split = Mesh(mesh.devices.reshape(sizes), ALL_AXES)
    wide_axes = ("hi", "zl", "core")
    return jax.shard_map(
        body,
        mesh=split,
        in_specs=(
            P(None, "narrow", wide_axes),
            P(None, None, ALL_AXES, None),
            P(None, wide_axes, "narrow"),
            P(),
            P(),
        ),
        out_specs=P(None, None, ALL_AXES),
        check_vma=False,
    )
```

```python
import functools

import jax
import jax.numpy as jnp
import numpy as np
from jax import lax
from jax.experimental import pallas as pl
from jax.experimental.pallas import tpu as pltpu
from jax.sharding import Mesh, PartitionSpec as P

LANES = 128
UNITS = 8
MIB = 1024 * 1024
ALL_AXES = ("hi", "zl", "core", "narrow")


def hadamard(length):
    h = np.ones((1, 1), np.float32)
    while h.shape[0] < length:
        h = np.block([[h, h], [h, -h]])
    return h


def butterfly(parts):
    step = 1
    while step < len(parts):
        parts = [
            parts[i] + parts[i ^ step] if not i & step else parts[i ^ step] - parts[i]
            for i in range(len(parts))
        ]
        step *= 2
    return parts


def plan_chunks(col_dev):
    tile = max(LANES, min(256, col_dev // UNITS))
    units = col_dev // tile
    first, third = max(1, units // 8), max(1, units // 4)
    return tile, [first, units - 2 * first - third, third, first]


def prep_kernel(real_blocks, zl_count, spans, in_ref, *out_refs):
    block = pl.program_id(1) * zl_count + pl.program_id(0)
    keep = block < real_blocks
    for (start, stop), out_ref in zip(spans, out_refs):
        value = in_ref[:, start:stop]
        out_ref[0] = jnp.where(keep, value, jnp.zeros_like(value))


def prepare(cot, zl_count, narrow_count, col_dev, read, spans):
    tokens, hidden = cot.shape
    real_blocks = hidden // col_dev
    stride = col_dev // read
    return pl.pallas_call(
        functools.partial(prep_kernel, real_blocks, zl_count, spans),
        grid=(zl_count, narrow_count),
        in_specs=[
            pl.BlockSpec(
                (tokens, read),
                lambda z, n: (0, jnp.minimum(n * zl_count + z, real_blocks - 1) * stride),
            )
        ],
        out_specs=[
            pl.BlockSpec(
                (1, tokens, stop - start), lambda z, n: (z * narrow_count + n, 0, 0)
            )
            for start, stop in spans
        ],
        out_shape=[
            jax.ShapeDtypeStruct(
                (zl_count * narrow_count, tokens, stop - start), cot.dtype
            )
            for start, stop in spans
        ],
        compiler_params=pltpu.CompilerParams(vmem_limit_bytes=60 * MIB),
        cost_estimate=pl.CostEstimate(
            flops=0, bytes_accessed=4 * cot.size // stride, transcendentals=0
        ),
        name="cut_columns",
    )(cot)


def chunk_kernel(hi_count, zl_count, place_ref, *refs):
    xt = refs[:zl_count]
    cots = refs[zl_count : zl_count + 2 * hi_count]
    signs = refs[zl_count + 2 * hi_count : 2 * zl_count + 2 * hi_count]
    row_mix = refs[-2]
    out_ref = refs[-1]
    hi, core = place_ref[0], place_ref[2]
    mixed = []
    for d in range(zl_count):
        total = None
        for h in range(hi_count):
            for c in range(2):
                for z in range(zl_count):
                    source = ((hi ^ h) * zl_count + z) * 2 + (core ^ c)
                    term = jnp.dot(
                        xt[d][source],
                        cots[h * 2 + c][z],
                        preferred_element_type=jnp.float32,
                    )
                    total = term if total is None else total + term
        value = total * signs[d][...].astype(jnp.float32)
        high = value.astype(jnp.bfloat16)
        low = (value - high.astype(jnp.float32)).astype(jnp.bfloat16)
        mixed.append(
            jnp.dot(row_mix[...], high, preferred_element_type=jnp.float32)
            + jnp.dot(row_mix[...], low, preferred_element_type=jnp.float32)
        )
    mixed = butterfly(mixed)
    for b in range(out_ref.shape[0]):
        for d in range(zl_count):
            out_ref[b, d] = mixed[d][:, b * LANES : (b + 1) * LANES]


def chunk_call(place, xt, cots, signs, row_mix, tile, steps, hi_count):
    zl_count = len(xt)
    sources, rows, tokens = xt[0].shape
    chunk = tile * steps
    resident = pl.Buffered(1)
    return pl.pallas_call(
        functools.partial(chunk_kernel, hi_count, zl_count),
        grid_spec=pltpu.PrefetchScalarGridSpec(
            num_scalar_prefetch=1,
            grid=(steps,),
            in_specs=[
                pl.BlockSpec(
                    (sources, rows, tokens), lambda i, p: (0, 0, 0), pipeline_mode=resident
                )
                for _ in xt
            ]
            + [
                pl.BlockSpec((zl_count, tokens, tile), lambda i, p: (0, 0, i))
                for _ in cots
            ]
            + [
                pl.BlockSpec((rows, tile), lambda i, p: (0, i))
                for _ in signs
            ]
            + [
                pl.BlockSpec((rows, rows), lambda i, p: (0, 0), pipeline_mode=resident)
            ],
            out_specs=pl.BlockSpec(
                (tile // LANES, zl_count, rows, LANES), lambda i, p: (i, 0, 0, 0)
            ),
        ),
        out_shape=jax.ShapeDtypeStruct(
            (chunk // LANES, zl_count, rows, LANES), jnp.float32
        ),
        compiler_params=pltpu.CompilerParams(vmem_limit_bytes=40 * MIB),
        cost_estimate=pl.CostEstimate(
            flops=zl_count * rows * chunk * tokens,
            bytes_accessed=4 * zl_count * rows * chunk,
            transcendentals=0,
        ),
        name="gradient_rows",
    )(place, *xt, *cots, *signs, row_mix)


def pick_kernel(parts, index_ref, *refs):
    blocks = refs[:parts]
    lane_signs, out_ref, mixed_ref, rows_ref = refs[parts:]
    rows = blocks[0].shape[1]
    slabs = [(block, b) for block in blocks for b in range(block.shape[0])]

    def mix(i, carry):
        spot = pl.ds(pl.multiple_of(i * 8, 8), 8)
        values = [block[b, spot, :] for block, b in slabs]
        for b, value in enumerate(butterfly(values)):
            mixed_ref[pl.ds(pl.multiple_of(b * rows + i * 8, 8), 8), :] = value
        return carry

    lax.fori_loop(0, rows // 8, mix, 0, unroll=2)

    def gather(g, carry):
        for j in range(LANES):
            row = index_ref[g * LANES + j]
            rows_ref[g, j : j + 1, :] = mixed_ref[pl.ds(row, 1), :]
        return carry

    groups = out_ref.shape[0]
    lax.fori_loop(0, groups, gather, 0)
    side = 8 if groups % 8 == 0 else 1

    def reduce(i, carry):
        for q in range(side):
            g = i * side + q
            spot = pl.ds(pl.multiple_of(g * LANES, LANES), LANES)
            product = rows_ref[g] * lane_signs[spot, :].astype(jnp.float32)
            out_ref[pl.ds(g, 1), :] = jnp.sum(product.T, axis=0, keepdims=True)
        return carry

    lax.fori_loop(0, groups // side, reduce, 0)


def pick_call(index, blocks, lane_signs):
    picks = index.shape[0]
    total = sum(block.shape[0] * block.shape[1] for block in blocks)
    return pl.pallas_call(
        functools.partial(pick_kernel, len(blocks)),
        grid_spec=pltpu.PrefetchScalarGridSpec(
            num_scalar_prefetch=1,
            grid=(1,),
            in_specs=[
                pl.BlockSpec(
                    block.shape, lambda i, p: (0, 0, 0), pipeline_mode=pl.Buffered(1)
                )
                for block in blocks
            ]
            + [
                pl.BlockSpec(
                    (picks, LANES), lambda i, p: (0, 0), pipeline_mode=pl.Buffered(1)
                )
            ],
            out_specs=pl.BlockSpec((picks // LANES, LANES), lambda i, p: (0, 0)),
            scratch_shapes=[
                pltpu.VMEM((total, LANES), jnp.float32),
                pltpu.VMEM((picks // LANES, LANES, LANES), jnp.float32),
            ],
        ),
        out_shape=jax.ShapeDtypeStruct((picks // LANES, LANES), jnp.float32),
        compiler_params=pltpu.CompilerParams(vmem_limit_bytes=40 * MIB),
        cost_estimate=pl.CostEstimate(
            flops=8 * total * LANES, bytes_accessed=4 * total * LANES, transcendentals=0
        ),
        name="pick_samples",
    )(index, *blocks, lane_signs)


def parity_sign(bits):
    for shift in (16, 8, 4, 2, 1):
        bits = bits ^ (bits >> shift)
    return 1 - 2 * (bits & 1)


def swap(value, axis, offset):
    count = lax.axis_size(axis)
    return lax.ppermute(value, axis, [(i, i ^ offset) for i in range(count)])


def after(value, *others):
    return lax.optimization_barrier((value, *others))[0]


def body(inputs, out_cotangent, sign_bits, row_pick, col_pick):
    hi_count = lax.axis_size("hi")
    zl_count = lax.axis_size("zl")
    narrow_count = lax.axis_size("narrow")
    hi, zl, core, narrow = [lax.axis_index(a) for a in ALL_AXES]
    wide_count = hi_count * zl_count * 2
    token_shard, rows = inputs.shape[1:]
    col_shard = sign_bits.shape[2]
    col_dev = col_shard // zl_count
    tile, chunks = plan_chunks(col_dev)
    tokens = token_shard * narrow_count // wide_count
    edges = [tile * sum(chunks[:i]) for i in range(len(chunks) + 1)]
    spans = list(zip(edges, edges[1:]))
    cot = out_cotangent[0, 0]
    cut = list(prepare(cot, zl_count, narrow_count, col_dev, edges[1], spans[:1]))
    cut += prepare(
        after(cot, cut[0]), zl_count, narrow_count, col_dev, col_dev, spans[1:]
    )

    own_xt = inputs[0].reshape(token_shard // tokens, tokens, rows).swapaxes(1, 2)
    xt_parts = [swap(own_xt, "zl", d) if d else own_xt for d in range(zl_count)]

    row_mix = jnp.asarray(hadamard(rows), jnp.bfloat16)
    place = jnp.stack([hi, zl, core]).astype(jnp.int32)
    count = len(chunks)
    own, far, signs, swapped = {}, {}, {}, {}
    blocks, xt = [], None
    bits = sign_bits[0]
    samples = (row_pick[0], col_pick[0])

    def sign_block(d, index):
        start = (zl ^ d) * col_dev + edges[index]
        part = lax.dynamic_slice_in_dim(bits, start, tile * chunks[index], axis=1)
        return (2 * part - 1).astype(jnp.bfloat16)

    for stage in range(count + 2):
        if stage < count:
            signs[stage] = [sign_block(d, stage) for d in range(zl_count)]
            own[stage] = lax.all_to_all(cut[stage], ("zl", "narrow"), 0, 0, tiled=True)
        if 1 <= stage <= count:
            c = stage - 1
            far[c] = [swap(own[c], "hi", h) for h in range(1, hi_count)]
            swapped[c] = [swap(own[c], "core", 1)]
            signs[c] = [swap(x, "zl", d) if d else x for d, x in enumerate(signs[c])]
        if stage >= 2:
            c = stage - 2
            swapped[c] += [swap(x, "core", 1) for x in far[c]]
            pairs = zip([own[c]] + far[c], swapped[c])
            cots = [
                x.reshape(zl_count, tokens, tile * chunks[c]) for pair in pairs for x in pair
            ]
            done = chunk_call(
                place, xt, cots, signs[c], row_mix, tile, chunks[c], hi_count
            )
            blocks.append(done.reshape(-1, zl_count * rows, LANES))
            place = after(place, done)
        if stage == 2:
            row, col = samples
            block = (col // LANES) % (col_dev // LANES)
            row_in = (row // (2 * rows)) % zl_count * rows + row % rows
            position = block * (zl_count * rows) + row_in
            row_base = ((hi * zl_count + zl) * 2 + core) * rows
            col_base = narrow * col_shard + zl * col_dev
            lane = lax.broadcasted_iota(jnp.int32, (1, LANES), 1)
            fold = parity_sign((row & row_base)[:, None]) * parity_sign((col_base + lane) & col[:, None])
            samples = (position, fold.astype(jnp.bfloat16))
        state = (cut, own, far, signs, swapped, blocks, bits, place, xt_parts, samples)
        state = lax.optimization_barrier(state)
        cut, own, far, signs, swapped, blocks, bits, place, xt_parts, samples = state
        if stage == 0:
            xt = [lax.all_gather(x, "narrow", axis=0, tiled=True) for x in [own_xt] + xt_parts[1:]]
    position, lane_signs = samples
    picked = pick_call(position, blocks, lane_signs)

    devices = wide_count * narrow_count
    terms = lax.all_to_all(
        picked.reshape(devices, position.shape[0] // devices), ALL_AXES, 0, 0, tiled=True
    )
    total = jnp.sum(terms, axis=0) / jnp.sqrt(jnp.float32(position.shape[0]))
    return total.reshape(1, 1, -1)


def solution(mesh):
    wide, narrow = mesh.shape["wide"], mesh.shape["narrow"]
    sizes = (2, wide // 4, 2, narrow)
    split = Mesh(mesh.devices.reshape(sizes), ALL_AXES)
    wide_axes = ("hi", "zl", "core")
    return jax.shard_map(
        body,
        mesh=split,
        in_specs=(
            P(None, "narrow", wide_axes),
            P(None, None, ALL_AXES, None),
            P(None, wide_axes, "narrow"),
            P(),
            P(),
        ),
        out_specs=P(None, None, ALL_AXES),
        check_vma=False,
    )
```
